32 devices in a mesh: dp: 4 (over y, x), tp: 8 (over z, core).
Axes of the slice: x: 2, y: 2, z: 4, core: 2. Of those that a mesh axis runs over, the one named last changes fastest.
Arguments:
- tokens: bfloat16 [512, 4096], P(('dp', 'tp')), may hold values from -6 to 6
- norm_scale_vector: float32 [4096], replicated, may hold values from 0.5 to 1.5
- gate_weight: bfloat16 [4096, 14336], P(None, 'tp'), may hold values from -0.09375 to 0.09375
- up_weight: bfloat16 [4096, 14336], P(None, 'tp'), may hold values from -0.09375 to 0.09375
- down_weight: bfloat16 [14336, 4096], P('tp'), may hold values from -0.046875 to 0.046875
- cotangent: bfloat16 [512, 4096], P(('dp', 'tp')), may hold values from -4 to 4
Outputs:
- mixed: bfloat16 [512, 4096], P(('dp', 'tp'))
- token_gradient: bfloat16 [512, 4096], P(('dp', 'tp'))
- grad_gate: bfloat16 [4096, 14336], P('dp', 'tp')
- grad_up: bfloat16 [4096, 14336], P('dp', 'tp')
- grad_down: bfloat16 [14336, 4096], P('tp', 'dp')
The draws below stay inside these ranges and needn't reach their ends.
All inputs are finite; a program needn't handle non-finite values.
Results may differ from the reference program's by a relative error of at most 0.025.
Values may be sent and summed in bfloat16 or wider, within the bound.
No kernel may reach another device: no remote copies, remote signals or barrier semaphores. Data moves between devices by JAX's collectives and lax.ppermute only.
A program may use at most 192 MiB of HBM per device.

```python
import jax
import jax.numpy as jnp
from jax import lax

D = 4096
FF = 14336
TOKENS = 512
N_DP = 4
N_TP = 8


def shard_levels(rng, extent, cuts, low, top_value):
    def one(axis_at, shards_of):
        steps = jax.random.uniform(jax.random.fold_in(jax.random.fold_in(rng, 6), axis_at), (shards_of,), jnp.float32, low / len(cuts), top_value / len(cuts))
        return jnp.repeat(jnp.exp(steps), extent[axis_at] // shards_of).reshape((-1,) + (1,) * (len(extent) - axis_at - 1))

    loudness = one(*cuts[0])
    for cut in cuts[1:]:
        loudness = loudness * one(*cut)
    return loudness


def scatter_about(key, extent, deviation, bound, cuts=(), kind=jnp.bfloat16):
    entries = jax.random.normal(key, extent, jnp.float32) * deviation
    if len(cuts) > 0:
        entries = shard_levels(key, extent, cuts, -0.22, 0.18) * entries
    return jnp.clip(entries, min=-bound, max=bound).astype(kind)


def setup_inputs(seed: int = 0) -> dict:
    keys = jax.random.split(jax.random.key(seed), 7)
    return {
        "tokens": scatter_about(keys[0], (TOKENS, D), 1.0, 6.0, ((0, 32),)),
        "norm_scale_vector": jnp.clip(1.0 + 0.1 * jax.random.normal(keys[1], (D,), jnp.float32), 0.5, 1.5),
        "gate_weight": scatter_about(keys[2], (D, FF), D ** -0.5, 0.09375, ((1, 8),)),
        "up_weight": scatter_about(keys[3], (D, FF), D ** -0.5, 0.09375, ((1, 8),)),
        "down_weight": scatter_about(keys[4], (FF, D), FF ** -0.5, 0.046875, ((0, 8),)),
        "cotangent": scatter_about(keys[5], (TOKENS, D), 0.25, 4.0, ((0, 32),)),
    }


def replica_sum(left, right):
    rows = left.shape[0] // N_DP
    first = left.astype(jnp.float32).reshape(N_DP, rows, left.shape[1])
    second = right.astype(jnp.float32).reshape(N_DP, rows, right.shape[1])
    parts = jnp.einsum('nra,nrb->nab', first, second).astype(jnp.bfloat16)
    parts = lax.optimization_barrier(parts)
    return lax.optimization_barrier(jnp.sum(parts.astype(jnp.float32), axis=0)).astype(jnp.bfloat16)

def reference(tokens, norm_scale_vector, gate_weight, up_weight, down_weight, cotangent):
    expanded_hidden = tokens.astype(jnp.float32)
    reciprocal_root_mean = lax.rsqrt(lax.optimization_barrier(jnp.mean(expanded_hidden * expanded_hidden, axis=-1, keepdims=True)) + 1e-05)
    unit_input = expanded_hidden * reciprocal_root_mean
    rescaled_input = (unit_input * norm_scale_vector).astype(jnp.bfloat16)
    width = FF // N_TP

    def block(carry, index):
        first = (index * width).astype(jnp.int32)
        gate_block = lax.dynamic_slice_in_dim(gate_weight, first, width, 1)
        up_block = lax.dynamic_slice_in_dim(up_weight, first, width, 1)
        down_block = lax.dynamic_slice_in_dim(down_weight, first, width, 0)
        gate = jnp.dot(rescaled_input, gate_block, preferred_element_type=jnp.float32)
        lifted = jnp.dot(rescaled_input, up_block, preferred_element_type=jnp.float32)
        sigmoid_gate = jax.nn.sigmoid(gate)
        activated = gate * sigmoid_gate
        hidden = (activated * lifted).astype(jnp.bfloat16)
        partial_out = jnp.dot(hidden, down_block, preferred_element_type=jnp.float32).astype(jnp.bfloat16)
        grad_hidden = jnp.dot(cotangent, down_block.T, preferred_element_type=jnp.float32)
        grad_pre = (grad_hidden * lifted * sigmoid_gate * (1.0 + gate * (1.0 - sigmoid_gate))).astype(jnp.bfloat16)
        grad_lifted = (grad_hidden * activated).astype(jnp.bfloat16)
        partial_in = (jnp.dot(grad_pre, gate_block.T, preferred_element_type=jnp.float32) + jnp.dot(grad_lifted, up_block.T, preferred_element_type=jnp.float32)).astype(jnp.bfloat16)
        weight_gate = replica_sum(rescaled_input, grad_pre)
        weight_up = replica_sum(rescaled_input, grad_lifted)
        weight_down = replica_sum(hidden, cotangent)
        branch_sum, input_sum = carry
        carry = (branch_sum + partial_out.astype(jnp.float32), input_sum + partial_in.astype(jnp.float32))
        return (carry, (weight_gate, weight_up, weight_down))
    start = (jnp.zeros(tokens.shape, jnp.float32), jnp.zeros(tokens.shape, jnp.float32))
    (branch, grad_normed), (stack_gate, stack_up, stack_down) = lax.scan(block, start, jnp.arange(N_TP, dtype=jnp.int32))
    mixed = (expanded_hidden + branch).astype(jnp.bfloat16)
    gain_applied = grad_normed * norm_scale_vector
    inner_product = lax.optimization_barrier(jnp.mean(gain_applied * unit_input, axis=-1, keepdims=True))
    token_gradient = (cotangent.astype(jnp.float32) + reciprocal_root_mean * (gain_applied - unit_input * inner_product)).astype(jnp.bfloat16)
    grad_gate = jnp.transpose(stack_gate, (1, 0, 2)).reshape(D, FF)
    grad_up = jnp.transpose(stack_up, (1, 0, 2)).reshape(D, FF)
    grad_down = stack_down.reshape(FF, D)
    return (mixed, token_gradient, grad_gate, grad_up, grad_down)
```

```python
import jax
import jax.numpy as jnp
from jax import lax
from jax.sharding import PartitionSpec as P


def contract_rows(left, right):
    return lax.dot_general(
        left, right, (((0,), (0,)), ((), ())), preferred_element_type=jnp.float32
    )


def contract_cols(left, right):
    return lax.dot_general(
        left, right, (((1,), (1,)), ((), ())), preferred_element_type=jnp.float32
    )


def gather_tokens(tokens, norm_scale_vector, gate_weight, up_weight, down_weight, cotangent):
    n_dp = lax.axis_size("dp")
    n_tp = lax.axis_size("tp")
    replica = lax.axis_index("dp")
    rows = tokens.shape[0] * n_tp
    width = tokens.shape[1] // n_dp
    expanded_hidden = tokens.astype(jnp.float32)
    reciprocal_root_mean = lax.rsqrt(
        jnp.mean(expanded_hidden * expanded_hidden, axis=-1, keepdims=True) + 1e-05
    )
    unit_input = expanded_hidden * reciprocal_root_mean
    rescaled_input = (unit_input * norm_scale_vector).astype(jnp.bfloat16)
    grad_all = lax.all_gather(cotangent, ("dp", "tp"), axis=0, tiled=True)
    normed_all = lax.all_gather(rescaled_input, ("dp", "tp"), axis=0, tiled=True)
    grad_hidden = contract_cols(grad_all, down_weight)
    gate = jnp.dot(normed_all, gate_weight, preferred_element_type=jnp.float32)
    lifted = jnp.dot(normed_all, up_weight, preferred_element_type=jnp.float32)
    sigmoid_gate = jax.nn.sigmoid(gate)
    activated = gate * sigmoid_gate
    hidden = (activated * lifted).astype(jnp.bfloat16)
    grad_pre = (grad_hidden * lifted * sigmoid_gate * (1.0 + gate * (1.0 - sigmoid_gate))).astype(
        jnp.bfloat16
    )
    grad_lifted = (grad_hidden * activated).astype(jnp.bfloat16)

    def mine(array):
        return lax.dynamic_slice_in_dim(array, replica * rows, rows, 0)

    def columns(array):
        return lax.dynamic_slice_in_dim(array, replica * width, width, 1)

    branch = lax.psum_scatter(
        jnp.dot(mine(hidden), down_weight, preferred_element_type=jnp.float32).astype(jnp.bfloat16),
        "tp",
        scatter_dimension=0,
        tiled=True,
    ).astype(jnp.float32)
    mixed = (expanded_hidden + branch).astype(jnp.bfloat16)
    grad_normed = lax.psum_scatter(
        (
            contract_cols(mine(grad_pre), gate_weight) + contract_cols(mine(grad_lifted), up_weight)
        ).astype(jnp.bfloat16),
        "tp",
        scatter_dimension=0,
        tiled=True,
    ).astype(jnp.float32)
    gain_applied = grad_normed * norm_scale_vector
    inner_product = jnp.mean(gain_applied * unit_input, axis=-1, keepdims=True)
    token_gradient = (
        cotangent.astype(jnp.float32)
        + reciprocal_root_mean * (gain_applied - unit_input * inner_product)
    ).astype(jnp.bfloat16)
    normed_columns = columns(normed_all)
    return (
        mixed,
        token_gradient,
        contract_rows(normed_columns, grad_pre).astype(jnp.bfloat16),
        contract_rows(normed_columns, grad_lifted).astype(jnp.bfloat16),
        contract_rows(hidden, columns(grad_all)).astype(jnp.bfloat16),
    )


def sum_weight_gradients(tokens, norm_scale_vector, gate_weight, up_weight, down_weight, cotangent):
    expanded_hidden = tokens.astype(jnp.float32)
    reciprocal_root_mean = lax.rsqrt(
        jnp.mean(expanded_hidden * expanded_hidden, axis=-1, keepdims=True) + 1e-05
    )
    unit_input = expanded_hidden * reciprocal_root_mean
    rescaled_input = (unit_input * norm_scale_vector).astype(jnp.bfloat16)
    normed_all = lax.all_gather(rescaled_input, "tp", axis=0, tiled=True)
    gate = jnp.dot(normed_all, gate_weight, preferred_element_type=jnp.float32)
    lifted = jnp.dot(normed_all, up_weight, preferred_element_type=jnp.float32)
    sigmoid_gate = jax.nn.sigmoid(gate)
    activated = gate * sigmoid_gate
    hidden = (activated * lifted).astype(jnp.bfloat16)
    branch = lax.psum_scatter(
        jnp.dot(hidden, down_weight, preferred_element_type=jnp.float32).astype(jnp.bfloat16),
        "tp",
        scatter_dimension=0,
        tiled=True,
    ).astype(jnp.float32)
    mixed = (expanded_hidden + branch).astype(jnp.bfloat16)
    grad_all = lax.all_gather(cotangent, "tp", axis=0, tiled=True)
    grad_hidden = contract_cols(grad_all, down_weight)
    grad_pre = (grad_hidden * lifted * sigmoid_gate * (1.0 + gate * (1.0 - sigmoid_gate))).astype(
        jnp.bfloat16
    )
    grad_lifted = (grad_hidden * activated).astype(jnp.bfloat16)
    grad_normed = lax.psum_scatter(
        (contract_cols(grad_pre, gate_weight) + contract_cols(grad_lifted, up_weight)).astype(
            jnp.bfloat16
        ),
        "tp",
        scatter_dimension=0,
        tiled=True,
    ).astype(jnp.float32)
    gain_applied = grad_normed * norm_scale_vector
    inner_product = jnp.mean(gain_applied * unit_input, axis=-1, keepdims=True)
    token_gradient = (
        cotangent.astype(jnp.float32)
        + reciprocal_root_mean * (gain_applied - unit_input * inner_product)
    ).astype(jnp.bfloat16)
    weight_gate = contract_rows(normed_all, grad_pre).astype(jnp.bfloat16)
    weight_up = contract_rows(normed_all, grad_lifted).astype(jnp.bfloat16)
    weight_down = contract_rows(hidden, grad_all).astype(jnp.bfloat16)
    sum_gate, sum_up, sum_down = (
        lax.psum_scatter(weight_gate, "dp", scatter_dimension=0, tiled=True).astype(jnp.float32),
        lax.psum_scatter(weight_up, "dp", scatter_dimension=0, tiled=True).astype(jnp.float32),
        lax.psum_scatter(weight_down, "dp", scatter_dimension=1, tiled=True).astype(jnp.float32),
    )
    return (
        mixed,
        token_gradient,
        sum_gate.astype(jnp.bfloat16),
        sum_up.astype(jnp.bfloat16),
        sum_down.astype(jnp.bfloat16),
    )


def solution(mesh):
    n_tp = mesh.shape["tp"]
    in_specs = (
        P(("dp", "tp"), None),
        P(),
        P(None, "tp"),
        P(None, "tp"),
        P("tp", None),
        P(("dp", "tp"), None),
    )
    out_specs = (
        P(("dp", "tp"), None),
        P(("dp", "tp"), None),
        P("dp", "tp"),
        P("dp", "tp"),
        P("tp", "dp"),
    )

    def run(tokens, norm_scale_vector, gate_weight, up_weight, down_weight, cotangent):
        gathered = tokens.size + cotangent.size
        weights = (gate_weight.size + up_weight.size + down_weight.size) // n_tp
        local = gather_tokens if gathered <= weights else sum_weight_gradients
        return jax.shard_map(
            local, mesh=mesh, in_specs=in_specs, out_specs=out_specs, check_vma=False
        )(tokens, norm_scale_vector, gate_weight, up_weight, down_weight, cotangent)

    return run
```

```python
import jax
import jax.numpy as jnp
from jax import lax
from jax.sharding import PartitionSpec as P


def contract_rows(left, right):
    return lax.dot_general(
        left, right, (((0,), (0,)), ((), ())), preferred_element_type=jnp.float32
    )


def contract_cols(left, right):
    return lax.dot_general(
        left, right, (((1,), (1,)), ((), ())), preferred_element_type=jnp.float32
    )


def gather_tokens(tokens, norm_scale_vector, gate_weight, up_weight, down_weight, cotangent):
    n_dp = lax.axis_size("dp")
    n_tp = lax.axis_size("tp")
    width = tokens.shape[1] // n_dp
    first = lax.axis_index("dp") * width
    rows = tokens.shape[0]

    def swap(array, dp_bits, tp_bits):
        pairs = [
            (d * n_tp + t, (d ^ dp_bits) * n_tp + (t ^ tp_bits))
            for d in range(n_dp)
            for t in range(n_tp)
        ]
        return lax.ppermute(array, ("dp", "tp"), pairs)

    expanded_hidden = tokens.astype(jnp.float32)
    reciprocal_root_mean = lax.rsqrt(
        jnp.mean(expanded_hidden * expanded_hidden, axis=-1, keepdims=True) + 1e-05
    )
    unit_input = expanded_hidden * reciprocal_root_mean
    rescaled_input = (unit_input * norm_scale_vector).astype(jnp.bfloat16)
    shard = jnp.stack([rescaled_input, cotangent])
    half = jnp.concatenate([shard] + [swap(shard, 0, b) for b in range(2, n_tp, 2)], axis=1)
    own = jnp.concatenate([half, swap(half, 0, 1)], axis=1)
    rest = jnp.concatenate([swap(half, b, 0) for b in range(1, n_dp)], axis=1)
    others = jnp.concatenate([rest, swap(rest, 0, 1)], axis=1)

    def forward(normed, grad_out):
        gate = jnp.dot(normed, gate_weight, preferred_element_type=jnp.float32)
        lifted = jnp.dot(normed, up_weight, preferred_element_type=jnp.float32)
        grad_hidden = contract_cols(grad_out, down_weight)
        sigmoid_gate = jax.nn.sigmoid(gate)
        activated = gate * sigmoid_gate
        hidden = (activated * lifted).astype(jnp.bfloat16)
        grad_pre = (
            grad_hidden * lifted * sigmoid_gate * (1.0 + gate * (1.0 - sigmoid_gate))
        ).astype(jnp.bfloat16)
        grad_lifted = (grad_hidden * activated).astype(jnp.bfloat16)
        return hidden, grad_pre, grad_lifted

    hidden, grad_pre, grad_lifted = forward(own[0], own[1])
    partial_out = jnp.dot(hidden, down_weight, preferred_element_type=jnp.float32)
    partial_in = contract_cols(grad_pre, gate_weight) + contract_cols(grad_lifted, up_weight)
    partials = jnp.stack([partial_out.astype(jnp.bfloat16), partial_in.astype(jnp.bfloat16)])
    kept, sent = jnp.split(partials, 2, axis=1)
    pair = (kept.astype(jnp.float32) + swap(sent, 0, 1).astype(jnp.float32)).astype(jnp.bfloat16)
    total = pair[:, :rows].astype(jnp.float32)
    for k in range(1, n_tp // 2):
        total += swap(pair[:, k * rows : (k + 1) * rows], 0, 2 * k).astype(jnp.float32)
    branch, grad_normed = total[0], total[1]
    mixed = (expanded_hidden + branch).astype(jnp.bfloat16)
    gain_applied = grad_normed * norm_scale_vector
    inner_product = jnp.mean(gain_applied * unit_input, axis=-1, keepdims=True)
    token_gradient = (
        cotangent.astype(jnp.float32)
        + reciprocal_root_mean * (gain_applied - unit_input * inner_product)
    ).astype(jnp.bfloat16)

    more = forward(others[0], others[1])
    hidden, grad_pre, grad_lifted = (
        jnp.concatenate(both, axis=0) for both in zip((hidden, grad_pre, grad_lifted), more)
    )
    columns = jnp.concatenate(
        [lax.dynamic_slice_in_dim(part, first, width, 2) for part in (own, others)], axis=1
    )
    return (
        mixed,
        token_gradient,
        contract_rows(columns[0], grad_pre).astype(jnp.bfloat16),
        contract_rows(columns[0], grad_lifted).astype(jnp.bfloat16),
        contract_rows(hidden, columns[1]).astype(jnp.bfloat16),
    )


def sum_weight_gradients(tokens, norm_scale_vector, gate_weight, up_weight, down_weight, cotangent):
    expanded_hidden = tokens.astype(jnp.float32)
    reciprocal_root_mean = lax.rsqrt(
        jnp.mean(expanded_hidden * expanded_hidden, axis=-1, keepdims=True) + 1e-05
    )
    unit_input = expanded_hidden * reciprocal_root_mean
    rescaled_input = (unit_input * norm_scale_vector).astype(jnp.bfloat16)
    normed_all = lax.all_gather(rescaled_input, "tp", axis=0, tiled=True)
    gate = jnp.dot(normed_all, gate_weight, preferred_element_type=jnp.float32)
    lifted = jnp.dot(normed_all, up_weight, preferred_element_type=jnp.float32)
    sigmoid_gate = jax.nn.sigmoid(gate)
    activated = gate * sigmoid_gate
    hidden = (activated * lifted).astype(jnp.bfloat16)
    branch = lax.psum_scatter(
        jnp.dot(hidden, down_weight, preferred_element_type=jnp.float32).astype(jnp.bfloat16),
        "tp",
        scatter_dimension=0,
        tiled=True,
    ).astype(jnp.float32)
    mixed = (expanded_hidden + branch).astype(jnp.bfloat16)
    grad_all = lax.all_gather(cotangent, "tp", axis=0, tiled=True)
    grad_hidden = contract_cols(grad_all, down_weight)
    grad_pre = (grad_hidden * lifted * sigmoid_gate * (1.0 + gate * (1.0 - sigmoid_gate))).astype(
        jnp.bfloat16
    )
    grad_lifted = (grad_hidden * activated).astype(jnp.bfloat16)
    grad_normed = lax.psum_scatter(
        (contract_cols(grad_pre, gate_weight) + contract_cols(grad_lifted, up_weight)).astype(
            jnp.bfloat16
        ),
        "tp",
        scatter_dimension=0,
        tiled=True,
    ).astype(jnp.float32)
    gain_applied = grad_normed * norm_scale_vector
    inner_product = jnp.mean(gain_applied * unit_input, axis=-1, keepdims=True)
    token_gradient = (
        cotangent.astype(jnp.float32)
        + reciprocal_root_mean * (gain_applied - unit_input * inner_product)
    ).astype(jnp.bfloat16)
    weight_gate = contract_rows(normed_all, grad_pre).astype(jnp.bfloat16)
    weight_up = contract_rows(normed_all, grad_lifted).astype(jnp.bfloat16)
    weight_down = contract_rows(hidden, grad_all).astype(jnp.bfloat16)
    sum_gate, sum_up, sum_down = (
        lax.psum_scatter(weight_gate, "dp", scatter_dimension=0, tiled=True).astype(jnp.float32),
        lax.psum_scatter(weight_up, "dp", scatter_dimension=0, tiled=True).astype(jnp.float32),
        lax.psum_scatter(weight_down, "dp", scatter_dimension=1, tiled=True).astype(jnp.float32),
    )
    return (
        mixed,
        token_gradient,
        sum_gate.astype(jnp.bfloat16),
        sum_up.astype(jnp.bfloat16),
        sum_down.astype(jnp.bfloat16),
    )


def solution(mesh):
    n_tp = mesh.shape["tp"]
    in_specs = (
        P(("dp", "tp"), None),
        P(),
        P(None, "tp"),
        P(None, "tp"),
        P("tp", None),
        P(("dp", "tp"), None),
    )
    out_specs = (
        P(("dp", "tp"), None),
        P(("dp", "tp"), None),
        P("dp", "tp"),
        P("dp", "tp"),
        P("tp", "dp"),
    )

    def run(tokens, norm_scale_vector, gate_weight, up_weight, down_weight, cotangent):
        gathered = tokens.size + cotangent.size
        weights = (gate_weight.size + up_weight.size + down_weight.size) // n_tp
        local = gather_tokens if gathered <= weights else sum_weight_gradients
        return jax.shard_map(
            local, mesh=mesh, in_specs=in_specs, out_specs=out_specs, check_vma=False
        )(tokens, norm_scale_vector, gate_weight, up_weight, down_weight, cotangent)

    return run
```

```python
import jax
import jax.numpy as jnp
from jax import lax
from jax.experimental import pallas as pl
from jax.experimental.pallas import tpu as pltpu
from jax.sharding import PartitionSpec as P


def contract_rows(left, right):
    return lax.dot_general(
        left, right, (((0,), (0,)), ((), ())), preferred_element_type=jnp.float32
    )


def contract_cols(left, right):
    return lax.dot_general(
        left, right, (((1,), (1,)), ((), ())), preferred_element_type=jnp.float32
    )


TILE = 256
CHUNK = 1024


def activations(normed, grad_out, gate_weight, up_weight, down_weight):
    gate = jnp.dot(normed, gate_weight, preferred_element_type=jnp.float32)
    lifted = jnp.dot(normed, up_weight, preferred_element_type=jnp.float32)
    grad_hidden = contract_cols(grad_out, down_weight)
    sigmoid_gate = jax.nn.sigmoid(gate)
    activated = gate * sigmoid_gate
    hidden = (activated * lifted).astype(jnp.bfloat16)
    grad_pre = (grad_hidden * lifted * sigmoid_gate * (1.0 + gate * (1.0 - sigmoid_gate))).astype(
        jnp.bfloat16
    )
    grad_lifted = (grad_hidden * activated).astype(jnp.bfloat16)
    return hidden, grad_pre, grad_lifted


def copy_all(copies):
    for copy in copies:
        copy.start()
    for copy in copies:
        copy.wait()


def own_kernel(
    near, far, gate_weight, up_weight, down_weight,
    hidden, grad_pre, grad_lifted, kept, sent,
    rows, out_sum, in_sum, arrived,
):
    step = pl.program_id(0)
    part = near.shape[1]

    @pl.when(step == 0)
    def _():
        copy_all([
            pltpu.make_async_copy(near, rows.at[:, pl.ds(0, part)], arrived.at[0]),
            pltpu.make_async_copy(far, rows.at[:, pl.ds(part, part)], arrived.at[1]),
        ])
        out_sum[...] = jnp.zeros_like(out_sum)
        in_sum[...] = jnp.zeros_like(in_sum)

    hidden[...], grad_pre[...], grad_lifted[...] = activations(
        rows[0], rows[1], gate_weight[...], up_weight[...], down_weight[...]
    )
    for at in range(0, out_sum.shape[1], CHUNK):
        here = slice(at, at + CHUNK)
        out_sum[:, here] += jnp.dot(
            hidden[...], down_weight[:, here], preferred_element_type=jnp.float32
        )
        in_sum[:, here] += contract_cols(grad_pre[...], gate_weight[here]) + contract_cols(
            grad_lifted[...], up_weight[here]
        )

    @pl.when(step == pl.num_programs(0) - 1)
    def _():
        for index, total in enumerate((out_sum, in_sum)):
            kept[index] = total[:part].astype(kept.dtype)
            sent[index] = total[part:].astype(sent.dtype)


def own_rows(near, far, gate_weight, up_weight, down_weight):
    part, depth = near.shape[1:]
    hidden_units = gate_weight.shape[1]
    block = (2 * part, TILE)
    tall = pl.BlockSpec((depth, TILE), lambda i: (0, i))
    wide = pl.BlockSpec((TILE, depth), lambda i: (i, 0))
    slim = pl.BlockSpec(block, lambda i: (0, i))
    whole = pl.BlockSpec((2, part, depth), lambda i: (0, 0, 0))
    kept = jax.ShapeDtypeStruct((2, part, depth), jnp.bfloat16)
    unit = jax.ShapeDtypeStruct((2 * part, hidden_units), jnp.bfloat16)
    return pl.pallas_call(
        own_kernel,
        grid=(hidden_units // TILE,),
        in_specs=[pl.BlockSpec(memory_space=pl.ANY)] * 2 + [tall, tall, wide],
        out_specs=[slim, slim, slim, whole, whole],
        out_shape=[unit, unit, unit, kept, kept],
        scratch_shapes=[
            pltpu.VMEM((2, 2 * part, depth), jnp.bfloat16),
            pltpu.VMEM((2 * part, depth), jnp.float32),
            pltpu.VMEM((2 * part, depth), jnp.float32),
            pltpu.SemaphoreType.DMA((2,)),
        ],
        compiler_params=pltpu.CompilerParams(vmem_limit_bytes=48 * 2**20),
        cost_estimate=pl.CostEstimate(
            flops=24 * part * depth * hidden_units,
            bytes_accessed=6 * depth * hidden_units,
            transcendentals=2 * part * hidden_units,
        ),
        name="own_rows",
    )(near, far, gate_weight, up_weight, down_weight)


def all_kernel(
    first, near, far, rest_near, rest_far, own_hidden, own_grad_pre, own_grad_lifted,
    gate_weight, up_weight, down_weight,
    grad_gate, grad_up, grad_down,
    rows, own, normed_t, grad_out, hidden, grad_pre, grad_lifted, arrived,
):
    step = pl.program_id(0)
    part, most = near.shape[1], rest_near.shape[1]
    width = normed_t.shape[0]

    @pl.when(step == 0)
    def _():
        columns = pl.ds(pl.multiple_of(first[0], 128), width)
        copy_all([
            pltpu.make_async_copy(near.at[:, :, columns], own.at[:, pl.ds(0, part)], arrived.at[0]),
            pltpu.make_async_copy(far.at[:, :, columns], own.at[:, pl.ds(part, part)], arrived.at[1]),
            pltpu.make_async_copy(rest_near, rows.at[:, pl.ds(0, most)], arrived.at[2]),
            pltpu.make_async_copy(rest_far, rows.at[:, pl.ds(most, most)], arrived.at[3]),
        ])
        normed_t[:, : 2 * part] = own[0].T
        normed_t[:, 2 * part :] = rows[0, :, columns].T
        grad_out[: 2 * part] = own[1]
        grad_out[2 * part :] = rows[1, :, columns]

    hidden[: 2 * part] = own_hidden[...]
    grad_pre[: 2 * part] = own_grad_pre[...]
    grad_lifted[: 2 * part] = own_grad_lifted[...]
    hidden[2 * part :], grad_pre[2 * part :], grad_lifted[2 * part :] = activations(
        rows[0], rows[1], gate_weight[...], up_weight[...], down_weight[...]
    )
    grad_gate[...] = jnp.dot(
        normed_t[...], grad_pre[...], preferred_element_type=jnp.float32
    ).astype(grad_gate.dtype)
    grad_up[...] = jnp.dot(
        normed_t[...], grad_lifted[...], preferred_element_type=jnp.float32
    ).astype(grad_up.dtype)
    grad_down[...] = jnp.dot(
        hidden[...].T, grad_out[...], preferred_element_type=jnp.float32
    ).astype(grad_down.dtype)


def all_rows(first, near, far, rest_near, rest_far, units, gate_weight, up_weight, down_weight, width):
    part, depth = near.shape[1:]
    most = rest_near.shape[1]
    count = 2 * (part + most)
    hidden_units = gate_weight.shape[1]
    tall = pl.BlockSpec((depth, TILE), lambda i: (0, i))
    wide = pl.BlockSpec((TILE, depth), lambda i: (i, 0))
    slim = pl.BlockSpec((2 * part, TILE), lambda i: (0, i))
    return pl.pallas_call(
        all_kernel,
        grid=(hidden_units // TILE,),
        in_specs=[pl.BlockSpec(memory_space=pltpu.SMEM)]
        + [pl.BlockSpec(memory_space=pl.ANY)] * 4
        + [slim, slim, slim, tall, tall, wide],
        out_specs=[
            pl.BlockSpec((width, TILE), lambda i: (0, i)),
            pl.BlockSpec((width, TILE), lambda i: (0, i)),
            pl.BlockSpec((TILE, width), lambda i: (i, 0)),
        ],
        out_shape=[
            jax.ShapeDtypeStruct((width, hidden_units), jnp.bfloat16),
            jax.ShapeDtypeStruct((width, hidden_units), jnp.bfloat16),
            jax.ShapeDtypeStruct((hidden_units, width), jnp.bfloat16),
        ],
        scratch_shapes=[
            pltpu.VMEM((2, 2 * most, depth), jnp.bfloat16),
            pltpu.VMEM((2, 2 * part, width), jnp.bfloat16),
            pltpu.VMEM((width, count), jnp.bfloat16),
            pltpu.VMEM((count, width), jnp.bfloat16),
            pltpu.VMEM((count, TILE), jnp.bfloat16),
            pltpu.VMEM((count, TILE), jnp.bfloat16),
            pltpu.VMEM((count, TILE), jnp.bfloat16),
            pltpu.SemaphoreType.DMA((4,)),
        ],
        compiler_params=pltpu.CompilerParams(vmem_limit_bytes=48 * 2**20),
        cost_estimate=pl.CostEstimate(
            flops=12 * most * depth * hidden_units + 6 * count * width * hidden_units,
            bytes_accessed=6 * (depth + width) * hidden_units,
            transcendentals=2 * most * hidden_units,
        ),
        name="all_rows",
    )(first, near, far, rest_near, rest_far, *units, gate_weight, up_weight, down_weight)


def gather_tokens(tokens, norm_scale_vector, gate_weight, up_weight, down_weight, cotangent):
    n_dp = lax.axis_size("dp")
    n_tp = lax.axis_size("tp")
    width = tokens.shape[1] // n_dp
    first = (lax.axis_index("dp") * width).astype(jnp.int32).reshape(1)
    rows = tokens.shape[0]

    def swap(array, dp_bits, tp_bits):
        pairs = [
            (d * n_tp + t, (d ^ dp_bits) * n_tp + (t ^ tp_bits))
            for d in range(n_dp)
            for t in range(n_tp)
        ]
        return lax.ppermute(array, ("dp", "tp"), pairs)

    expanded_hidden = tokens.astype(jnp.float32)
    reciprocal_root_mean = lax.rsqrt(
        jnp.mean(expanded_hidden * expanded_hidden, axis=-1, keepdims=True) + 1e-05
    )
    unit_input = expanded_hidden * reciprocal_root_mean
    rescaled_input = (unit_input * norm_scale_vector).astype(jnp.bfloat16)
    shard = jnp.stack([rescaled_input, cotangent])
    near = jnp.concatenate([shard] + [swap(shard, 0, b) for b in range(2, n_tp, 2)], axis=1)
    far = swap(near, 0, 1)
    rest_near = jnp.concatenate([swap(near, b, 0) for b in range(1, n_dp)], axis=1)
    *units, kept, sent = own_rows(near, far, gate_weight, up_weight, down_weight)
    rest_far = swap(rest_near, 0, 1)

    pair = (kept.astype(jnp.float32) + swap(sent, 0, 1).astype(jnp.float32)).astype(jnp.bfloat16)
    parts = [swap(pair[:, k * rows : (k + 1) * rows], 0, 2 * k) for k in range(1, n_tp // 2)]
    weight_gradients = all_rows(
        first, near, far, rest_near, rest_far, units, gate_weight, up_weight, down_weight, width
    )
    total = pair[:, :rows].astype(jnp.float32) + sum(part.astype(jnp.float32) for part in parts)
    branch, grad_normed = total[0], total[1]
    mixed = (expanded_hidden + branch).astype(jnp.bfloat16)
    gain_applied = grad_normed * norm_scale_vector
    inner_product = jnp.mean(gain_applied * unit_input, axis=-1, keepdims=True)
    token_gradient = (
        cotangent.astype(jnp.float32)
        + reciprocal_root_mean * (gain_applied - unit_input * inner_product)
    ).astype(jnp.bfloat16)
    return mixed, token_gradient, *weight_gradients


def sum_weight_gradients(tokens, norm_scale_vector, gate_weight, up_weight, down_weight, cotangent):
    expanded_hidden = tokens.astype(jnp.float32)
    reciprocal_root_mean = lax.rsqrt(
        jnp.mean(expanded_hidden * expanded_hidden, axis=-1, keepdims=True) + 1e-05
    )
    unit_input = expanded_hidden * reciprocal_root_mean
    rescaled_input = (unit_input * norm_scale_vector).astype(jnp.bfloat16)
    normed_all = lax.all_gather(rescaled_input, "tp", axis=0, tiled=True)
    gate = jnp.dot(normed_all, gate_weight, preferred_element_type=jnp.float32)
    lifted = jnp.dot(normed_all, up_weight, preferred_element_type=jnp.float32)
    sigmoid_gate = jax.nn.sigmoid(gate)
    activated = gate * sigmoid_gate
    hidden = (activated * lifted).astype(jnp.bfloat16)
    branch = lax.psum_scatter(
        jnp.dot(hidden, down_weight, preferred_element_type=jnp.float32).astype(jnp.bfloat16),
        "tp",
        scatter_dimension=0,
        tiled=True,
    ).astype(jnp.float32)
    mixed = (expanded_hidden + branch).astype(jnp.bfloat16)
    grad_all = lax.all_gather(cotangent, "tp", axis=0, tiled=True)
    grad_hidden = contract_cols(grad_all, down_weight)
    grad_pre = (grad_hidden * lifted * sigmoid_gate * (1.0 + gate * (1.0 - sigmoid_gate))).astype(
        jnp.bfloat16
    )
    grad_lifted = (grad_hidden * activated).astype(jnp.bfloat16)
    grad_normed = lax.psum_scatter(
        (contract_cols(grad_pre, gate_weight) + contract_cols(grad_lifted, up_weight)).astype(
            jnp.bfloat16
        ),
        "tp",
        scatter_dimension=0,
        tiled=True,
    ).astype(jnp.float32)
    gain_applied = grad_normed * norm_scale_vector
    inner_product = jnp.mean(gain_applied * unit_input, axis=-1, keepdims=True)
    token_gradient = (
        cotangent.astype(jnp.float32)
        + reciprocal_root_mean * (gain_applied - unit_input * inner_product)
    ).astype(jnp.bfloat16)
    weight_gate = contract_rows(normed_all, grad_pre).astype(jnp.bfloat16)
    weight_up = contract_rows(normed_all, grad_lifted).astype(jnp.bfloat16)
    weight_down = contract_rows(hidden, grad_all).astype(jnp.bfloat16)
    sum_gate, sum_up, sum_down = (
        lax.psum_scatter(weight_gate, "dp", scatter_dimension=0, tiled=True).astype(jnp.float32),
        lax.psum_scatter(weight_up, "dp", scatter_dimension=0, tiled=True).astype(jnp.float32),
        lax.psum_scatter(weight_down, "dp", scatter_dimension=1, tiled=True).astype(jnp.float32),
    )
    return (
        mixed,
        token_gradient,
        sum_gate.astype(jnp.bfloat16),
        sum_up.astype(jnp.bfloat16),
        sum_down.astype(jnp.bfloat16),
    )


def solution(mesh):
    n_tp = mesh.shape["tp"]
    in_specs = (
        P(("dp", "tp"), None),
        P(),
        P(None, "tp"),
        P(None, "tp"),
        P("tp", None),
        P(("dp", "tp"), None),
    )
    out_specs = (
        P(("dp", "tp"), None),
        P(("dp", "tp"), None),
        P("dp", "tp"),
        P("dp", "tp"),
        P("tp", "dp"),
    )

    def run(tokens, norm_scale_vector, gate_weight, up_weight, down_weight, cotangent):
        gathered = tokens.size + cotangent.size
        weights = (gate_weight.size + up_weight.size + down_weight.size) // n_tp
        local = gather_tokens if gathered <= weights else sum_weight_gradients
        return jax.shard_map(
            local, mesh=mesh, in_specs=in_specs, out_specs=out_specs, check_vma=False
        )(tokens, norm_scale_vector, gate_weight, up_weight, down_weight, cotangent)

    return run
```

```python
import functools

import jax
import jax.numpy as jnp
from jax import lax
from jax.experimental import pallas as pl
from jax.experimental.pallas import tpu as pltpu
from jax.sharding import PartitionSpec as P


def contract_rows(left, right):
    return lax.dot_general(
        left, right, (((0,), (0,)), ((), ())), preferred_element_type=jnp.float32
    )


def contract_cols(left, right):
    return lax.dot_general(
        left, right, (((1,), (1,)), ((), ())), preferred_element_type=jnp.float32
    )


TILE = 256
COLUMNS = 512


def activations(normed, grad_hidden, gate_weight, up_weight):
    gate = jnp.dot(normed, gate_weight, preferred_element_type=jnp.float32)
    lifted = jnp.dot(normed, up_weight, preferred_element_type=jnp.float32)
    sigmoid_gate = jax.nn.sigmoid(gate)
    activated = gate * sigmoid_gate
    hidden = (activated * lifted).astype(jnp.bfloat16)
    grad_pre = (grad_hidden * lifted * sigmoid_gate * (1.0 + gate * (1.0 - sigmoid_gate))).astype(
        jnp.bfloat16
    )
    grad_lifted = (grad_hidden * activated).astype(jnp.bfloat16)
    return hidden, grad_pre, grad_lifted


def copy_all(copies):
    for copy in copies:
        copy.start()
    for copy in copies:
        copy.wait()


def pack(pieces, rows, arrived):
    height = pieces[0].shape[1]
    copy_all([
        pltpu.make_async_copy(piece, rows.at[:, pl.ds(i * height, height)], arrived.at[i])
        for i, piece in enumerate(pieces)
    ])


def own_kernel(n_pieces, *refs):
    pieces, refs = refs[:n_pieces], refs[n_pieces:]
    gate_weight, up_weight, down_weight, hidden, grad_pre, grad_lifted, rows, arrived = refs

    @pl.when(pl.program_id(0) == 0)
    def _():
        pack(pieces, rows, arrived)

    grad_hidden = contract_cols(rows[1], down_weight[...])
    hidden[...], grad_pre[...], grad_lifted[...] = activations(
        rows[0], grad_hidden, gate_weight[...], up_weight[...]
    )


def own_rows(pieces, gate_weight, up_weight, down_weight):
    depth, hidden_units = gate_weight.shape
    count = sum(piece.shape[1] for piece in pieces)
    tall = pl.BlockSpec((depth, TILE), lambda i: (0, i))
    wide = pl.BlockSpec((TILE, depth), lambda i: (i, 0))
    slim = pl.BlockSpec((count, TILE), lambda i: (0, i))
    unit = jax.ShapeDtypeStruct((count, hidden_units), jnp.bfloat16)
    return pl.pallas_call(
        functools.partial(own_kernel, len(pieces)),
        grid=(hidden_units // TILE,),
        in_specs=[pl.BlockSpec(memory_space=pl.ANY)] * len(pieces) + [tall, tall, wide],
        out_specs=[slim, slim, slim],
        out_shape=[unit, unit, unit],
        scratch_shapes=[
            pltpu.VMEM((2, count, depth), jnp.bfloat16),
            pltpu.SemaphoreType.DMA((len(pieces),)),
        ],
        compiler_params=pltpu.CompilerParams(vmem_limit_bytes=24 * 2**20),
        cost_estimate=pl.CostEstimate(
            flops=6 * count * depth * hidden_units,
            bytes_accessed=6 * depth * hidden_units,
            transcendentals=count * hidden_units,
        ),
        name="own_rows",
    )(*pieces, gate_weight, up_weight, down_weight)


def partial_kernel(
    hidden, grad_pre, grad_lifted, gate_weight, up_weight, down_weight,
    kept, sent, grad_pre_t, grad_lifted_t,
):
    part = kept.shape[1]

    @pl.when(pl.program_id(0) == 0)
    def _():
        grad_pre_t[...] = grad_pre[...].T
        grad_lifted_t[...] = grad_lifted[...].T

    partial_out = jnp.dot(hidden[...], down_weight[...], preferred_element_type=jnp.float32)
    partial_in = (
        jnp.dot(gate_weight[...], grad_pre_t[...], preferred_element_type=jnp.float32)
        + jnp.dot(up_weight[...], grad_lifted_t[...], preferred_element_type=jnp.float32)
    ).T
    for index, total in enumerate((partial_out, partial_in)):
        kept[index] = total[:part].astype(kept.dtype)
        sent[index] = total[part:].astype(sent.dtype)


def partial_sums(units, gate_weight, up_weight, down_weight):
    depth, hidden_units = gate_weight.shape
    count = units[0].shape[0]
    whole = pl.BlockSpec((count, hidden_units), lambda i: (0, 0))
    wide = pl.BlockSpec((COLUMNS, hidden_units), lambda i: (i, 0))
    tall = pl.BlockSpec((hidden_units, COLUMNS), lambda i: (0, i))
    slim = pl.BlockSpec((2, count // 2, COLUMNS), lambda i: (0, 0, i))
    kept = jax.ShapeDtypeStruct((2, count // 2, depth), jnp.bfloat16)
    return pl.pallas_call(
        partial_kernel,
        grid=(depth // COLUMNS,),
        in_specs=[whole, whole, whole, wide, wide, tall],
        out_specs=[slim, slim],
        out_shape=[kept, kept],
        scratch_shapes=[pltpu.VMEM((hidden_units, count), jnp.bfloat16)] * 2,
        compiler_params=pltpu.CompilerParams(vmem_limit_bytes=24 * 2**20),
        cost_estimate=pl.CostEstimate(
            flops=6 * count * depth * hidden_units,
            bytes_accessed=6 * depth * hidden_units,
            transcendentals=0,
        ),
        name="partial_sums",
    )(*units, gate_weight, up_weight, down_weight)


def all_kernel(n_own, n_rest, *refs):
    first, refs = refs[0], refs[1:]
    own_pieces, rest_pieces, refs = refs[:n_own], refs[n_own : n_own + n_rest], refs[n_own + n_rest :]
    own_hidden, own_grad_pre, own_grad_lifted, gate_weight, up_weight, down_weight = refs[:6]
    grad_gate, grad_up, grad_down = refs[6:9]
    rows, own, normed_t, grad_out, grad_out_t, hidden, grad_pre, grad_lifted, arrived = refs[9:]
    step = pl.program_id(0)
    mine = own.shape[1]
    width = normed_t.shape[0]

    @pl.when(step == 0)
    def _():
        columns = pl.ds(pl.multiple_of(first[0], 128), width)
        pack([piece.at[:, :, columns] for piece in own_pieces], own, arrived)
        pack(rest_pieces, rows, arrived)
        grad_out_t[...] = rows[1].T
        normed_t[:, :mine] = own[0].T
        normed_t[:, mine:] = rows[0, :, columns].T
        grad_out[:mine] = own[1]
        grad_out[mine:] = rows[1, :, columns]

    hidden[:mine] = own_hidden[...]
    grad_pre[:mine] = own_grad_pre[...]
    grad_lifted[:mine] = own_grad_lifted[...]
    grad_hidden = jnp.dot(down_weight[...], grad_out_t[...], preferred_element_type=jnp.float32).T
    hidden[mine:], grad_pre[mine:], grad_lifted[mine:] = activations(
        rows[0], grad_hidden, gate_weight[...], up_weight[...]
    )
    grad_gate[...] = jnp.dot(
        normed_t[...], grad_pre[...], preferred_element_type=jnp.float32
    ).astype(grad_gate.dtype)
    grad_up[...] = jnp.dot(
        normed_t[...], grad_lifted[...], preferred_element_type=jnp.float32
    ).astype(grad_up.dtype)
    grad_down[...] = jnp.dot(
        hidden[...].T, grad_out[...], preferred_element_type=jnp.float32
    ).astype(grad_down.dtype)


def all_rows(first, own_pieces, rest_pieces, units, gate_weight, up_weight, down_weight, width):
    depth, hidden_units = gate_weight.shape
    mine = sum(piece.shape[1] for piece in own_pieces)
    most = sum(piece.shape[1] for piece in rest_pieces)
    count = mine + most
    tall = pl.BlockSpec((depth, TILE), lambda i: (0, i))
    wide = pl.BlockSpec((TILE, depth), lambda i: (i, 0))
    slim = pl.BlockSpec((mine, TILE), lambda i: (0, i))
    n_pieces = len(own_pieces) + len(rest_pieces)
    return pl.pallas_call(
        functools.partial(all_kernel, len(own_pieces), len(rest_pieces)),
        grid=(hidden_units // TILE,),
        in_specs=[pl.BlockSpec(memory_space=pltpu.SMEM)]
        + [pl.BlockSpec(memory_space=pl.ANY)] * n_pieces
        + [slim, slim, slim, tall, tall, wide],
        out_specs=[
            pl.BlockSpec((width, TILE), lambda i: (0, i)),
            pl.BlockSpec((width, TILE), lambda i: (0, i)),
            pl.BlockSpec((TILE, width), lambda i: (i, 0)),
        ],
        out_shape=[
            jax.ShapeDtypeStruct((width, hidden_units), jnp.bfloat16),
            jax.ShapeDtypeStruct((width, hidden_units), jnp.bfloat16),
            jax.ShapeDtypeStruct((hidden_units, width), jnp.bfloat16),
        ],
        scratch_shapes=[
            pltpu.VMEM((2, most, depth), jnp.bfloat16),
            pltpu.VMEM((2, mine, width), jnp.bfloat16),
            pltpu.VMEM((width, count), jnp.bfloat16),
            pltpu.VMEM((count, width), jnp.bfloat16),
            pltpu.VMEM((depth, most), jnp.bfloat16),
            pltpu.VMEM((count, TILE), jnp.bfloat16),
            pltpu.VMEM((count, TILE), jnp.bfloat16),
            pltpu.VMEM((count, TILE), jnp.bfloat16),
            pltpu.SemaphoreType.DMA((max(len(own_pieces), len(rest_pieces)),)),
        ],
        compiler_params=pltpu.CompilerParams(vmem_limit_bytes=48 * 2**20),
        cost_estimate=pl.CostEstimate(
            flops=6 * most * depth * hidden_units + 6 * count * width * hidden_units,
            bytes_accessed=6 * (depth + width) * hidden_units,
            transcendentals=most * hidden_units,
        ),
        name="all_rows",
    )(first, *own_pieces, *rest_pieces, *units, gate_weight, up_weight, down_weight)


def gather_tokens(tokens, norm_scale_vector, gate_weight, up_weight, down_weight, cotangent):
    n_dp = lax.axis_size("dp")
    n_tp = lax.axis_size("tp")
    width = tokens.shape[1] // n_dp
    first = (lax.axis_index("dp") * width).astype(jnp.int32).reshape(1)
    rows = tokens.shape[0]

    def swap(array, dp_bits, tp_bits):
        pairs = [
            (d * n_tp + t, (d ^ dp_bits) * n_tp + (t ^ tp_bits))
            for d in range(n_dp)
            for t in range(n_tp)
        ]
        return lax.ppermute(array, ("dp", "tp"), pairs)

    expanded_hidden = tokens.astype(jnp.float32)
    reciprocal_root_mean = lax.rsqrt(
        jnp.mean(expanded_hidden * expanded_hidden, axis=-1, keepdims=True) + 1e-05
    )
    unit_input = expanded_hidden * reciprocal_root_mean
    rescaled_input = (unit_input * norm_scale_vector).astype(jnp.bfloat16)
    shard = jnp.stack([rescaled_input, cotangent])
    shards = [shard] + [swap(shard, 0, b) for b in range(2, n_tp, 2)]
    near = [jnp.concatenate(group, axis=1) for group in (shards[:2], shards[2:])]
    far = [swap(piece, 0, 1) for piece in near]
    rest_early, rest_late = ([swap(piece, b, 0) for b in range(1, n_dp)] for piece in near)
    units = own_rows(near + far, gate_weight, up_weight, down_weight)
    units, rest_early = lax.optimization_barrier((units, rest_early))
    kept, sent = partial_sums(units, gate_weight, up_weight, down_weight)
    rest_early += [swap(piece, 0, 1) for piece in rest_early]
    kept, sent, rest_early, rest_late = lax.optimization_barrier(
        (kept, sent, rest_early, rest_late)
    )
    rest_late += [swap(piece, 0, 1) for piece in rest_late]

    pair = (kept.astype(jnp.float32) + swap(sent, 0, 1).astype(jnp.float32)).astype(jnp.bfloat16)
    parts = [swap(pair[:, k * rows : (k + 1) * rows], 0, 2 * k) for k in range(1, n_tp // 2)]
    weight_gradients = all_rows(
        first, near + far, rest_early + rest_late, units, gate_weight, up_weight, down_weight, width
    )
    parts, weight_gradients = lax.optimization_barrier((parts, weight_gradients))
    total = pair[:, :rows].astype(jnp.float32) + sum(part.astype(jnp.float32) for part in parts)
    branch, grad_normed = total[0], total[1]
    mixed = (expanded_hidden + branch).astype(jnp.bfloat16)
    gain_applied = grad_normed * norm_scale_vector
    inner_product = jnp.mean(gain_applied * unit_input, axis=-1, keepdims=True)
    token_gradient = (
        cotangent.astype(jnp.float32)
        + reciprocal_root_mean * (gain_applied - unit_input * inner_product)
    ).astype(jnp.bfloat16)
    return mixed, token_gradient, *weight_gradients


def sum_weight_gradients(tokens, norm_scale_vector, gate_weight, up_weight, down_weight, cotangent):
    expanded_hidden = tokens.astype(jnp.float32)
    reciprocal_root_mean = lax.rsqrt(
        jnp.mean(expanded_hidden * expanded_hidden, axis=-1, keepdims=True) + 1e-05
    )
    unit_input = expanded_hidden * reciprocal_root_mean
    rescaled_input = (unit_input * norm_scale_vector).astype(jnp.bfloat16)
    normed_all = lax.all_gather(rescaled_input, "tp", axis=0, tiled=True)
    gate = jnp.dot(normed_all, gate_weight, preferred_element_type=jnp.float32)
    lifted = jnp.dot(normed_all, up_weight, preferred_element_type=jnp.float32)
    sigmoid_gate = jax.nn.sigmoid(gate)
    activated = gate * sigmoid_gate
    hidden = (activated * lifted).astype(jnp.bfloat16)
    branch = lax.psum_scatter(
        jnp.dot(hidden, down_weight, preferred_element_type=jnp.float32).astype(jnp.bfloat16),
        "tp",
        scatter_dimension=0,
        tiled=True,
    ).astype(jnp.float32)
    mixed = (expanded_hidden + branch).astype(jnp.bfloat16)
    grad_all = lax.all_gather(cotangent, "tp", axis=0, tiled=True)
    grad_hidden = contract_cols(grad_all, down_weight)
    grad_pre = (grad_hidden * lifted * sigmoid_gate * (1.0 + gate * (1.0 - sigmoid_gate))).astype(
        jnp.bfloat16
    )
    grad_lifted = (grad_hidden * activated).astype(jnp.bfloat16)
    grad_normed = lax.psum_scatter(
        (contract_cols(grad_pre, gate_weight) + contract_cols(grad_lifted, up_weight)).astype(
            jnp.bfloat16
        ),
        "tp",
        scatter_dimension=0,
        tiled=True,
    ).astype(jnp.float32)
    gain_applied = grad_normed * norm_scale_vector
    inner_product = jnp.mean(gain_applied * unit_input, axis=-1, keepdims=True)
    token_gradient = (
        cotangent.astype(jnp.float32)
        + reciprocal_root_mean * (gain_applied - unit_input * inner_product)
    ).astype(jnp.bfloat16)
    weight_gate = contract_rows(normed_all, grad_pre).astype(jnp.bfloat16)
    weight_up = contract_rows(normed_all, grad_lifted).astype(jnp.bfloat16)
    weight_down = contract_rows(hidden, grad_all).astype(jnp.bfloat16)
    sum_gate, sum_up, sum_down = (
        lax.psum_scatter(weight_gate, "dp", scatter_dimension=0, tiled=True).astype(jnp.float32),
        lax.psum_scatter(weight_up, "dp", scatter_dimension=0, tiled=True).astype(jnp.float32),
        lax.psum_scatter(weight_down, "dp", scatter_dimension=1, tiled=True).astype(jnp.float32),
    )
    return (
        mixed,
        token_gradient,
        sum_gate.astype(jnp.bfloat16),
        sum_up.astype(jnp.bfloat16),
        sum_down.astype(jnp.bfloat16),
    )


def solution(mesh):
    n_tp = mesh.shape["tp"]
    in_specs = (
        P(("dp", "tp"), None),
        P(),
        P(None, "tp"),
        P(None, "tp"),
        P("tp", None),
        P(("dp", "tp"), None),
    )
    out_specs = (
        P(("dp", "tp"), None),
        P(("dp", "tp"), None),
        P("dp", "tp"),
        P("dp", "tp"),
        P("tp", "dp"),
    )

    def run(tokens, norm_scale_vector, gate_weight, up_weight, down_weight, cotangent):
        gathered = tokens.size + cotangent.size
        weights = (gate_weight.size + up_weight.size + down_weight.size) // n_tp
        local = gather_tokens if gathered <= weights else sum_weight_gradients
        return jax.shard_map(
            local, mesh=mesh, in_specs=in_specs, out_specs=out_specs, check_vma=False
        )(tokens, norm_scale_vector, gate_weight, up_weight, down_weight, cotangent)

    return run
```

```python
import functools

import jax
import jax.numpy as jnp
from jax import lax
from jax.experimental import pallas as pl
from jax.experimental.pallas import tpu as pltpu
from jax.sharding import PartitionSpec as P


def contract_rows(left, right):
    return lax.dot_general(
        left, right, (((0,), (0,)), ((), ())), preferred_element_type=jnp.float32
    )


def contract_cols(left, right):
    return lax.dot_general(
        left, right, (((1,), (1,)), ((), ())), preferred_element_type=jnp.float32
    )


TILE = 256
CHUNK = 1024


def activations(normed, grad_out_t, gate_weight, up_weight, down_weight):
    gate = jnp.dot(normed, gate_weight, preferred_element_type=jnp.float32)
    lifted = jnp.dot(normed, up_weight, preferred_element_type=jnp.float32)
    grad_hidden = jnp.dot(down_weight, grad_out_t, preferred_element_type=jnp.float32).T
    sigmoid_gate = jax.nn.sigmoid(gate)
    activated = gate * sigmoid_gate
    hidden = (activated * lifted).astype(jnp.bfloat16)
    grad_pre = (grad_hidden * lifted * sigmoid_gate * (1.0 + gate * (1.0 - sigmoid_gate))).astype(
        jnp.bfloat16
    )
    grad_lifted = (grad_hidden * activated).astype(jnp.bfloat16)
    return hidden, grad_pre, grad_lifted


def copy_all(copies):
    for copy in copies:
        copy.start()
    for copy in copies:
        copy.wait()


def pack(pieces, rows, arrived):
    copies, at = [], 0
    for i, piece in enumerate(pieces):
        height = piece.shape[1]
        copies.append(pltpu.make_async_copy(piece, rows.at[:, pl.ds(at, height)], arrived.at[i]))
        at += height
    copy_all(copies)


def own_kernel(*refs):
    replica, refs = refs[0], refs[1:]
    (near, late, far_gathered, far_late), refs = refs[:4], refs[4:]
    gate_weight, up_weight, down_weight, hidden, grad_pre, grad_lifted, kept, sent = refs[:8]
    rows, grad_out_t, out_sum, in_sum, arrived = refs[8:]
    step = pl.program_id(0)
    part = kept.shape[1]

    @pl.when(step == 0)
    def _():
        pack([near, late, far_gathered.at[replica[0]], far_late], rows, arrived)
        grad_out_t[...] = rows[1].T
        out_sum[...] = jnp.zeros_like(out_sum)
        in_sum[...] = jnp.zeros_like(in_sum)

    hidden[...], grad_pre[...], grad_lifted[...] = activations(
        rows[0], grad_out_t[...], gate_weight[...], up_weight[...], down_weight[...]
    )
    grad_pre_t, grad_lifted_t = grad_pre[...].T, grad_lifted[...].T
    for at in range(0, out_sum.shape[1], CHUNK):
        here = slice(at, at + CHUNK)
        out_sum[:, here] += jnp.dot(
            hidden[...], down_weight[:, here], preferred_element_type=jnp.float32
        )
        in_sum[here] += jnp.dot(
            gate_weight[here], grad_pre_t, preferred_element_type=jnp.float32
        ) + jnp.dot(up_weight[here], grad_lifted_t, preferred_element_type=jnp.float32)

    @pl.when(step == pl.num_programs(0) - 1)
    def _():
        kept[0] = out_sum[:part].astype(kept.dtype)
        sent[0] = out_sum[part:].astype(sent.dtype)
        summed = in_sum[...].T
        kept[1] = summed[:part].astype(kept.dtype)
        sent[1] = summed[part:].astype(sent.dtype)


def own_rows(replica, near, late, far_gathered, far_late, gate_weight, up_weight, down_weight):
    depth, hidden_units = gate_weight.shape
    count = 2 * (near.shape[1] + late.shape[1])
    tall = pl.BlockSpec((depth, TILE), lambda i: (0, i))
    wide = pl.BlockSpec((TILE, depth), lambda i: (i, 0))
    slim = pl.BlockSpec((count, TILE), lambda i: (0, i))
    whole = pl.BlockSpec((2, count // 2, depth), lambda i: (0, 0, 0))
    kept = jax.ShapeDtypeStruct((2, count // 2, depth), jnp.bfloat16)
    unit = jax.ShapeDtypeStruct((count, hidden_units), jnp.bfloat16)
    return pl.pallas_call(
        own_kernel,
        grid=(hidden_units // TILE,),
        in_specs=[pl.BlockSpec(memory_space=pltpu.SMEM)]
        + [pl.BlockSpec(memory_space=pl.ANY)] * 4
        + [tall, tall, wide],
        out_specs=[slim, slim, slim, whole, whole],
        out_shape=[unit, unit, unit, kept, kept],
        scratch_shapes=[
            pltpu.VMEM((2, count, depth), jnp.bfloat16),
            pltpu.VMEM((depth, count), jnp.bfloat16),
            pltpu.VMEM((count, depth), jnp.float32),
            pltpu.VMEM((depth, count), jnp.float32),
            pltpu.SemaphoreType.DMA((4,)),
        ],
        compiler_params=pltpu.CompilerParams(vmem_limit_bytes=48 * 2**20),
        cost_estimate=pl.CostEstimate(
            flops=12 * count * depth * hidden_units,
            bytes_accessed=6 * depth * hidden_units,
            transcendentals=count * hidden_units,
        ),
        name="own_rows",
    )(replica, near, late, far_gathered, far_late, gate_weight, up_weight, down_weight)


def all_kernel(n_rest, *refs):
    replica, refs = refs[0], refs[1:]
    (late, far_late, gathered, far_gathered), refs = refs[:4], refs[4:]
    rest_late, refs = refs[:n_rest], refs[n_rest:]
    own_hidden, own_grad_pre, own_grad_lifted, gate_weight, up_weight, down_weight = refs[:6]
    grad_gate, grad_up, grad_down = refs[6:9]
    rows, own, normed_t, grad_out, grad_out_t, hidden, grad_pre, grad_lifted, arrived = refs[9:]
    step = pl.program_id(0)
    mine = own.shape[1]
    width = normed_t.shape[0]

    @pl.when(step == 0)
    def _():
        me = replica[0]
        columns = pl.ds(pl.multiple_of(me * width, 128), width)
        own_pieces = [gathered.at[me], late, far_gathered.at[me], far_late]
        pack([piece.at[:, :, columns] for piece in own_pieces], own, arrived)
        others = range(1, gathered.shape[0])
        rest_pieces = [part.at[me ^ b] for part in (gathered, far_gathered) for b in others]
        pack(rest_pieces + list(rest_late), rows, arrived)
        grad_out_t[...] = rows[1].T
        normed_t[:, :mine] = own[0].T
        normed_t[:, mine:] = rows[0, :, columns].T
        grad_out[:mine] = own[1]
        grad_out[mine:] = rows[1, :, columns]

    hidden[:mine] = own_hidden[...]
    grad_pre[:mine] = own_grad_pre[...]
    grad_lifted[:mine] = own_grad_lifted[...]
    hidden[mine:], grad_pre[mine:], grad_lifted[mine:] = activations(
        rows[0], grad_out_t[...], gate_weight[...], up_weight[...], down_weight[...]
    )
    grad_gate[...] = jnp.dot(
        normed_t[...], grad_pre[...], preferred_element_type=jnp.float32
    ).astype(grad_gate.dtype)
    grad_up[...] = jnp.dot(
        normed_t[...], grad_lifted[...], preferred_element_type=jnp.float32
    ).astype(grad_up.dtype)
    grad_down[...] = jnp.dot(
        hidden[...].T, grad_out[...], preferred_element_type=jnp.float32
    ).astype(grad_down.dtype)


def all_rows(replica, own_late, gathered, rest_late, units, gate_weight, up_weight, down_weight):
    depth, hidden_units = gate_weight.shape
    mine = units[0].shape[0]
    count = mine * gathered[0].shape[0]
    most = count - mine
    width = depth // gathered[0].shape[0]
    tall = pl.BlockSpec((depth, TILE), lambda i: (0, i))
    wide = pl.BlockSpec((TILE, depth), lambda i: (i, 0))
    slim = pl.BlockSpec((mine, TILE), lambda i: (0, i))
    return pl.pallas_call(
        functools.partial(all_kernel, len(rest_late)),
        grid=(hidden_units // TILE,),
        in_specs=[pl.BlockSpec(memory_space=pltpu.SMEM)]
        + [pl.BlockSpec(memory_space=pl.ANY)] * (4 + len(rest_late))
        + [slim, slim, slim, tall, tall, wide],
        out_specs=[
            pl.BlockSpec((width, TILE), lambda i: (0, i)),
            pl.BlockSpec((width, TILE), lambda i: (0, i)),
            pl.BlockSpec((TILE, width), lambda i: (i, 0)),
        ],
        out_shape=[
            jax.ShapeDtypeStruct((width, hidden_units), jnp.bfloat16),
            jax.ShapeDtypeStruct((width, hidden_units), jnp.bfloat16),
            jax.ShapeDtypeStruct((hidden_units, width), jnp.bfloat16),
        ],
        scratch_shapes=[
            pltpu.VMEM((2, most, depth), jnp.bfloat16),
            pltpu.VMEM((2, mine, width), jnp.bfloat16),
            pltpu.VMEM((width, count), jnp.bfloat16),
            pltpu.VMEM((count, width), jnp.bfloat16),
            pltpu.VMEM((depth, most), jnp.bfloat16),
            pltpu.VMEM((count, TILE), jnp.bfloat16),
            pltpu.VMEM((count, TILE), jnp.bfloat16),
            pltpu.VMEM((count, TILE), jnp.bfloat16),
            pltpu.SemaphoreType.DMA((4 * gathered[0].shape[0],)),
        ],
        compiler_params=pltpu.CompilerParams(vmem_limit_bytes=48 * 2**20),
        cost_estimate=pl.CostEstimate(
            flops=6 * most * depth * hidden_units + 6 * count * width * hidden_units,
            bytes_accessed=6 * (depth + width) * hidden_units,
            transcendentals=most * hidden_units,
        ),
        name="all_rows",
    )(replica, *own_late, *gathered, *rest_late, *units, gate_weight, up_weight, down_weight)


def gather_tokens(tokens, norm_scale_vector, gate_weight, up_weight, down_weight, cotangent):
    n_dp = lax.axis_size("dp")
    n_tp = lax.axis_size("tp")
    replica = lax.axis_index("dp").astype(jnp.int32).reshape(1)
    rows = tokens.shape[0]

    def swap(array, dp_bits, tp_bits):
        pairs = [
            (d * n_tp + t, (d ^ dp_bits) * n_tp + (t ^ tp_bits))
            for d in range(n_dp)
            for t in range(n_tp)
        ]
        return lax.ppermute(array, ("dp", "tp"), pairs)

    expanded_hidden = tokens.astype(jnp.float32)
    reciprocal_root_mean = lax.rsqrt(
        jnp.mean(expanded_hidden * expanded_hidden, axis=-1, keepdims=True) + 1e-05
    )
    unit_input = expanded_hidden * reciprocal_root_mean
    rescaled_input = (unit_input * norm_scale_vector).astype(jnp.bfloat16)
    shard = jnp.stack([rescaled_input, cotangent])
    gathered = lax.all_gather(shard, "dp", axis=0)
    late = jnp.concatenate([swap(shard, 0, b) for b in range(2, n_tp, 2)], axis=1)
    far_gathered, far_late = swap(gathered, 0, 1), swap(late, 0, 1)
    rest = [swap(late, b, 0) for b in range(1, n_dp)]
    *units, kept, sent = own_rows(
        replica, shard, late, far_gathered, far_late, gate_weight, up_weight, down_weight
    )
    kept, sent, rest = lax.optimization_barrier((kept, sent, rest))
    rest += [swap(piece, 0, 1) for piece in rest]

    pair = (kept.astype(jnp.float32) + swap(sent, 0, 1).astype(jnp.float32)).astype(jnp.bfloat16)
    parts = [swap(pair[:, k * rows : (k + 1) * rows], 0, 2 * k) for k in range(1, n_tp // 2)]
    weight_gradients = all_rows(
        replica,
        (late, far_late),
        (gathered, far_gathered),
        rest,
        units,
        gate_weight,
        up_weight,
        down_weight,
    )
    parts, weight_gradients = lax.optimization_barrier((parts, weight_gradients))
    total = pair[:, :rows].astype(jnp.float32) + sum(part.astype(jnp.float32) for part in parts)
    branch, grad_normed = total[0], total[1]
    mixed = (expanded_hidden + branch).astype(jnp.bfloat16)
    gain_applied = grad_normed * norm_scale_vector
    inner_product = jnp.mean(gain_applied * unit_input, axis=-1, keepdims=True)
    token_gradient = (
        cotangent.astype(jnp.float32)
        + reciprocal_root_mean * (gain_applied - unit_input * inner_product)
    ).astype(jnp.bfloat16)
    return mixed, token_gradient, *weight_gradients


def sum_weight_gradients(tokens, norm_scale_vector, gate_weight, up_weight, down_weight, cotangent):
    expanded_hidden = tokens.astype(jnp.float32)
    reciprocal_root_mean = lax.rsqrt(
        jnp.mean(expanded_hidden * expanded_hidden, axis=-1, keepdims=True) + 1e-05
    )
    unit_input = expanded_hidden * reciprocal_root_mean
    rescaled_input = (unit_input * norm_scale_vector).astype(jnp.bfloat16)
    normed_all = lax.all_gather(rescaled_input, "tp", axis=0, tiled=True)
    gate = jnp.dot(normed_all, gate_weight, preferred_element_type=jnp.float32)
    lifted = jnp.dot(normed_all, up_weight, preferred_element_type=jnp.float32)
    sigmoid_gate = jax.nn.sigmoid(gate)
    activated = gate * sigmoid_gate
    hidden = (activated * lifted).astype(jnp.bfloat16)
    branch = lax.psum_scatter(
        jnp.dot(hidden, down_weight, preferred_element_type=jnp.float32).astype(jnp.bfloat16),
        "tp",
        scatter_dimension=0,
        tiled=True,
    ).astype(jnp.float32)
    mixed = (expanded_hidden + branch).astype(jnp.bfloat16)
    grad_all = lax.all_gather(cotangent, "tp", axis=0, tiled=True)
    grad_hidden = contract_cols(grad_all, down_weight)
    grad_pre = (grad_hidden * lifted * sigmoid_gate * (1.0 + gate * (1.0 - sigmoid_gate))).astype(
        jnp.bfloat16
    )
    grad_lifted = (grad_hidden * activated).astype(jnp.bfloat16)
    grad_normed = lax.psum_scatter(
        (contract_cols(grad_pre, gate_weight) + contract_cols(grad_lifted, up_weight)).astype(
            jnp.bfloat16
        ),
        "tp",
        scatter_dimension=0,
        tiled=True,
    ).astype(jnp.float32)
    gain_applied = grad_normed * norm_scale_vector
    inner_product = jnp.mean(gain_applied * unit_input, axis=-1, keepdims=True)
    token_gradient = (
        cotangent.astype(jnp.float32)
        + reciprocal_root_mean * (gain_applied - unit_input * inner_product)
    ).astype(jnp.bfloat16)
    weight_gate = contract_rows(normed_all, grad_pre).astype(jnp.bfloat16)
    weight_up = contract_rows(normed_all, grad_lifted).astype(jnp.bfloat16)
    weight_down = contract_rows(hidden, grad_all).astype(jnp.bfloat16)
    sum_gate, sum_up, sum_down = (
        lax.psum_scatter(weight_gate, "dp", scatter_dimension=0, tiled=True).astype(jnp.float32),
        lax.psum_scatter(weight_up, "dp", scatter_dimension=0, tiled=True).astype(jnp.float32),
        lax.psum_scatter(weight_down, "dp", scatter_dimension=1, tiled=True).astype(jnp.float32),
    )
    return (
        mixed,
        token_gradient,
        sum_gate.astype(jnp.bfloat16),
        sum_up.astype(jnp.bfloat16),
        sum_down.astype(jnp.bfloat16),
    )


def solution(mesh):
    n_tp = mesh.shape["tp"]
    in_specs = (
        P(("dp", "tp"), None),
        P(),
        P(None, "tp"),
        P(None, "tp"),
        P("tp", None),
        P(("dp", "tp"), None),
    )
    out_specs = (
        P(("dp", "tp"), None),
        P(("dp", "tp"), None),
        P("dp", "tp"),
        P("dp", "tp"),
        P("tp", "dp"),
    )

    def run(tokens, norm_scale_vector, gate_weight, up_weight, down_weight, cotangent):
        gathered = tokens.size + cotangent.size
        weights = (gate_weight.size + up_weight.size + down_weight.size) // n_tp
        local = gather_tokens if gathered <= weights else sum_weight_gradients
        return jax.shard_map(
            local, mesh=mesh, in_specs=in_specs, out_specs=out_specs, check_vma=False
        )(tokens, norm_scale_vector, gate_weight, up_weight, down_weight, cotangent)

    return run
```

```python
import functools

import jax
import jax.numpy as jnp
from jax import lax
from jax.experimental import pallas as pl
from jax.experimental.pallas import tpu as pltpu
from jax.sharding import PartitionSpec as P


def contract_rows(left, right):
    return lax.dot_general(
        left, right, (((0,), (0,)), ((), ())), preferred_element_type=jnp.float32
    )


def contract_cols(left, right):
    return lax.dot_general(
        left, right, (((1,), (1,)), ((), ())), preferred_element_type=jnp.float32
    )


TILE = 256
CHUNK = 1024


def activations(normed, grad_out_t, gate_weight, up_weight, down_weight):
    gate = jnp.dot(normed, gate_weight, preferred_element_type=jnp.float32)
    lifted = jnp.dot(normed, up_weight, preferred_element_type=jnp.float32)
    grad_hidden = jnp.dot(down_weight, grad_out_t, preferred_element_type=jnp.float32).T
    sigmoid_gate = jax.nn.sigmoid(gate)
    activated = gate * sigmoid_gate
    hidden = (activated * lifted).astype(jnp.bfloat16)
    grad_pre = (grad_hidden * lifted * sigmoid_gate * (1.0 + gate * (1.0 - sigmoid_gate))).astype(
        jnp.bfloat16
    )
    grad_lifted = (grad_hidden * activated).astype(jnp.bfloat16)
    return hidden, grad_pre, grad_lifted


def pack(pieces, rows, arrived):
    copies, at = [], 0
    for i, piece in enumerate(pieces):
        height = piece.shape[1]
        copies.append(pltpu.make_async_copy(piece, rows.at[:, pl.ds(at, height)], arrived.at[i]))
        at += height
    for copy in copies:
        copy.start()
    for copy in copies:
        copy.wait()


def height(pieces):
    return sum(piece.shape[1] for piece in pieces)


def first_kernel(n_pieces, *refs):
    pieces, refs = refs[:n_pieces], refs[n_pieces:]
    gate_weight, up_weight, down_weight, hidden, grad_pre, grad_lifted, kept, sent = refs[:8]
    rows, grad_out_t, out_sum, in_sum, arrived = refs[8:]
    step = pl.program_id(0)
    part = kept.shape[1]
    own = out_sum.shape[0]

    @pl.when(step == 0)
    def _():
        pack(pieces, rows, arrived)
        grad_out_t[...] = rows[1].T
        out_sum[...] = jnp.zeros_like(out_sum)
        in_sum[...] = jnp.zeros_like(in_sum)

    hidden[...], grad_pre[...], grad_lifted[...] = activations(
        rows[0], grad_out_t[...], gate_weight[...], up_weight[...], down_weight[...]
    )
    grad_pre_t, grad_lifted_t = grad_pre[:own].T, grad_lifted[:own].T
    for at in range(0, out_sum.shape[1], CHUNK):
        here = slice(at, at + CHUNK)
        out_sum[:, here] += jnp.dot(
            hidden[:own], down_weight[:, here], preferred_element_type=jnp.float32
        )
        in_sum[here] += jnp.dot(
            gate_weight[here], grad_pre_t, preferred_element_type=jnp.float32
        ) + jnp.dot(up_weight[here], grad_lifted_t, preferred_element_type=jnp.float32)

    @pl.when(step == pl.num_programs(0) - 1)
    def _():
        kept[0] = out_sum[:part].astype(kept.dtype)
        sent[0] = out_sum[part:].astype(sent.dtype)
        summed = in_sum[...].T
        kept[1] = summed[:part].astype(kept.dtype)
        sent[1] = summed[part:].astype(sent.dtype)


def first_rows(own_pieces, more_pieces, gate_weight, up_weight, down_weight):
    depth, hidden_units = gate_weight.shape
    pieces = own_pieces + more_pieces
    own, count = height(own_pieces), height(pieces)
    tall = pl.BlockSpec((depth, TILE), lambda i: (0, i))
    wide = pl.BlockSpec((TILE, depth), lambda i: (i, 0))
    slim = pl.BlockSpec((count, TILE), lambda i: (0, i))
    whole = pl.BlockSpec((2, own // 2, depth), lambda i: (0, 0, 0))
    kept = jax.ShapeDtypeStruct((2, own // 2, depth), jnp.bfloat16)
    unit = jax.ShapeDtypeStruct((count, hidden_units), jnp.bfloat16)
    return pl.pallas_call(
        functools.partial(first_kernel, len(pieces)),
        grid=(hidden_units // TILE,),
        in_specs=[pl.BlockSpec(memory_space=pl.ANY)] * len(pieces) + [tall, tall, wide],
        out_specs=[slim, slim, slim, whole, whole],
        out_shape=[unit, unit, unit, kept, kept],
        scratch_shapes=[
            pltpu.VMEM((2, count, depth), jnp.bfloat16),
            pltpu.VMEM((depth, count), jnp.bfloat16),
            pltpu.VMEM((own, depth), jnp.float32),
            pltpu.VMEM((depth, own), jnp.float32),
            pltpu.SemaphoreType.DMA((len(pieces),)),
        ],
        compiler_params=pltpu.CompilerParams(vmem_limit_bytes=44 * 2**20),
        cost_estimate=pl.CostEstimate(
            flops=6 * (count + own) * depth * hidden_units,
            bytes_accessed=6 * depth * hidden_units,
            transcendentals=count * hidden_units,
        ),
        name="first_rows",
    )(*pieces, gate_weight, up_weight, down_weight)


def all_kernel(n_first, n_last, *refs):
    replica, refs = refs[0], refs[1:]
    first_pieces, refs = refs[:n_first], refs[n_first:]
    last_pieces, refs = refs[:n_last], refs[n_last:]
    first_hidden, first_grad_pre, first_grad_lifted = refs[:3]
    gate_weight, up_weight, down_weight, grad_gate, grad_up, grad_down = refs[3:9]
    rows, first, normed_t, grad_out, grad_out_t, hidden, grad_pre, grad_lifted, arrived = refs[9:]
    ahead = first.shape[1]
    width = normed_t.shape[0]

    @pl.when(pl.program_id(0) == 0)
    def _():
        columns = pl.ds(pl.multiple_of(replica[0] * width, 128), width)
        pack(last_pieces, rows, arrived)
        pack([piece.at[:, :, columns] for piece in first_pieces], first, arrived)
        grad_out_t[...] = rows[1].T
        normed_t[:, :ahead] = first[0].T
        normed_t[:, ahead:] = rows[0, :, columns].T
        grad_out[:ahead] = first[1]
        grad_out[ahead:] = rows[1, :, columns]

    hidden[:ahead] = first_hidden[...]
    grad_pre[:ahead] = first_grad_pre[...]
    grad_lifted[:ahead] = first_grad_lifted[...]
    hidden[ahead:], grad_pre[ahead:], grad_lifted[ahead:] = activations(
        rows[0], grad_out_t[...], gate_weight[...], up_weight[...], down_weight[...]
    )
    grad_gate[...] = jnp.dot(
        normed_t[...], grad_pre[...], preferred_element_type=jnp.float32
    ).astype(grad_gate.dtype)
    grad_up[...] = jnp.dot(
        normed_t[...], grad_lifted[...], preferred_element_type=jnp.float32
    ).astype(grad_up.dtype)
    grad_down[...] = jnp.dot(
        hidden[...].T, grad_out[...], preferred_element_type=jnp.float32
    ).astype(grad_down.dtype)


def all_rows(replica, n_dp, first_pieces, last_pieces, units, gate_weight, up_weight, down_weight):
    depth, hidden_units = gate_weight.shape
    ahead, behind = height(first_pieces), height(last_pieces)
    count = ahead + behind
    width = depth // n_dp
    tall = pl.BlockSpec((depth, TILE), lambda i: (0, i))
    wide = pl.BlockSpec((TILE, depth), lambda i: (i, 0))
    slim = pl.BlockSpec((ahead, TILE), lambda i: (0, i))
    n_pieces = len(first_pieces), len(last_pieces)
    return pl.pallas_call(
        functools.partial(all_kernel, *n_pieces),
        grid=(hidden_units // TILE,),
        in_specs=[pl.BlockSpec(memory_space=pltpu.SMEM)]
        + [pl.BlockSpec(memory_space=pl.ANY)] * sum(n_pieces)
        + [slim, slim, slim, tall, tall, wide],
        out_specs=[
            pl.BlockSpec((width, TILE), lambda i: (0, i)),
            pl.BlockSpec((width, TILE), lambda i: (0, i)),
            pl.BlockSpec((TILE, width), lambda i: (i, 0)),
        ],
        out_shape=[
            jax.ShapeDtypeStruct((width, hidden_units), jnp.bfloat16),
            jax.ShapeDtypeStruct((width, hidden_units), jnp.bfloat16),
            jax.ShapeDtypeStruct((hidden_units, width), jnp.bfloat16),
        ],
        scratch_shapes=[
            pltpu.VMEM((2, behind, depth), jnp.bfloat16),
            pltpu.VMEM((2, ahead, width), jnp.bfloat16),
            pltpu.VMEM((width, count), jnp.bfloat16),
            pltpu.VMEM((count, width), jnp.bfloat16),
            pltpu.VMEM((depth, behind), jnp.bfloat16),
            pltpu.VMEM((count, TILE), jnp.bfloat16),
            pltpu.VMEM((count, TILE), jnp.bfloat16),
            pltpu.VMEM((count, TILE), jnp.bfloat16),
            pltpu.SemaphoreType.DMA((max(n_pieces),)),
        ],
        compiler_params=pltpu.CompilerParams(vmem_limit_bytes=40 * 2**20),
        cost_estimate=pl.CostEstimate(
            flops=6 * (behind * depth + count * width) * hidden_units,
            bytes_accessed=6 * (depth + width) * hidden_units,
            transcendentals=behind * hidden_units,
        ),
        name="all_rows",
    )(replica, *first_pieces, *last_pieces, *units, gate_weight, up_weight, down_weight)


def gather_tokens(tokens, norm_scale_vector, gate_weight, up_weight, down_weight, cotangent):
    n_dp = lax.axis_size("dp")
    n_tp = lax.axis_size("tp")
    replica = lax.axis_index("dp").astype(jnp.int32).reshape(1)
    rows = tokens.shape[0]

    def swap(array, dp_bits, tp_bits):
        pairs = [
            (d * n_tp + t, (d ^ dp_bits) * n_tp + (t ^ tp_bits))
            for d in range(n_dp)
            for t in range(n_tp)
        ]
        return lax.ppermute(array, ("dp", "tp"), pairs)

    def far(pieces):
        return [swap(piece, 0, 1) for piece in pieces]

    expanded_hidden = tokens.astype(jnp.float32)
    reciprocal_root_mean = lax.rsqrt(
        jnp.mean(expanded_hidden * expanded_hidden, axis=-1, keepdims=True) + 1e-05
    )
    unit_input = expanded_hidden * reciprocal_root_mean
    rescaled_input = (unit_input * norm_scale_vector).astype(jnp.bfloat16)
    unit0 = jnp.stack([rescaled_input, cotangent])
    unit1, unit2 = swap(unit0, 0, 2), swap(unit0, 0, 4)
    more = [swap(unit0, b, 0) for b in range(1, n_dp)]
    unit1, unit2, more = lax.optimization_barrier((unit1, unit2, more))
    unit3, across = swap(unit2, 0, 2), swap(unit1, 1, 0)
    far_more, far_unit0 = far(more), swap(unit0, 0, 1)
    unit3, across, far_more, far_unit0 = lax.optimization_barrier(
        (unit3, across, far_more, far_unit0)
    )
    last = jnp.concatenate([unit2, unit3], axis=1)
    late = jnp.concatenate([unit1, unit2, unit3], axis=1)
    own = [unit0, late, far_unit0, swap(late, 0, 1)]
    more += [across] + far_more + far([across])
    own, more = lax.optimization_barrier((own, more))
    rest = [swap(last, 1, 0)] + [swap(late, b, 0) for b in range(2, n_dp)]
    *units, kept, sent = first_rows(own, more, gate_weight, up_weight, down_weight)
    kept, sent, rest = lax.optimization_barrier((kept, sent, rest))
    rest += far(rest)

    pair = (kept.astype(jnp.float32) + swap(sent, 0, 1).astype(jnp.float32)).astype(jnp.bfloat16)
    parts = [swap(pair[:, k * rows : (k + 1) * rows], 0, 2 * k) for k in range(1, n_tp // 2)]
    weight_gradients = all_rows(
        replica, n_dp, own + more, rest, units, gate_weight, up_weight, down_weight
    )
    parts, weight_gradients = lax.optimization_barrier((parts, weight_gradients))
    total = pair[:, :rows].astype(jnp.float32) + sum(part.astype(jnp.float32) for part in parts)
    branch, grad_normed = total[0], total[1]
    mixed = (expanded_hidden + branch).astype(jnp.bfloat16)
    gain_applied = grad_normed * norm_scale_vector
    inner_product = jnp.mean(gain_applied * unit_input, axis=-1, keepdims=True)
    token_gradient = (
        cotangent.astype(jnp.float32)
        + reciprocal_root_mean * (gain_applied - unit_input * inner_product)
    ).astype(jnp.bfloat16)
    return mixed, token_gradient, *weight_gradients


def sum_weight_gradients(tokens, norm_scale_vector, gate_weight, up_weight, down_weight, cotangent):
    expanded_hidden = tokens.astype(jnp.float32)
    reciprocal_root_mean = lax.rsqrt(
        jnp.mean(expanded_hidden * expanded_hidden, axis=-1, keepdims=True) + 1e-05
    )
    unit_input = expanded_hidden * reciprocal_root_mean
    rescaled_input = (unit_input * norm_scale_vector).astype(jnp.bfloat16)
    normed_all = lax.all_gather(rescaled_input, "tp", axis=0, tiled=True)
    gate = jnp.dot(normed_all, gate_weight, preferred_element_type=jnp.float32)
    lifted = jnp.dot(normed_all, up_weight, preferred_element_type=jnp.float32)
    sigmoid_gate = jax.nn.sigmoid(gate)
    activated = gate * sigmoid_gate
    hidden = (activated * lifted).astype(jnp.bfloat16)
    branch = lax.psum_scatter(
        jnp.dot(hidden, down_weight, preferred_element_type=jnp.float32).astype(jnp.bfloat16),
        "tp",
        scatter_dimension=0,
        tiled=True,
    ).astype(jnp.float32)
    mixed = (expanded_hidden + branch).astype(jnp.bfloat16)
    grad_all = lax.all_gather(cotangent, "tp", axis=0, tiled=True)
    grad_hidden = contract_cols(grad_all, down_weight)
    grad_pre = (grad_hidden * lifted * sigmoid_gate * (1.0 + gate * (1.0 - sigmoid_gate))).astype(
        jnp.bfloat16
    )
    grad_lifted = (grad_hidden * activated).astype(jnp.bfloat16)
    grad_normed = lax.psum_scatter(
        (contract_cols(grad_pre, gate_weight) + contract_cols(grad_lifted, up_weight)).astype(
            jnp.bfloat16
        ),
        "tp",
        scatter_dimension=0,
        tiled=True,
    ).astype(jnp.float32)
    gain_applied = grad_normed * norm_scale_vector
    inner_product = jnp.mean(gain_applied * unit_input, axis=-1, keepdims=True)
    token_gradient = (
        cotangent.astype(jnp.float32)
        + reciprocal_root_mean * (gain_applied - unit_input * inner_product)
    ).astype(jnp.bfloat16)
    weight_gate = contract_rows(normed_all, grad_pre).astype(jnp.bfloat16)
    weight_up = contract_rows(normed_all, grad_lifted).astype(jnp.bfloat16)
    weight_down = contract_rows(hidden, grad_all).astype(jnp.bfloat16)
    sum_gate, sum_up, sum_down = (
        lax.psum_scatter(weight_gate, "dp", scatter_dimension=0, tiled=True).astype(jnp.float32),
        lax.psum_scatter(weight_up, "dp", scatter_dimension=0, tiled=True).astype(jnp.float32),
        lax.psum_scatter(weight_down, "dp", scatter_dimension=1, tiled=True).astype(jnp.float32),
    )
    return (
        mixed,
        token_gradient,
        sum_gate.astype(jnp.bfloat16),
        sum_up.astype(jnp.bfloat16),
        sum_down.astype(jnp.bfloat16),
    )


def solution(mesh):
    n_dp, n_tp = mesh.shape["dp"], mesh.shape["tp"]
    in_specs = (
        P(("dp", "tp"), None),
        P(),
        P(None, "tp"),
        P(None, "tp"),
        P("tp", None),
        P(("dp", "tp"), None),
    )
    out_specs = (
        P(("dp", "tp"), None),
        P(("dp", "tp"), None),
        P("dp", "tp"),
        P("dp", "tp"),
        P("tp", "dp"),
    )

    def run(tokens, norm_scale_vector, gate_weight, up_weight, down_weight, cotangent):
        gathered = tokens.size + cotangent.size
        weights = (gate_weight.size + up_weight.size + down_weight.size) // n_tp
        local = sum_weight_gradients
        if (n_dp, n_tp) == (4, 8) and gathered <= weights:
            local = gather_tokens
        return jax.shard_map(
            local, mesh=mesh, in_specs=in_specs, out_specs=out_specs, check_vma=False
        )(tokens, norm_scale_vector, gate_weight, up_weight, down_weight, cotangent)

    return run
```

```python
import functools

import jax
import jax.numpy as jnp
from jax import lax
from jax.experimental import pallas as pl
from jax.experimental.pallas import tpu as pltpu
from jax.sharding import PartitionSpec as P


def contract_rows(left, right):
    return lax.dot_general(
        left, right, (((0,), (0,)), ((), ())), preferred_element_type=jnp.float32
    )


def contract_cols(left, right):
    return lax.dot_general(
        left, right, (((1,), (1,)), ((), ())), preferred_element_type=jnp.float32
    )


TILE = 256
CHUNK = 1024


def project(normed, grad_out_t, gate_weight, up_weight, down_weight):
    gate = jnp.dot(normed, gate_weight, preferred_element_type=jnp.float32)
    lifted = jnp.dot(normed, up_weight, preferred_element_type=jnp.float32)
    grad_hidden = jnp.dot(down_weight, grad_out_t, preferred_element_type=jnp.float32).T
    return gate, lifted, grad_hidden


def activations(gate, lifted, grad_hidden):
    sigmoid_gate = jax.nn.sigmoid(gate)
    activated = gate * sigmoid_gate
    hidden = (activated * lifted).astype(jnp.bfloat16)
    grad_pre = (grad_hidden * lifted * sigmoid_gate * (1.0 + gate * (1.0 - sigmoid_gate))).astype(
        jnp.bfloat16
    )
    grad_lifted = (grad_hidden * activated).astype(jnp.bfloat16)
    return hidden, grad_pre, grad_lifted


def pack(pieces, rows, arrived):
    copies, at = [], 0
    for i, piece in enumerate(pieces):
        height = piece.shape[1]
        copies.append(pltpu.make_async_copy(piece, rows.at[:, pl.ds(at, height)], arrived.at[i]))
        at += height
    for copy in copies:
        copy.start()
    for copy in copies:
        copy.wait()


def height(pieces):
    return sum(piece.shape[1] for piece in pieces)


def own_kernel(n_pieces, *refs):
    pieces, refs = refs[:n_pieces], refs[n_pieces:]
    gate_weight, up_weight, down_weight, hidden, grad_pre, grad_lifted, kept, sent = refs[:8]
    rows, grad_out_t, out_sum, in_sum, arrived = refs[8:]
    step = pl.program_id(0)
    part = kept.shape[1]

    @pl.when(step == 0)
    def _():
        pack(pieces, rows, arrived)
        grad_out_t[...] = rows[1].T
        out_sum[...] = jnp.zeros_like(out_sum)
        in_sum[...] = jnp.zeros_like(in_sum)

    hidden[...], grad_pre[...], grad_lifted[...] = activations(
        *project(rows[0], grad_out_t[...], gate_weight[...], up_weight[...], down_weight[...])
    )
    grad_pre_t, grad_lifted_t = grad_pre[...].T, grad_lifted[...].T
    for at in range(0, out_sum.shape[1], CHUNK):
        here = slice(at, at + CHUNK)
        out_sum[:, here] += jnp.dot(
            hidden[...], down_weight[:, here], preferred_element_type=jnp.float32
        )
        in_sum[here] += jnp.dot(
            gate_weight[here], grad_pre_t, preferred_element_type=jnp.float32
        ) + jnp.dot(up_weight[here], grad_lifted_t, preferred_element_type=jnp.float32)

    @pl.when(step == pl.num_programs(0) - 1)
    def _():
        kept[0] = out_sum[:part].astype(kept.dtype)
        sent[0] = out_sum[part:].astype(sent.dtype)
        summed = in_sum[...].T
        kept[1] = summed[:part].astype(kept.dtype)
        sent[1] = summed[part:].astype(sent.dtype)


def own_rows(pieces, gate_weight, up_weight, down_weight):
    depth, hidden_units = gate_weight.shape
    count = height(pieces)
    tall = pl.BlockSpec((depth, TILE), lambda i: (0, i))
    wide = pl.BlockSpec((TILE, depth), lambda i: (i, 0))
    slim = pl.BlockSpec((count, TILE), lambda i: (0, i))
    whole = pl.BlockSpec((2, count // 2, depth), lambda i: (0, 0, 0))
    kept = jax.ShapeDtypeStruct((2, count // 2, depth), jnp.bfloat16)
    unit = jax.ShapeDtypeStruct((count, hidden_units), jnp.bfloat16)
    return pl.pallas_call(
        functools.partial(own_kernel, len(pieces)),
        grid=(hidden_units // TILE,),
        in_specs=[pl.BlockSpec(memory_space=pltpu.HBM)] * len(pieces) + [tall, tall, wide],
        out_specs=[slim, slim, slim, whole, whole],
        out_shape=[unit, unit, unit, kept, kept],
        scratch_shapes=[
            pltpu.VMEM((2, count, depth), jnp.bfloat16),
            pltpu.VMEM((depth, count), jnp.bfloat16),
            pltpu.VMEM((count, depth), jnp.float32),
            pltpu.VMEM((depth, count), jnp.float32),
            pltpu.SemaphoreType.DMA((len(pieces),)),
        ],
        compiler_params=pltpu.CompilerParams(vmem_limit_bytes=46 * 2**20),
        cost_estimate=pl.CostEstimate(
            flops=12 * count * depth * hidden_units,
            bytes_accessed=6 * depth * hidden_units,
            transcendentals=count * hidden_units,
        ),
        name="own_rows",
    )(*pieces, gate_weight, up_weight, down_weight)


def all_kernel(n_own, n_last, *refs):
    replica, refs = refs[0], refs[1:]
    own_pieces, refs = refs[:n_own], refs[n_own:]
    last_pieces, refs = refs[:n_last], refs[n_last:]
    own_hidden, own_grad_pre, own_grad_lifted = refs[:3]
    gate_weight, up_weight, down_weight, grad_gate, grad_up, grad_down = refs[3:9]
    rows, first, normed_t, grad_out, grad_out_t, hidden, grad_pre, grad_lifted, arrived = refs[9:]
    step, last = pl.program_id(0), pl.num_programs(0) - 1
    ahead = first.shape[1]
    width = normed_t.shape[0]

    @pl.when(step == 0)
    def _():
        columns = pl.ds(pl.multiple_of(replica[0] * width, 128), width)
        pack(last_pieces, rows, arrived)
        pack([piece.at[:, :, columns] for piece in own_pieces], first, arrived)
        grad_out_t[...] = rows[1].T
        normed_t[:, :ahead] = first[0].T
        normed_t[:, ahead:] = rows[0, :, columns].T
        grad_out[:ahead] = first[1]
        grad_out[ahead:] = rows[1, :, columns]

    def weight_gradients():
        grad_gate[...] = jnp.dot(
            normed_t[...], grad_pre[...], preferred_element_type=jnp.float32
        ).astype(grad_gate.dtype)
        grad_up[...] = jnp.dot(
            normed_t[...], grad_lifted[...], preferred_element_type=jnp.float32
        ).astype(grad_up.dtype)
        grad_down[...] = jnp.dot(
            hidden[...].T, grad_out[...], preferred_element_type=jnp.float32
        ).astype(grad_down.dtype)

    @pl.when(step < last)
    def _():
        products = project(
            rows[0], grad_out_t[...], gate_weight[...], up_weight[...], down_weight[...]
        )
        weight_gradients()
        hidden[:ahead] = own_hidden[...]
        grad_pre[:ahead] = own_grad_pre[...]
        grad_lifted[:ahead] = own_grad_lifted[...]
        hidden[ahead:], grad_pre[ahead:], grad_lifted[ahead:] = activations(*products)

    @pl.when(step == last)
    def _():
        weight_gradients()


def all_rows(replica, n_dp, own_pieces, last_pieces, units, gate_weight, up_weight, down_weight):
    depth, hidden_units = gate_weight.shape
    ahead, behind = height(own_pieces), height(last_pieces)
    count = ahead + behind
    width = depth // n_dp
    tiles = hidden_units // TILE
    tall = pl.BlockSpec((depth, TILE), lambda i: (0, jnp.minimum(i, tiles - 1)))
    wide = pl.BlockSpec((TILE, depth), lambda i: (jnp.minimum(i, tiles - 1), 0))
    slim = pl.BlockSpec((ahead, TILE), lambda i: (0, jnp.minimum(i, tiles - 1)))
    n_pieces = len(own_pieces), len(last_pieces)
    return pl.pallas_call(
        functools.partial(all_kernel, *n_pieces),
        grid=(tiles + 1,),
        in_specs=[pl.BlockSpec(memory_space=pltpu.SMEM)]
        + [pl.BlockSpec(memory_space=pltpu.HBM)] * sum(n_pieces)
        + [slim, slim, slim, tall, tall, wide],
        out_specs=[
            pl.BlockSpec((width, TILE), lambda i: (0, jnp.maximum(i - 1, 0))),
            pl.BlockSpec((width, TILE), lambda i: (0, jnp.maximum(i - 1, 0))),
            pl.BlockSpec((TILE, width), lambda i: (jnp.maximum(i - 1, 0), 0)),
        ],
        out_shape=[
            jax.ShapeDtypeStruct((width, hidden_units), jnp.bfloat16),
            jax.ShapeDtypeStruct((width, hidden_units), jnp.bfloat16),
            jax.ShapeDtypeStruct((hidden_units, width), jnp.bfloat16),
        ],
        scratch_shapes=[
            pltpu.VMEM((2, behind, depth), jnp.bfloat16),
            pltpu.VMEM((2, ahead, width), jnp.bfloat16),
            pltpu.VMEM((width, count), jnp.bfloat16),
            pltpu.VMEM((count, width), jnp.bfloat16),
            pltpu.VMEM((depth, behind), jnp.bfloat16),
            pltpu.VMEM((count, TILE), jnp.bfloat16),
            pltpu.VMEM((count, TILE), jnp.bfloat16),
            pltpu.VMEM((count, TILE), jnp.bfloat16),
            pltpu.SemaphoreType.DMA((max(n_pieces),)),
        ],
        compiler_params=pltpu.CompilerParams(vmem_limit_bytes=46 * 2**20),
        cost_estimate=pl.CostEstimate(
            flops=6 * (behind * depth + count * width) * hidden_units,
            bytes_accessed=6 * (depth + width) * hidden_units,
            transcendentals=behind * hidden_units,
        ),
        name="all_rows",
    )(replica, *own_pieces, *last_pieces, *units, gate_weight, up_weight, down_weight)


def gather_tokens(tokens, norm_scale_vector, gate_weight, up_weight, down_weight, cotangent):
    n_dp = lax.axis_size("dp")
    n_tp = lax.axis_size("tp")
    replica = lax.axis_index("dp").astype(jnp.int32).reshape(1)
    rows = tokens.shape[0]

    def swap(array, dp_bits, tp_bits):
        pairs = [
            (d * n_tp + t, (d ^ dp_bits) * n_tp + (t ^ tp_bits))
            for d in range(n_dp)
            for t in range(n_tp)
        ]
        return lax.ppermute(array, ("dp", "tp"), pairs)

    def far(pieces):
        return [swap(piece, 0, 1) for piece in pieces]

    expanded_hidden = tokens.astype(jnp.float32)
    reciprocal_root_mean = lax.rsqrt(
        jnp.mean(expanded_hidden * expanded_hidden, axis=-1, keepdims=True) + 1e-05
    )
    unit_input = expanded_hidden * reciprocal_root_mean
    rescaled_input = (unit_input * norm_scale_vector).astype(jnp.bfloat16)
    unit0 = jnp.stack([rescaled_input, cotangent])
    unit1, unit2 = swap(unit0, 0, 2), swap(unit0, 0, 4)
    more = [swap(unit0, b, 0) for b in reversed(range(1, n_dp))]
    *more, unit1, unit2 = lax.optimization_barrier((*more, unit1, unit2))
    unit3, far_unit0, far_more = swap(unit2, 0, 2), swap(unit0, 0, 1), far(more)
    far_more, far_unit0, unit3 = lax.optimization_barrier((far_more, far_unit0, unit3))
    late = jnp.concatenate([unit1, unit2, unit3], axis=1)
    own = [unit0, late, far_unit0, swap(late, 0, 1)]
    more += far_more
    own, more = lax.optimization_barrier((own, more))
    rest = [swap(late, b, 0) for b in range(1, n_dp)]
    *units, kept, sent = own_rows(own, gate_weight, up_weight, down_weight)
    kept, sent, rest = lax.optimization_barrier((kept, sent, rest))
    rest += far(rest) + more

    pair = (kept.astype(jnp.float32) + swap(sent, 0, 1).astype(jnp.float32)).astype(jnp.bfloat16)
    parts = [swap(pair[:, k * rows : (k + 1) * rows], 0, 2 * k) for k in range(1, n_tp // 2)]
    weight_gradients = all_rows(
        replica, n_dp, own, rest, units, gate_weight, up_weight, down_weight
    )
    parts, weight_gradients = lax.optimization_barrier((parts, weight_gradients))
    total = pair[:, :rows].astype(jnp.float32) + sum(part.astype(jnp.float32) for part in parts)
    branch, grad_normed = total[0], total[1]
    mixed = (expanded_hidden + branch).astype(jnp.bfloat16)
    gain_applied = grad_normed * norm_scale_vector
    inner_product = jnp.mean(gain_applied * unit_input, axis=-1, keepdims=True)
    token_gradient = (
        cotangent.astype(jnp.float32)
        + reciprocal_root_mean * (gain_applied - unit_input * inner_product)
    ).astype(jnp.bfloat16)
    return mixed, token_gradient, *weight_gradients


def sum_weight_gradients(tokens, norm_scale_vector, gate_weight, up_weight, down_weight, cotangent):
    expanded_hidden = tokens.astype(jnp.float32)
    reciprocal_root_mean = lax.rsqrt(
        jnp.mean(expanded_hidden * expanded_hidden, axis=-1, keepdims=True) + 1e-05
    )
    unit_input = expanded_hidden * reciprocal_root_mean
    rescaled_input = (unit_input * norm_scale_vector).astype(jnp.bfloat16)
    normed_all = lax.all_gather(rescaled_input, "tp", axis=0, tiled=True)
    gate = jnp.dot(normed_all, gate_weight, preferred_element_type=jnp.float32)
    lifted = jnp.dot(normed_all, up_weight, preferred_element_type=jnp.float32)
    sigmoid_gate = jax.nn.sigmoid(gate)
    activated = gate * sigmoid_gate
    hidden = (activated * lifted).astype(jnp.bfloat16)
    branch = lax.psum_scatter(
        jnp.dot(hidden, down_weight, preferred_element_type=jnp.float32).astype(jnp.bfloat16),
        "tp",
        scatter_dimension=0,
        tiled=True,
    ).astype(jnp.float32)
    mixed = (expanded_hidden + branch).astype(jnp.bfloat16)
    grad_all = lax.all_gather(cotangent, "tp", axis=0, tiled=True)
    grad_hidden = contract_cols(grad_all, down_weight)
    grad_pre = (grad_hidden * lifted * sigmoid_gate * (1.0 + gate * (1.0 - sigmoid_gate))).astype(
        jnp.bfloat16
    )
    grad_lifted = (grad_hidden * activated).astype(jnp.bfloat16)
    grad_normed = lax.psum_scatter(
        (contract_cols(grad_pre, gate_weight) + contract_cols(grad_lifted, up_weight)).astype(
            jnp.bfloat16
        ),
        "tp",
        scatter_dimension=0,
        tiled=True,
    ).astype(jnp.float32)
    gain_applied = grad_normed * norm_scale_vector
    inner_product = jnp.mean(gain_applied * unit_input, axis=-1, keepdims=True)
    token_gradient = (
        cotangent.astype(jnp.float32)
        + reciprocal_root_mean * (gain_applied - unit_input * inner_product)
    ).astype(jnp.bfloat16)
    weight_gate = contract_rows(normed_all, grad_pre).astype(jnp.bfloat16)
    weight_up = contract_rows(normed_all, grad_lifted).astype(jnp.bfloat16)
    weight_down = contract_rows(hidden, grad_all).astype(jnp.bfloat16)
    sum_gate, sum_up, sum_down = (
        lax.psum_scatter(weight_gate, "dp", scatter_dimension=0, tiled=True).astype(jnp.float32),
        lax.psum_scatter(weight_up, "dp", scatter_dimension=0, tiled=True).astype(jnp.float32),
        lax.psum_scatter(weight_down, "dp", scatter_dimension=1, tiled=True).astype(jnp.float32),
    )
    return (
        mixed,
        token_gradient,
        sum_gate.astype(jnp.bfloat16),
        sum_up.astype(jnp.bfloat16),
        sum_down.astype(jnp.bfloat16),
    )


def solution(mesh):
    n_dp, n_tp = mesh.shape["dp"], mesh.shape["tp"]
    in_specs = (
        P(("dp", "tp"), None),
        P(),
        P(None, "tp"),
        P(None, "tp"),
        P("tp", None),
        P(("dp", "tp"), None),
    )
    out_specs = (
        P(("dp", "tp"), None),
        P(("dp", "tp"), None),
        P("dp", "tp"),
        P("dp", "tp"),
        P("tp", "dp"),
    )

    def run(tokens, norm_scale_vector, gate_weight, up_weight, down_weight, cotangent):
        gathered = tokens.size + cotangent.size
        weights = (gate_weight.size + up_weight.size + down_weight.size) // n_tp
        local = sum_weight_gradients
        if (n_dp, n_tp) == (4, 8) and gathered <= weights:
            local = gather_tokens
        return jax.shard_map(
            local, mesh=mesh, in_specs=in_specs, out_specs=out_specs, check_vma=False
        )(tokens, norm_scale_vector, gate_weight, up_weight, down_weight, cotangent)

    return run
```

```python
import functools

import jax
import jax.numpy as jnp
from jax import lax
from jax.experimental import pallas as pl
from jax.experimental.pallas import tpu as pltpu
from jax.sharding import PartitionSpec as P


def contract_rows(left, right):
    return lax.dot_general(
        left, right, (((0,), (0,)), ((), ())), preferred_element_type=jnp.float32
    )


def contract_cols(left, right):
    return lax.dot_general(
        left, right, (((1,), (1,)), ((), ())), preferred_element_type=jnp.float32
    )


TILE = 256
CHUNK = 1024


def project(normed, grad_out_t, gate_weight, up_weight, down_weight):
    gate = jnp.dot(normed, gate_weight, preferred_element_type=jnp.float32)
    lifted = jnp.dot(normed, up_weight, preferred_element_type=jnp.float32)
    grad_hidden = jnp.dot(down_weight, grad_out_t, preferred_element_type=jnp.float32).T
    return gate, lifted, grad_hidden


def activations(gate, lifted, grad_hidden):
    sigmoid_gate = jax.nn.sigmoid(gate)
    activated = gate * sigmoid_gate
    hidden = (activated * lifted).astype(jnp.bfloat16)
    grad_pre = (grad_hidden * lifted * sigmoid_gate * (1.0 + gate * (1.0 - sigmoid_gate))).astype(
        jnp.bfloat16
    )
    grad_lifted = (grad_hidden * activated).astype(jnp.bfloat16)
    return hidden, grad_pre, grad_lifted


def pack(pieces, rows, arrived):
    copies, at = [], 0
    for i, piece in enumerate(pieces):
        height = piece.shape[1]
        copies.append(pltpu.make_async_copy(piece, rows.at[:, pl.ds(at, height)], arrived.at[i]))
        at += height
    for copy in copies:
        copy.start()
    for copy in copies:
        copy.wait()


def in_hbm(*arrays):
    return [pltpu.with_memory_space_constraint(array, pltpu.HBM) for array in arrays]


def height(pieces):
    return sum(piece.shape[1] for piece in pieces)


def own_kernel(n_pieces, *refs):
    pieces, refs = refs[:n_pieces], refs[n_pieces:]
    gate_weight, up_weight, down_weight, hidden, grad_pre, grad_lifted, kept, sent = refs[:8]
    rows, grad_out_t, out_sum, in_sum, arrived = refs[8:]
    step = pl.program_id(0)
    part = kept.shape[1]

    @pl.when(step == 0)
    def _():
        pack(pieces, rows, arrived)
        grad_out_t[...] = rows[1].T
        out_sum[...] = jnp.zeros_like(out_sum)
        in_sum[...] = jnp.zeros_like(in_sum)

    hidden[...], grad_pre[...], grad_lifted[...] = activations(
        *project(rows[0], grad_out_t[...], gate_weight[...], up_weight[...], down_weight[...])
    )
    grad_pre_t, grad_lifted_t = grad_pre[...].T, grad_lifted[...].T
    for at in range(0, out_sum.shape[1], CHUNK):
        here = slice(at, at + CHUNK)
        out_sum[:, here] += jnp.dot(
            hidden[...], down_weight[:, here], preferred_element_type=jnp.float32
        )
        in_sum[here] += jnp.dot(
            gate_weight[here], grad_pre_t, preferred_element_type=jnp.float32
        ) + jnp.dot(up_weight[here], grad_lifted_t, preferred_element_type=jnp.float32)

    @pl.when(step == pl.num_programs(0) - 1)
    def _():
        kept[0] = out_sum[:part].astype(kept.dtype)
        sent[0] = out_sum[part:].astype(sent.dtype)
        summed = in_sum[...].T
        kept[1] = summed[:part].astype(kept.dtype)
        sent[1] = summed[part:].astype(sent.dtype)


def own_rows(pieces, gate_weight, up_weight, down_weight):
    depth, hidden_units = gate_weight.shape
    count = height(pieces)
    tall = pl.BlockSpec((depth, TILE), lambda i: (0, i))
    wide = pl.BlockSpec((TILE, depth), lambda i: (i, 0))
    slim = pl.BlockSpec((count, TILE), lambda i: (0, i))
    whole = pl.BlockSpec((2, count // 2, depth), lambda i: (0, 0, 0))
    kept = jax.ShapeDtypeStruct((2, count // 2, depth), jnp.bfloat16)
    unit = jax.ShapeDtypeStruct((count, hidden_units), jnp.bfloat16)
    return pl.pallas_call(
        functools.partial(own_kernel, len(pieces)),
        grid=(hidden_units // TILE,),
        in_specs=[pl.BlockSpec(memory_space=pl.ANY)] * len(pieces) + [tall, tall, wide],
        out_specs=[slim, slim, slim, whole, whole],
        out_shape=[unit, unit, unit, kept, kept],
        scratch_shapes=[
            pltpu.VMEM((2, count, depth), jnp.bfloat16),
            pltpu.VMEM((depth, count), jnp.bfloat16),
            pltpu.VMEM((count, depth), jnp.float32),
            pltpu.VMEM((depth, count), jnp.float32),
            pltpu.SemaphoreType.DMA((len(pieces),)),
        ],
        compiler_params=pltpu.CompilerParams(vmem_limit_bytes=28 * 2**20),
        cost_estimate=pl.CostEstimate(
            flops=12 * count * depth * hidden_units,
            bytes_accessed=6 * depth * hidden_units,
            transcendentals=count * hidden_units,
        ),
        name="own_rows",
    )(*pieces, *in_hbm(gate_weight, up_weight, down_weight))


def all_kernel(n_own, n_last, *refs):
    replica, refs = refs[0], refs[1:]
    own_pieces, refs = refs[:n_own], refs[n_own:]
    last_pieces, refs = refs[:n_last], refs[n_last:]
    own_hidden, own_grad_pre, own_grad_lifted = refs[:3]
    gate_weight, up_weight, down_weight, grad_gate, grad_up, grad_down = refs[3:9]
    rows, first, normed_t, grad_out, grad_out_t, hidden, grad_pre, grad_lifted, arrived = refs[9:]
    step, last = pl.program_id(0), pl.num_programs(0) - 1
    ahead = first.shape[1]
    width = normed_t.shape[0]

    @pl.when(step == 0)
    def _():
        columns = pl.ds(pl.multiple_of(replica[0] * width, 128), width)
        pack(last_pieces, rows, arrived)
        pack([piece.at[:, :, columns] for piece in own_pieces], first, arrived)
        grad_out_t[...] = rows[1].T
        normed_t[:, :ahead] = first[0].T
        normed_t[:, ahead:] = rows[0, :, columns].T
        grad_out[:ahead] = first[1]
        grad_out[ahead:] = rows[1, :, columns]

    def weight_gradients():
        grad_gate[...] = jnp.dot(
            normed_t[...], grad_pre[...], preferred_element_type=jnp.float32
        ).astype(grad_gate.dtype)
        grad_up[...] = jnp.dot(
            normed_t[...], grad_lifted[...], preferred_element_type=jnp.float32
        ).astype(grad_up.dtype)
        grad_down[...] = jnp.dot(
            hidden[...].T, grad_out[...], preferred_element_type=jnp.float32
        ).astype(grad_down.dtype)

    @pl.when(step < last)
    def _():
        products = project(
            rows[0], grad_out_t[...], gate_weight[...], up_weight[...], down_weight[...]
        )
        weight_gradients()
        hidden[:ahead] = own_hidden[...]
        grad_pre[:ahead] = own_grad_pre[...]
        grad_lifted[:ahead] = own_grad_lifted[...]
        hidden[ahead:], grad_pre[ahead:], grad_lifted[ahead:] = activations(*products)

    @pl.when(step == last)
    def _():
        weight_gradients()


def all_rows(replica, n_dp, own_pieces, last_pieces, units, gate_weight, up_weight, down_weight):
    depth, hidden_units = gate_weight.shape
    ahead, behind = height(own_pieces), height(last_pieces)
    count = ahead + behind
    width = depth // n_dp
    tiles = hidden_units // TILE
    tall = pl.BlockSpec((depth, TILE), lambda i: (0, jnp.minimum(i, tiles - 1)))
    wide = pl.BlockSpec((TILE, depth), lambda i: (jnp.minimum(i, tiles - 1), 0))
    slim = pl.BlockSpec((ahead, TILE), lambda i: (0, jnp.minimum(i, tiles - 1)))
    n_pieces = len(own_pieces), len(last_pieces)
    return pl.pallas_call(
        functools.partial(all_kernel, *n_pieces),
        grid=(tiles + 1,),
        in_specs=[pl.BlockSpec(memory_space=pltpu.SMEM)]
        + [pl.BlockSpec(memory_space=pl.ANY)] * sum(n_pieces)
        + [slim, slim, slim, tall, tall, wide],
        out_specs=[
            pl.BlockSpec((width, TILE), lambda i: (0, jnp.maximum(i - 1, 0))),
            pl.BlockSpec((width, TILE), lambda i: (0, jnp.maximum(i - 1, 0))),
            pl.BlockSpec((TILE, width), lambda i: (jnp.maximum(i - 1, 0), 0)),
        ],
        out_shape=[
            jax.ShapeDtypeStruct((width, hidden_units), jnp.bfloat16),
            jax.ShapeDtypeStruct((width, hidden_units), jnp.bfloat16),
            jax.ShapeDtypeStruct((hidden_units, width), jnp.bfloat16),
        ],
        scratch_shapes=[
            pltpu.VMEM((2, behind, depth), jnp.bfloat16),
            pltpu.VMEM((2, ahead, width), jnp.bfloat16),
            pltpu.VMEM((width, count), jnp.bfloat16),
            pltpu.VMEM((count, width), jnp.bfloat16),
            pltpu.VMEM((depth, behind), jnp.bfloat16),
            pltpu.VMEM((count, TILE), jnp.bfloat16),
            pltpu.VMEM((count, TILE), jnp.bfloat16),
            pltpu.VMEM((count, TILE), jnp.bfloat16),
            pltpu.SemaphoreType.DMA((max(n_pieces),)),
        ],
        compiler_params=pltpu.CompilerParams(vmem_limit_bytes=32 * 2**20),
        cost_estimate=pl.CostEstimate(
            flops=6 * (behind * depth + count * width) * hidden_units,
            bytes_accessed=6 * (depth + width) * hidden_units,
            transcendentals=behind * hidden_units,
        ),
        name="all_rows",
    )(replica, *own_pieces, *last_pieces, *units, *in_hbm(gate_weight, up_weight, down_weight))


def gather_tokens(tokens, norm_scale_vector, gate_weight, up_weight, down_weight, cotangent):
    n_dp = lax.axis_size("dp")
    n_tp = lax.axis_size("tp")
    replica = lax.axis_index("dp").astype(jnp.int32).reshape(1)
    rows = tokens.shape[0]

    def swap(array, dp_bits, tp_bits):
        pairs = [
            (d * n_tp + t, (d ^ dp_bits) * n_tp + (t ^ tp_bits))
            for d in range(n_dp)
            for t in range(n_tp)
        ]
        return lax.ppermute(array, ("dp", "tp"), pairs)

    def far(pieces):
        return [swap(piece, 0, 1) for piece in pieces]

    expanded_hidden = tokens.astype(jnp.float32)
    reciprocal_root_mean = lax.rsqrt(
        jnp.mean(expanded_hidden * expanded_hidden, axis=-1, keepdims=True) + 1e-05
    )
    unit_input = expanded_hidden * reciprocal_root_mean
    rescaled_input = (unit_input * norm_scale_vector).astype(jnp.bfloat16)
    unit0 = jnp.stack([rescaled_input, cotangent])
    unit1, unit2 = swap(unit0, 0, 2), swap(unit0, 0, 4)
    across0 = [swap(unit0, b, 0) for b in range(1, n_dp)]
    unit3 = swap(unit2, 0, 2)
    across0, unit1 = lax.optimization_barrier((across0, unit1))
    across1 = [swap(unit1, 1, 0), swap(unit1, 2, 0)]
    far_units, far_across0 = far([unit0, unit1]), far(across0)
    far_across0, far_units, across1, unit3 = lax.optimization_barrier(
        (far_across0, far_units, across1, unit3)
    )
    last = jnp.concatenate([unit2, unit3], axis=1)
    own = [unit0, unit1, last] + far_units + [swap(last, 0, 1)]
    more = across0 + far_across0 + across1
    own, more = lax.optimization_barrier((own, more))
    rest = [swap(unit1, 3, 0)] + [swap(last, b, 0) for b in range(1, n_dp)]
    *units, kept, sent = own_rows(own, gate_weight, up_weight, down_weight)
    kept, sent, rest = lax.optimization_barrier((kept, sent, rest))
    pair = (kept.astype(jnp.float32) + swap(sent, 0, 1).astype(jnp.float32)).astype(jnp.bfloat16)
    rest += more + far(across1 + rest)
    parts = [swap(pair[:, k * rows : (k + 1) * rows], 0, 2 * k) for k in range(1, n_tp // 2)]
    weight_gradients = all_rows(
        replica, n_dp, own, rest, units, gate_weight, up_weight, down_weight
    )
    parts, weight_gradients = lax.optimization_barrier((parts, weight_gradients))
    total = pair[:, :rows].astype(jnp.float32) + sum(part.astype(jnp.float32) for part in parts)
    branch, grad_normed = total[0], total[1]
    mixed = (expanded_hidden + branch).astype(jnp.bfloat16)
    gain_applied = grad_normed * norm_scale_vector
    inner_product = jnp.mean(gain_applied * unit_input, axis=-1, keepdims=True)
    token_gradient = (
        cotangent.astype(jnp.float32)
        + reciprocal_root_mean * (gain_applied - unit_input * inner_product)
    ).astype(jnp.bfloat16)
    return mixed, token_gradient, *weight_gradients


def sum_weight_gradients(tokens, norm_scale_vector, gate_weight, up_weight, down_weight, cotangent):
    expanded_hidden = tokens.astype(jnp.float32)
    reciprocal_root_mean = lax.rsqrt(
        jnp.mean(expanded_hidden * expanded_hidden, axis=-1, keepdims=True) + 1e-05
    )
    unit_input = expanded_hidden * reciprocal_root_mean
    rescaled_input = (unit_input * norm_scale_vector).astype(jnp.bfloat16)
    normed_all = lax.all_gather(rescaled_input, "tp", axis=0, tiled=True)
    gate = jnp.dot(normed_all, gate_weight, preferred_element_type=jnp.float32)
    lifted = jnp.dot(normed_all, up_weight, preferred_element_type=jnp.float32)
    sigmoid_gate = jax.nn.sigmoid(gate)
    activated = gate * sigmoid_gate
    hidden = (activated * lifted).astype(jnp.bfloat16)
    branch = lax.psum_scatter(
        jnp.dot(hidden, down_weight, preferred_element_type=jnp.float32).astype(jnp.bfloat16),
        "tp",
        scatter_dimension=0,
        tiled=True,
    ).astype(jnp.float32)
    mixed = (expanded_hidden + branch).astype(jnp.bfloat16)
    grad_all = lax.all_gather(cotangent, "tp", axis=0, tiled=True)
    grad_hidden = contract_cols(grad_all, down_weight)
    grad_pre = (grad_hidden * lifted * sigmoid_gate * (1.0 + gate * (1.0 - sigmoid_gate))).astype(
        jnp.bfloat16
    )
    grad_lifted = (grad_hidden * activated).astype(jnp.bfloat16)
    grad_normed = lax.psum_scatter(
        (contract_cols(grad_pre, gate_weight) + contract_cols(grad_lifted, up_weight)).astype(
            jnp.bfloat16
        ),
        "tp",
        scatter_dimension=0,
        tiled=True,
    ).astype(jnp.float32)
    gain_applied = grad_normed * norm_scale_vector
    inner_product = jnp.mean(gain_applied * unit_input, axis=-1, keepdims=True)
    token_gradient = (
        cotangent.astype(jnp.float32)
        + reciprocal_root_mean * (gain_applied - unit_input * inner_product)
    ).astype(jnp.bfloat16)
    weight_gate = contract_rows(normed_all, grad_pre).astype(jnp.bfloat16)
    weight_up = contract_rows(normed_all, grad_lifted).astype(jnp.bfloat16)
    weight_down = contract_rows(hidden, grad_all).astype(jnp.bfloat16)
    sum_gate, sum_up, sum_down = (
        lax.psum_scatter(weight_gate, "dp", scatter_dimension=0, tiled=True).astype(jnp.float32),
        lax.psum_scatter(weight_up, "dp", scatter_dimension=0, tiled=True).astype(jnp.float32),
        lax.psum_scatter(weight_down, "dp", scatter_dimension=1, tiled=True).astype(jnp.float32),
    )
    return (
        mixed,
        token_gradient,
        sum_gate.astype(jnp.bfloat16),
        sum_up.astype(jnp.bfloat16),
        sum_down.astype(jnp.bfloat16),
    )


def solution(mesh):
    n_dp, n_tp = mesh.shape["dp"], mesh.shape["tp"]
    in_specs = (
        P(("dp", "tp"), None),
        P(),
        P(None, "tp"),
        P(None, "tp"),
        P("tp", None),
        P(("dp", "tp"), None),
    )
    out_specs = (
        P(("dp", "tp"), None),
        P(("dp", "tp"), None),
        P("dp", "tp"),
        P("dp", "tp"),
        P("tp", "dp"),
    )

    def run(tokens, norm_scale_vector, gate_weight, up_weight, down_weight, cotangent):
        gathered = tokens.size + cotangent.size
        weights = (gate_weight.size + up_weight.size + down_weight.size) // n_tp
        local = sum_weight_gradients
        if (n_dp, n_tp) == (4, 8) and gathered <= weights:
            local = gather_tokens
        return jax.shard_map(
            local, mesh=mesh, in_specs=in_specs, out_specs=out_specs, check_vma=False
        )(tokens, norm_scale_vector, gate_weight, up_weight, down_weight, cotangent)

    return run
```

```python
import functools

import jax
import jax.numpy as jnp
from jax import lax
from jax.experimental import pallas as pl
from jax.experimental.pallas import tpu as pltpu
from jax.sharding import PartitionSpec as P


def contract_rows(left, right):
    return lax.dot_general(
        left, right, (((0,), (0,)), ((), ())), preferred_element_type=jnp.float32
    )


def contract_cols(left, right):
    return lax.dot_general(
        left, right, (((1,), (1,)), ((), ())), preferred_element_type=jnp.float32
    )


TILE = 256
CHUNK = 1024


def project(normed, grad_out_t, gate_weight, up_weight, down_weight):
    gate = jnp.dot(normed, gate_weight, preferred_element_type=jnp.float32)
    lifted = jnp.dot(normed, up_weight, preferred_element_type=jnp.float32)
    grad_hidden = jnp.dot(down_weight, grad_out_t, preferred_element_type=jnp.float32).T
    return gate, lifted, grad_hidden


def activations(gate, lifted, grad_hidden):
    sigmoid_gate = jax.nn.sigmoid(gate)
    activated = gate * sigmoid_gate
    hidden = (activated * lifted).astype(jnp.bfloat16)
    grad_pre = (grad_hidden * lifted * sigmoid_gate * (1.0 + gate * (1.0 - sigmoid_gate))).astype(
        jnp.bfloat16
    )
    grad_lifted = (grad_hidden * activated).astype(jnp.bfloat16)
    return hidden, grad_pre, grad_lifted


def pack(pieces, rows, arrived):
    copies, at = [], 0
    for i, piece in enumerate(pieces):
        height = piece.shape[1]
        copies.append(pltpu.make_async_copy(piece, rows.at[:, pl.ds(at, height)], arrived.at[i]))
        at += height
    for copy in copies:
        copy.start()
    for copy in copies:
        copy.wait()


def in_hbm(*arrays):
    return [pltpu.with_memory_space_constraint(array, pltpu.HBM) for array in arrays]


def height(pieces):
    return sum(piece.shape[1] for piece in pieces)


def norm_kernel(tokens, norm_scale_vector, cotangent, unit):
    expanded_hidden = tokens[...].astype(jnp.float32)
    reciprocal_root_mean = lax.rsqrt(
        jnp.mean(expanded_hidden * expanded_hidden, axis=-1, keepdims=True) + 1e-05
    )
    rescaled_input = expanded_hidden * reciprocal_root_mean * norm_scale_vector[...]
    unit[0] = rescaled_input.astype(unit.dtype)
    unit[1] = cotangent[...]


def normalize(tokens, norm_scale_vector, cotangent):
    return pl.pallas_call(
        norm_kernel,
        out_shape=jax.ShapeDtypeStruct((2, *tokens.shape), jnp.bfloat16),
        name="normalize",
    )(*in_hbm(tokens, norm_scale_vector.reshape(1, -1), cotangent))


def own_kernel(n_pieces, *refs):
    replica, pieces, refs = refs[0], refs[1 : n_pieces + 1], refs[n_pieces + 1 :]
    gate_weight, up_weight, down_weight, hidden, grad_pre, grad_lifted = refs[:6]
    columns, kept, sent, rows, grad_out_t, out_sum, in_sum, arrived = refs[6:]
    step = pl.program_id(0)
    part = kept.shape[1]

    @pl.when(step == 0)
    def _():
        pack(pieces, rows, arrived)
        width = columns.shape[2]
        columns[...] = rows[:, :, pl.ds(pl.multiple_of(replica[0] * width, 128), width)]
        grad_out_t[...] = rows[1].T
        out_sum[...] = jnp.zeros_like(out_sum)
        in_sum[...] = jnp.zeros_like(in_sum)

    hidden[...], grad_pre[...], grad_lifted[...] = activations(
        *project(rows[0], grad_out_t[...], gate_weight[...], up_weight[...], down_weight[...])
    )
    grad_pre_t, grad_lifted_t = grad_pre[...].T, grad_lifted[...].T
    for at in range(0, out_sum.shape[1], CHUNK):
        here = slice(at, at + CHUNK)
        out_sum[:, here] += jnp.dot(
            hidden[...], down_weight[:, here], preferred_element_type=jnp.float32
        )
        in_sum[here] += jnp.dot(
            gate_weight[here], grad_pre_t, preferred_element_type=jnp.float32
        ) + jnp.dot(up_weight[here], grad_lifted_t, preferred_element_type=jnp.float32)

    @pl.when(step == pl.num_programs(0) - 1)
    def _():
        kept[0] = out_sum[:part].astype(kept.dtype)
        sent[0] = out_sum[part:].astype(sent.dtype)
        summed = in_sum[...].T
        kept[1] = summed[:part].astype(kept.dtype)
        sent[1] = summed[part:].astype(sent.dtype)


def own_rows(replica, n_dp, pieces, gate_weight, up_weight, down_weight):
    depth, hidden_units = gate_weight.shape
    count = height(pieces)
    tall = pl.BlockSpec((depth, TILE), lambda i: (0, i))
    wide = pl.BlockSpec((TILE, depth), lambda i: (i, 0))
    slim = pl.BlockSpec((count, TILE), lambda i: (0, i))
    whole = pl.BlockSpec((2, count // 2, depth), lambda i: (0, 0, 0))
    kept = jax.ShapeDtypeStruct((2, count // 2, depth), jnp.bfloat16)
    columns = (2, count, depth // n_dp)
    unit = pltpu.HBM((count, hidden_units), jnp.bfloat16)
    return pl.pallas_call(
        functools.partial(own_kernel, len(pieces)),
        grid=(hidden_units // TILE,),
        in_specs=[pl.BlockSpec(memory_space=pltpu.SMEM)]
        + [pl.BlockSpec(memory_space=pl.ANY)] * len(pieces)
        + [tall, tall, wide],
        out_specs=[slim, slim, slim, pl.BlockSpec(columns, lambda i: (0, 0, 0)), whole, whole],
        out_shape=[unit, unit, unit, pltpu.HBM(columns, jnp.bfloat16), kept, kept],
        scratch_shapes=[
            pltpu.VMEM((2, count, depth), jnp.bfloat16),
            pltpu.VMEM((depth, count), jnp.bfloat16),
            pltpu.VMEM((count, depth), jnp.float32),
            pltpu.VMEM((depth, count), jnp.float32),
            pltpu.SemaphoreType.DMA((len(pieces),)),
        ],
        compiler_params=pltpu.CompilerParams(vmem_limit_bytes=28 * 2**20),
        cost_estimate=pl.CostEstimate(
            flops=12 * count * depth * hidden_units,
            bytes_accessed=6 * depth * hidden_units,
            transcendentals=count * hidden_units,
        ),
        name="own_rows",
    )(replica, *pieces, *in_hbm(gate_weight, up_weight, down_weight))


def all_kernel(n_pieces, *refs):
    replica, pieces, refs = refs[0], refs[1 : n_pieces + 1], refs[n_pieces + 1 :]
    own_hidden, own_grad_pre, own_grad_lifted, own_columns = refs[:4]
    gate_weight, up_weight, down_weight, grad_gate, grad_up, grad_down = refs[4:10]
    rows, normed_t, grad_out, grad_out_t, hidden, grad_pre, grad_lifted, arrived = refs[10:]
    step, last = pl.program_id(0), pl.num_programs(0) - 1
    ahead = own_columns.shape[1]
    width = normed_t.shape[0]

    @pl.when(step == 0)
    def _():
        columns = pl.ds(pl.multiple_of(replica[0] * width, 128), width)
        pack(pieces, rows, arrived)
        grad_out_t[...] = rows[1].T
        normed_t[:, :ahead] = own_columns[0].T
        normed_t[:, ahead:] = rows[0, :, columns].T
        grad_out[:ahead] = own_columns[1]
        grad_out[ahead:] = rows[1, :, columns]

    def weight_gradients():
        grad_gate[...] = jnp.dot(
            normed_t[...], grad_pre[...], preferred_element_type=jnp.float32
        ).astype(grad_gate.dtype)
        grad_up[...] = jnp.dot(
            normed_t[...], grad_lifted[...], preferred_element_type=jnp.float32
        ).astype(grad_up.dtype)
        grad_down[...] = jnp.dot(
            hidden[...].T, grad_out[...], preferred_element_type=jnp.float32
        ).astype(grad_down.dtype)

    @pl.when(step < last)
    def _():
        products = project(
            rows[0], grad_out_t[...], gate_weight[...], up_weight[...], down_weight[...]
        )
        weight_gradients()
        hidden[:ahead] = own_hidden[...]
        grad_pre[:ahead] = own_grad_pre[...]
        grad_lifted[:ahead] = own_grad_lifted[...]
        hidden[ahead:], grad_pre[ahead:], grad_lifted[ahead:] = activations(*products)

    @pl.when(step == last)
    def _():
        weight_gradients()


def all_rows(replica, pieces, units, own_columns, gate_weight, up_weight, down_weight):
    depth, hidden_units = gate_weight.shape
    ahead, width = own_columns.shape[1:]
    behind = height(pieces)
    count = ahead + behind
    tiles = hidden_units // TILE
    tall = pl.BlockSpec((depth, TILE), lambda i: (0, jnp.minimum(i, tiles - 1)))
    wide = pl.BlockSpec((TILE, depth), lambda i: (jnp.minimum(i, tiles - 1), 0))
    slim = pl.BlockSpec((ahead, TILE), lambda i: (0, jnp.minimum(i, tiles - 1)))
    return pl.pallas_call(
        functools.partial(all_kernel, len(pieces)),
        grid=(tiles + 1,),
        in_specs=[pl.BlockSpec(memory_space=pltpu.SMEM)]
        + [pl.BlockSpec(memory_space=pl.ANY)] * len(pieces)
        + [slim, slim, slim, pl.BlockSpec(own_columns.shape, lambda i: (0, 0, 0))]
        + [tall, tall, wide],
        out_specs=[
            pl.BlockSpec((width, TILE), lambda i: (0, jnp.maximum(i - 1, 0))),
            pl.BlockSpec((width, TILE), lambda i: (0, jnp.maximum(i - 1, 0))),
            pl.BlockSpec((TILE, width), lambda i: (jnp.maximum(i - 1, 0), 0)),
        ],
        out_shape=[
            jax.ShapeDtypeStruct((width, hidden_units), jnp.bfloat16),
            jax.ShapeDtypeStruct((width, hidden_units), jnp.bfloat16),
            jax.ShapeDtypeStruct((hidden_units, width), jnp.bfloat16),
        ],
        scratch_shapes=[
            pltpu.VMEM((2, behind, depth), jnp.bfloat16),
            pltpu.VMEM((width, count), jnp.bfloat16),
            pltpu.VMEM((count, width), jnp.bfloat16),
            pltpu.VMEM((depth, behind), jnp.bfloat16),
            pltpu.VMEM((count, TILE), jnp.bfloat16),
            pltpu.VMEM((count, TILE), jnp.bfloat16),
            pltpu.VMEM((count, TILE), jnp.bfloat16),
            pltpu.SemaphoreType.DMA((len(pieces),)),
        ],
        compiler_params=pltpu.CompilerParams(vmem_limit_bytes=32 * 2**20),
        cost_estimate=pl.CostEstimate(
            flops=6 * (behind * depth + count * width) * hidden_units,
            bytes_accessed=6 * (depth + width) * hidden_units,
            transcendentals=behind * hidden_units,
        ),
        name="all_rows",
    )(replica, *in_hbm(*pieces, *units, own_columns, gate_weight, up_weight, down_weight))


def gather_tokens(tokens, norm_scale_vector, gate_weight, up_weight, down_weight, cotangent):
    n_dp = lax.axis_size("dp")
    n_tp = lax.axis_size("tp")
    replica = lax.axis_index("dp").astype(jnp.int32).reshape(1)
    rows = tokens.shape[0]

    def swap(array, dp_bits, tp_bits):
        pairs = [
            (d * n_tp + t, (d ^ dp_bits) * n_tp + (t ^ tp_bits))
            for d in range(n_dp)
            for t in range(n_tp)
        ]
        return lax.ppermute(array, ("dp", "tp"), pairs)

    def far(pieces):
        return [swap(piece, 0, 1) for piece in pieces]

    expanded_hidden = tokens.astype(jnp.float32)
    reciprocal_root_mean = lax.rsqrt(
        jnp.mean(expanded_hidden * expanded_hidden, axis=-1, keepdims=True) + 1e-05
    )
    unit_input = expanded_hidden * reciprocal_root_mean
    unit0 = normalize(tokens, norm_scale_vector, cotangent)
    unit2, unit1 = swap(unit0, 0, 4), swap(unit0, 0, 2)
    across = [swap(unit0, b, 0) for b in range(1, n_dp)]
    unit3 = swap(unit2, 0, 2)
    far_units, far_across = far([unit0, unit1]), far(across)
    across, far_units, unit3 = lax.optimization_barrier((across, far_units, unit3))
    last = jnp.concatenate([unit2, unit3], axis=1)
    late = jnp.concatenate([unit1, unit2, unit3], axis=1)
    own = [unit0, unit1, last] + far_units + [swap(last, 0, 1)]
    rest = [swap(late, b, 0) for b in range(1, n_dp)]
    *units, own_columns, kept, sent = own_rows(
        replica, n_dp, own, gate_weight, up_weight, down_weight
    )
    kept, sent, rest = lax.optimization_barrier((kept, sent, rest))
    pair = (kept.astype(jnp.float32) + swap(sent, 0, 1).astype(jnp.float32)).astype(jnp.bfloat16)
    rest += far(rest) + across + far_across
    parts = [swap(pair[:, k * rows : (k + 1) * rows], 0, 2 * k) for k in range(1, n_tp // 2)]
    weight_gradients = all_rows(
        replica, rest, units, own_columns, gate_weight, up_weight, down_weight
    )
    parts, weight_gradients = lax.optimization_barrier((parts, weight_gradients))
    total = pair[:, :rows].astype(jnp.float32) + sum(part.astype(jnp.float32) for part in parts)
    branch, grad_normed = total[0], total[1]
    mixed = (expanded_hidden + branch).astype(jnp.bfloat16)
    gain_applied = grad_normed * norm_scale_vector
    inner_product = jnp.mean(gain_applied * unit_input, axis=-1, keepdims=True)
    token_gradient = (
        cotangent.astype(jnp.float32)
        + reciprocal_root_mean * (gain_applied - unit_input * inner_product)
    ).astype(jnp.bfloat16)
    return mixed, token_gradient, *weight_gradients


def sum_weight_gradients(tokens, norm_scale_vector, gate_weight, up_weight, down_weight, cotangent):
    expanded_hidden = tokens.astype(jnp.float32)
    reciprocal_root_mean = lax.rsqrt(
        jnp.mean(expanded_hidden * expanded_hidden, axis=-1, keepdims=True) + 1e-05
    )
    unit_input = expanded_hidden * reciprocal_root_mean
    rescaled_input = (unit_input * norm_scale_vector).astype(jnp.bfloat16)
    normed_all = lax.all_gather(rescaled_input, "tp", axis=0, tiled=True)
    gate = jnp.dot(normed_all, gate_weight, preferred_element_type=jnp.float32)
    lifted = jnp.dot(normed_all, up_weight, preferred_element_type=jnp.float32)
    sigmoid_gate = jax.nn.sigmoid(gate)
    activated = gate * sigmoid_gate
    hidden = (activated * lifted).astype(jnp.bfloat16)
    branch = lax.psum_scatter(
        jnp.dot(hidden, down_weight, preferred_element_type=jnp.float32).astype(jnp.bfloat16),
        "tp",
        scatter_dimension=0,
        tiled=True,
    ).astype(jnp.float32)
    mixed = (expanded_hidden + branch).astype(jnp.bfloat16)
    grad_all = lax.all_gather(cotangent, "tp", axis=0, tiled=True)
    grad_hidden = contract_cols(grad_all, down_weight)
    grad_pre = (grad_hidden * lifted * sigmoid_gate * (1.0 + gate * (1.0 - sigmoid_gate))).astype(
        jnp.bfloat16
    )
    grad_lifted = (grad_hidden * activated).astype(jnp.bfloat16)
    grad_normed = lax.psum_scatter(
        (contract_cols(grad_pre, gate_weight) + contract_cols(grad_lifted, up_weight)).astype(
            jnp.bfloat16
        ),
        "tp",
        scatter_dimension=0,
        tiled=True,
    ).astype(jnp.float32)
    gain_applied = grad_normed * norm_scale_vector
    inner_product = jnp.mean(gain_applied * unit_input, axis=-1, keepdims=True)
    token_gradient = (
        cotangent.astype(jnp.float32)
        + reciprocal_root_mean * (gain_applied - unit_input * inner_product)
    ).astype(jnp.bfloat16)
    weight_gate = contract_rows(normed_all, grad_pre).astype(jnp.bfloat16)
    weight_up = contract_rows(normed_all, grad_lifted).astype(jnp.bfloat16)
    weight_down = contract_rows(hidden, grad_all).astype(jnp.bfloat16)
    sum_gate, sum_up, sum_down = (
        lax.psum_scatter(weight_gate, "dp", scatter_dimension=0, tiled=True).astype(jnp.float32),
        lax.psum_scatter(weight_up, "dp", scatter_dimension=0, tiled=True).astype(jnp.float32),
        lax.psum_scatter(weight_down, "dp", scatter_dimension=1, tiled=True).astype(jnp.float32),
    )
    return (
        mixed,
        token_gradient,
        sum_gate.astype(jnp.bfloat16),
        sum_up.astype(jnp.bfloat16),
        sum_down.astype(jnp.bfloat16),
    )


def solution(mesh):
    n_dp, n_tp = mesh.shape["dp"], mesh.shape["tp"]
    in_specs = (
        P(("dp", "tp"), None),
        P(),
        P(None, "tp"),
        P(None, "tp"),
        P("tp", None),
        P(("dp", "tp"), None),
    )
    out_specs = (
        P(("dp", "tp"), None),
        P(("dp", "tp"), None),
        P("dp", "tp"),
        P("dp", "tp"),
        P("tp", "dp"),
    )

    def run(tokens, norm_scale_vector, gate_weight, up_weight, down_weight, cotangent):
        gathered = tokens.size + cotangent.size
        weights = (gate_weight.size + up_weight.size + down_weight.size) // n_tp
        local = sum_weight_gradients
        if (n_dp, n_tp) == (4, 8) and gathered <= weights:
            local = gather_tokens
        return jax.shard_map(
            local, mesh=mesh, in_specs=in_specs, out_specs=out_specs, check_vma=False
        )(tokens, norm_scale_vector, gate_weight, up_weight, down_weight, cotangent)

    return run
```

```python
import functools

import jax
import jax.numpy as jnp
from jax import lax
from jax.experimental import pallas as pl
from jax.experimental.pallas import tpu as pltpu
from jax.sharding import PartitionSpec as P


def contract_rows(left, right):
    return lax.dot_general(
        left, right, (((0,), (0,)), ((), ())), preferred_element_type=jnp.float32
    )


def contract_cols(left, right):
    return lax.dot_general(
        left, right, (((1,), (1,)), ((), ())), preferred_element_type=jnp.float32
    )


TILE = 256
CHUNK = 1024


def project_back(grad_out_t, down_weight):
    return jnp.dot(down_weight, grad_out_t, preferred_element_type=jnp.float32).T


def project(normed, grad_out_t, gate_weight, up_weight, down_weight):
    gate = jnp.dot(normed, gate_weight, preferred_element_type=jnp.float32)
    lifted = jnp.dot(normed, up_weight, preferred_element_type=jnp.float32)
    return gate, lifted, project_back(grad_out_t, down_weight)


def activations(gate, lifted, grad_hidden):
    sigmoid_gate = jax.nn.sigmoid(gate)
    activated = gate * sigmoid_gate
    hidden = (activated * lifted).astype(jnp.bfloat16)
    grad_pre = (grad_hidden * lifted * sigmoid_gate * (1.0 + gate * (1.0 - sigmoid_gate))).astype(
        jnp.bfloat16
    )
    grad_lifted = (grad_hidden * activated).astype(jnp.bfloat16)
    return hidden, grad_pre, grad_lifted


def pack(pieces, rows, arrived):
    copies, at = [], 0
    for i, piece in enumerate(pieces):
        here = pl.ds(at, piece.shape[1])
        copies.append(
            [pltpu.make_async_copy(piece.at[j], rows.at[j, here], arrived.at[j, i]) for j in (0, 1)]
        )
        at += piece.shape[1]
    normed, grad_out = zip(*copies)
    for copy in normed + grad_out:
        copy.start()
    return normed, grad_out


def wait(copies):
    for copy in copies:
        copy.wait()


def in_hbm(*arrays):
    return [pltpu.with_memory_space_constraint(array, pltpu.HBM) for array in arrays]


def height(pieces):
    return sum(piece.shape[1] for piece in pieces)


def norm_kernel(tokens, norm_scale_vector, cotangent, unit):
    expanded_hidden = tokens[...].astype(jnp.float32)
    reciprocal_root_mean = lax.rsqrt(
        jnp.mean(expanded_hidden * expanded_hidden, axis=-1, keepdims=True) + 1e-05
    )
    rescaled_input = expanded_hidden * reciprocal_root_mean * norm_scale_vector[...]
    unit[0] = rescaled_input.astype(unit.dtype)
    unit[1] = cotangent[...]


def normalize(tokens, norm_scale_vector, cotangent):
    return pl.pallas_call(
        norm_kernel,
        out_shape=jax.ShapeDtypeStruct((2, *tokens.shape), jnp.bfloat16),
        name="normalize",
    )(*in_hbm(tokens, norm_scale_vector.reshape(1, -1), cotangent))


def own_kernel(n_pieces, *refs):
    replica, pieces, refs = refs[0], refs[1 : n_pieces + 1], refs[n_pieces + 1 :]
    gate_weight, up_weight, down_weight, hidden, grad_pre, grad_lifted = refs[:6]
    columns, kept, sent, rows, grad_out_t, out_sum, in_sum, arrived = refs[6:]
    step = pl.program_id(0)
    part = kept.shape[1]

    @pl.when(step == 0)
    def _():
        for copies in pack(pieces, rows, arrived):
            wait(copies)
        width = columns.shape[2]
        columns[...] = rows[:, :, pl.ds(pl.multiple_of(replica[0] * width, 128), width)]
        grad_out_t[...] = rows[1].T
        out_sum[...] = jnp.zeros_like(out_sum)
        in_sum[...] = jnp.zeros_like(in_sum)

    hidden[...], grad_pre[...], grad_lifted[...] = activations(
        *project(rows[0], grad_out_t[...], gate_weight[...], up_weight[...], down_weight[...])
    )
    grad_pre_t, grad_lifted_t = grad_pre[...].T, grad_lifted[...].T
    for at in range(0, out_sum.shape[1], CHUNK):
        here = slice(at, at + CHUNK)
        out_sum[:, here] += jnp.dot(
            hidden[...], down_weight[:, here], preferred_element_type=jnp.float32
        )
        in_sum[here] += jnp.dot(
            gate_weight[here], grad_pre_t, preferred_element_type=jnp.float32
        ) + jnp.dot(up_weight[here], grad_lifted_t, preferred_element_type=jnp.float32)

    @pl.when(step == pl.num_programs(0) - 1)
    def _():
        kept[0] = out_sum[:part].astype(kept.dtype)
        sent[0] = out_sum[part:].astype(sent.dtype)
        summed = in_sum[...].T
        kept[1] = summed[:part].astype(kept.dtype)
        sent[1] = summed[part:].astype(sent.dtype)


def own_rows(replica, n_dp, pieces, gate_weight, up_weight, down_weight):
    depth, hidden_units = gate_weight.shape
    count = height(pieces)
    tall = pl.BlockSpec((depth, TILE), lambda i: (0, i))
    wide = pl.BlockSpec((TILE, depth), lambda i: (i, 0))
    slim = pl.BlockSpec((count, TILE), lambda i: (0, i))
    whole = pl.BlockSpec((2, count // 2, depth), lambda i: (0, 0, 0))
    kept = jax.ShapeDtypeStruct((2, count // 2, depth), jnp.bfloat16)
    columns = (2, count, depth // n_dp)
    unit = pltpu.HBM((count, hidden_units), jnp.bfloat16)
    return pl.pallas_call(
        functools.partial(own_kernel, len(pieces)),
        grid=(hidden_units // TILE,),
        in_specs=[pl.BlockSpec(memory_space=pltpu.SMEM)]
        + [pl.BlockSpec(memory_space=pl.ANY)] * len(pieces)
        + [tall, tall, wide],
        out_specs=[slim, slim, slim, pl.BlockSpec(columns, lambda i: (0, 0, 0)), whole, whole],
        out_shape=[unit, unit, unit, pltpu.HBM(columns, jnp.bfloat16), kept, kept],
        scratch_shapes=[
            pltpu.VMEM((2, count, depth), jnp.bfloat16),
            pltpu.VMEM((depth, count), jnp.bfloat16),
            pltpu.VMEM((count, depth), jnp.float32),
            pltpu.VMEM((depth, count), jnp.float32),
            pltpu.SemaphoreType.DMA((2, len(pieces))),
        ],
        compiler_params=pltpu.CompilerParams(vmem_limit_bytes=28 * 2**20),
        cost_estimate=pl.CostEstimate(
            flops=12 * count * depth * hidden_units,
            bytes_accessed=6 * depth * hidden_units,
            transcendentals=count * hidden_units,
        ),
        name="own_rows",
    )(replica, *in_hbm(pieces[0]), *pieces[1:], *in_hbm(gate_weight, up_weight, down_weight))


def all_kernel(n_pieces, *refs):
    replica, pieces, refs = refs[0], refs[1 : n_pieces + 1], refs[n_pieces + 1 :]
    own_hidden, own_grad_pre, own_grad_lifted, own_columns = refs[:4]
    gate_weight, up_weight, down_weight, grad_gate, grad_up, grad_down = refs[4:10]
    rows, normed_t, grad_out, grad_out_t, hidden, grad_pre, grad_lifted, arrived = refs[10:]
    step, last = pl.program_id(0), pl.num_programs(0) - 1
    ahead = own_columns.shape[1]
    width = normed_t.shape[0]

    def weight_gradients():
        grad_gate[...] = jnp.dot(
            normed_t[...], grad_pre[...], preferred_element_type=jnp.float32
        ).astype(grad_gate.dtype)
        grad_up[...] = jnp.dot(
            normed_t[...], grad_lifted[...], preferred_element_type=jnp.float32
        ).astype(grad_up.dtype)
        grad_down[...] = jnp.dot(
            hidden[...].T, grad_out[...], preferred_element_type=jnp.float32
        ).astype(grad_down.dtype)

    def fill(gate, lifted, grad_hidden):
        hidden[:ahead] = own_hidden[...]
        grad_pre[:ahead] = own_grad_pre[...]
        grad_lifted[:ahead] = own_grad_lifted[...]
        hidden[ahead:], grad_pre[ahead:], grad_lifted[ahead:] = activations(
            gate, lifted, grad_hidden
        )

    @pl.when(step == 0)
    def _():
        columns = pl.ds(pl.multiple_of(replica[0] * width, 128), width)
        normed_copies, grad_out_copies = pack(pieces, rows, arrived)
        normed_t[:, :ahead] = own_columns[0].T
        grad_out[:ahead] = own_columns[1]
        wait(normed_copies)
        gate = jnp.dot(rows[0], gate_weight[...], preferred_element_type=jnp.float32)
        lifted = jnp.dot(rows[0], up_weight[...], preferred_element_type=jnp.float32)
        normed_t[:, ahead:] = rows[0, :, columns].T
        wait(grad_out_copies)
        grad_out_t[...] = rows[1].T
        grad_out[ahead:] = rows[1, :, columns]
        fill(gate, lifted, project_back(grad_out_t[...], down_weight[...]))

    @pl.when((step > 0) & (step < last))
    def _():
        products = project(
            rows[0], grad_out_t[...], gate_weight[...], up_weight[...], down_weight[...]
        )
        weight_gradients()
        fill(*products)

    @pl.when(step == last)
    def _():
        weight_gradients()


def all_rows(replica, pieces, units, own_columns, gate_weight, up_weight, down_weight):
    depth, hidden_units = gate_weight.shape
    ahead, width = own_columns.shape[1:]
    behind = height(pieces)
    count = ahead + behind
    tiles = hidden_units // TILE
    tall = pl.BlockSpec((depth, TILE), lambda i: (0, jnp.minimum(i, tiles - 1)))
    wide = pl.BlockSpec((TILE, depth), lambda i: (jnp.minimum(i, tiles - 1), 0))
    slim = pl.BlockSpec((ahead, TILE), lambda i: (0, jnp.minimum(i, tiles - 1)))
    return pl.pallas_call(
        functools.partial(all_kernel, len(pieces)),
        grid=(tiles + 1,),
        in_specs=[pl.BlockSpec(memory_space=pltpu.SMEM)]
        + [pl.BlockSpec(memory_space=pl.ANY)] * len(pieces)
        + [slim, slim, slim, pl.BlockSpec(own_columns.shape, lambda i: (0, 0, 0))]
        + [tall, tall, wide],
        out_specs=[
            pl.BlockSpec((width, TILE), lambda i: (0, jnp.maximum(i - 1, 0))),
            pl.BlockSpec((width, TILE), lambda i: (0, jnp.maximum(i - 1, 0))),
            pl.BlockSpec((TILE, width), lambda i: (jnp.maximum(i - 1, 0), 0)),
        ],
        out_shape=[
            jax.ShapeDtypeStruct((width, hidden_units), jnp.bfloat16),
            jax.ShapeDtypeStruct((width, hidden_units), jnp.bfloat16),
            jax.ShapeDtypeStruct((hidden_units, width), jnp.bfloat16),
        ],
        scratch_shapes=[
            pltpu.VMEM((2, behind, depth), jnp.bfloat16),
            pltpu.VMEM((width, count), jnp.bfloat16),
            pltpu.VMEM((count, width), jnp.bfloat16),
            pltpu.VMEM((depth, behind), jnp.bfloat16),
            pltpu.VMEM((count, TILE), jnp.bfloat16),
            pltpu.VMEM((count, TILE), jnp.bfloat16),
            pltpu.VMEM((count, TILE), jnp.bfloat16),
            pltpu.SemaphoreType.DMA((2, len(pieces))),
        ],
        compiler_params=pltpu.CompilerParams(vmem_limit_bytes=32 * 2**20),
        cost_estimate=pl.CostEstimate(
            flops=6 * (behind * depth + count * width) * hidden_units,
            bytes_accessed=6 * (depth + width) * hidden_units,
            transcendentals=behind * hidden_units,
        ),
        name="all_rows",
    )(replica, *in_hbm(*pieces, *units, own_columns, gate_weight, up_weight, down_weight))


def gather_tokens(tokens, norm_scale_vector, gate_weight, up_weight, down_weight, cotangent):
    n_dp = lax.axis_size("dp")
    n_tp = lax.axis_size("tp")
    replica = lax.axis_index("dp").astype(jnp.int32).reshape(1)
    rows = tokens.shape[0]

    def swap(array, dp_bits, tp_bits):
        pairs = [
            (d * n_tp + t, (d ^ dp_bits) * n_tp + (t ^ tp_bits))
            for d in range(n_dp)
            for t in range(n_tp)
        ]
        return lax.ppermute(array, ("dp", "tp"), pairs)

    def far(pieces):
        return [swap(piece, 0, 1) for piece in pieces]

    expanded_hidden = tokens.astype(jnp.float32)
    reciprocal_root_mean = lax.rsqrt(
        jnp.mean(expanded_hidden * expanded_hidden, axis=-1, keepdims=True) + 1e-05
    )
    unit_input = expanded_hidden * reciprocal_root_mean
    unit0 = normalize(tokens, norm_scale_vector, cotangent)
    unit2, unit1 = swap(unit0, 0, 4), swap(unit0, 0, 2)
    across0 = [swap(unit0, 1, 0), swap(unit0, 2, 0)]
    unit2, unit1, across0, far_unit0, again0 = lax.optimization_barrier(
        (unit2, unit1, across0, swap(unit0, 0, 1), unit0)
    )
    unit3 = swap(unit2, 0, 2)
    across1 = [swap(unit1, 1, 0), swap(unit1, 2, 0), swap(again0, 3, 0)]
    far_unit1, far_across0 = swap(unit1, 0, 1), far(across0)
    unit3, across1, far_unit1, far_across0 = lax.optimization_barrier(
        (unit3, across1, far_unit1, far_across0)
    )
    last = jnp.concatenate([unit2, unit3], axis=1)
    late = jnp.concatenate([unit1, unit2, unit3], axis=1)
    own = [unit0, unit1, last, far_unit0, far_unit1, swap(last, 0, 1)]
    rest = [swap(last, 1, 0), swap(last, 2, 0), swap(late, 3, 0)]
    *units, own_columns, kept, sent = own_rows(
        replica, n_dp, own, gate_weight, up_weight, down_weight
    )
    kept, sent, rest = lax.optimization_barrier((kept, sent, rest))
    pair = (kept.astype(jnp.float32) + swap(sent, 0, 1).astype(jnp.float32)).astype(jnp.bfloat16)
    rest += across1 + far(across1 + rest) + across0 + far_across0
    parts = [swap(pair[:, k * rows : (k + 1) * rows], 0, 2 * k) for k in range(1, n_tp // 2)]
    weight_gradients = all_rows(
        replica, rest, units, own_columns, gate_weight, up_weight, down_weight
    )
    parts, weight_gradients = lax.optimization_barrier((parts, weight_gradients))
    total = pair[:, :rows].astype(jnp.float32) + sum(part.astype(jnp.float32) for part in parts)
    branch, grad_normed = total[0], total[1]
    mixed = (expanded_hidden + branch).astype(jnp.bfloat16)
    gain_applied = grad_normed * norm_scale_vector
    inner_product = jnp.mean(gain_applied * unit_input, axis=-1, keepdims=True)
    token_gradient = (
        cotangent.astype(jnp.float32)
        + reciprocal_root_mean * (gain_applied - unit_input * inner_product)
    ).astype(jnp.bfloat16)
    return mixed, token_gradient, *weight_gradients


def sum_weight_gradients(tokens, norm_scale_vector, gate_weight, up_weight, down_weight, cotangent):
    expanded_hidden = tokens.astype(jnp.float32)
    reciprocal_root_mean = lax.rsqrt(
        jnp.mean(expanded_hidden * expanded_hidden, axis=-1, keepdims=True) + 1e-05
    )
    unit_input = expanded_hidden * reciprocal_root_mean
    rescaled_input = (unit_input * norm_scale_vector).astype(jnp.bfloat16)
    normed_all = lax.all_gather(rescaled_input, "tp", axis=0, tiled=True)
    gate = jnp.dot(normed_all, gate_weight, preferred_element_type=jnp.float32)
    lifted = jnp.dot(normed_all, up_weight, preferred_element_type=jnp.float32)
    sigmoid_gate = jax.nn.sigmoid(gate)
    activated = gate * sigmoid_gate
    hidden = (activated * lifted).astype(jnp.bfloat16)
    branch = lax.psum_scatter(
        jnp.dot(hidden, down_weight, preferred_element_type=jnp.float32).astype(jnp.bfloat16),
        "tp",
        scatter_dimension=0,
        tiled=True,
    ).astype(jnp.float32)
    mixed = (expanded_hidden + branch).astype(jnp.bfloat16)
    grad_all = lax.all_gather(cotangent, "tp", axis=0, tiled=True)
    grad_hidden = contract_cols(grad_all, down_weight)
    grad_pre = (grad_hidden * lifted * sigmoid_gate * (1.0 + gate * (1.0 - sigmoid_gate))).astype(
        jnp.bfloat16
    )
    grad_lifted = (grad_hidden * activated).astype(jnp.bfloat16)
    grad_normed = lax.psum_scatter(
        (contract_cols(grad_pre, gate_weight) + contract_cols(grad_lifted, up_weight)).astype(
            jnp.bfloat16
        ),
        "tp",
        scatter_dimension=0,
        tiled=True,
    ).astype(jnp.float32)
    gain_applied = grad_normed * norm_scale_vector
    inner_product = jnp.mean(gain_applied * unit_input, axis=-1, keepdims=True)
    token_gradient = (
        cotangent.astype(jnp.float32)
        + reciprocal_root_mean * (gain_applied - unit_input * inner_product)
    ).astype(jnp.bfloat16)
    weight_gate = contract_rows(normed_all, grad_pre).astype(jnp.bfloat16)
    weight_up = contract_rows(normed_all, grad_lifted).astype(jnp.bfloat16)
    weight_down = contract_rows(hidden, grad_all).astype(jnp.bfloat16)
    sum_gate, sum_up, sum_down = (
        lax.psum_scatter(weight_gate, "dp", scatter_dimension=0, tiled=True).astype(jnp.float32),
        lax.psum_scatter(weight_up, "dp", scatter_dimension=0, tiled=True).astype(jnp.float32),
        lax.psum_scatter(weight_down, "dp", scatter_dimension=1, tiled=True).astype(jnp.float32),
    )
    return (
        mixed,
        token_gradient,
        sum_gate.astype(jnp.bfloat16),
        sum_up.astype(jnp.bfloat16),
        sum_down.astype(jnp.bfloat16),
    )


def solution(mesh):
    n_dp, n_tp = mesh.shape["dp"], mesh.shape["tp"]
    in_specs = (
        P(("dp", "tp"), None),
        P(),
        P(None, "tp"),
        P(None, "tp"),
        P("tp", None),
        P(("dp", "tp"), None),
    )
    out_specs = (
        P(("dp", "tp"), None),
        P(("dp", "tp"), None),
        P("dp", "tp"),
        P("dp", "tp"),
        P("tp", "dp"),
    )

    def run(tokens, norm_scale_vector, gate_weight, up_weight, down_weight, cotangent):
        gathered = tokens.size + cotangent.size
        weights = (gate_weight.size + up_weight.size + down_weight.size) // n_tp
        local = sum_weight_gradients
        if (n_dp, n_tp) == (4, 8) and gathered <= weights:
            local = gather_tokens
        return jax.shard_map(
            local, mesh=mesh, in_specs=in_specs, out_specs=out_specs, check_vma=False
        )(tokens, norm_scale_vector, gate_weight, up_weight, down_weight, cotangent)

    return run
```

```python
import functools

import jax
import jax.numpy as jnp
from jax import lax
from jax.experimental import pallas as pl
from jax.experimental.pallas import tpu as pltpu
from jax.sharding import PartitionSpec as P


def contract_rows(left, right):
    return lax.dot_general(
        left, right, (((0,), (0,)), ((), ())), preferred_element_type=jnp.float32
    )


def contract_cols(left, right):
    return lax.dot_general(
        left, right, (((1,), (1,)), ((), ())), preferred_element_type=jnp.float32
    )


TILE = 256
CHUNK = 1024


def project_back(grad_out_t, down_weight):
    return jnp.dot(down_weight, grad_out_t, preferred_element_type=jnp.float32).T


def project(normed, grad_out_t, gate_weight, up_weight, down_weight):
    gate = jnp.dot(normed, gate_weight, preferred_element_type=jnp.float32)
    lifted = jnp.dot(normed, up_weight, preferred_element_type=jnp.float32)
    return gate, lifted, project_back(grad_out_t, down_weight)


def activations(gate, lifted, grad_hidden):
    sigmoid_gate = jax.nn.sigmoid(gate)
    activated = gate * sigmoid_gate
    hidden = (activated * lifted).astype(jnp.bfloat16)
    grad_pre = (grad_hidden * lifted * sigmoid_gate * (1.0 + gate * (1.0 - sigmoid_gate))).astype(
        jnp.bfloat16
    )
    grad_lifted = (grad_hidden * activated).astype(jnp.bfloat16)
    return hidden, grad_pre, grad_lifted


def pack(pieces, rows, arrived):
    copies, at = [], 0
    for i, piece in enumerate(pieces):
        here = pl.ds(at, piece.shape[1])
        copies.append(
            [pltpu.make_async_copy(piece.at[j], rows.at[j, here], arrived.at[j, i]) for j in (0, 1)]
        )
        at += piece.shape[1]
    normed, grad_out = zip(*copies)
    for copy in normed + grad_out:
        copy.start()
    return normed, grad_out


def wait(copies):
    for copy in copies:
        copy.wait()


def in_hbm(*arrays):
    return [pltpu.with_memory_space_constraint(array, pltpu.HBM) for array in arrays]


def in_vmem(*arrays):
    return [pltpu.with_memory_space_constraint(array, pltpu.VMEM) for array in arrays]


def height(pieces):
    return sum(piece.shape[1] for piece in pieces)


def norm_kernel(tokens, norm_scale_vector, cotangent, unit):
    expanded_hidden = tokens[...].astype(jnp.float32)
    reciprocal_root_mean = lax.rsqrt(
        jnp.mean(expanded_hidden * expanded_hidden, axis=-1, keepdims=True) + 1e-05
    )
    rescaled_input = expanded_hidden * reciprocal_root_mean * norm_scale_vector[...]
    unit[0] = rescaled_input.astype(unit.dtype)
    unit[1] = cotangent[...]


def normalize(tokens, norm_scale_vector, cotangent):
    return pl.pallas_call(
        norm_kernel,
        out_shape=pltpu.VMEM((2, *tokens.shape), jnp.bfloat16),
        name="normalize",
    )(*in_hbm(tokens, norm_scale_vector.reshape(1, -1), cotangent))


def own_kernel(n_pieces, *refs):
    replica, pieces, refs = refs[0], refs[1 : n_pieces + 1], refs[n_pieces + 1 :]
    gate_weight, up_weight, down_weight, hidden, grad_pre, grad_lifted = refs[:6]
    columns, kept, sent, rows, grad_out_t, out_sum, in_sum, arrived = refs[6:]
    step = pl.program_id(0)
    part = kept.shape[1]

    @pl.when(step == 0)
    def _():
        for copies in pack(pieces, rows, arrived):
            wait(copies)
        width = columns.shape[2]
        columns[...] = rows[:, :, pl.ds(pl.multiple_of(replica[0] * width, 128), width)]
        grad_out_t[...] = rows[1].T
        out_sum[...] = jnp.zeros_like(out_sum)
        in_sum[...] = jnp.zeros_like(in_sum)

    hidden[...], grad_pre[...], grad_lifted[...] = activations(
        *project(rows[0], grad_out_t[...], gate_weight[...], up_weight[...], down_weight[...])
    )
    grad_pre_t, grad_lifted_t = grad_pre[...].T, grad_lifted[...].T
    for at in range(0, out_sum.shape[1], CHUNK):
        here = slice(at, at + CHUNK)
        out_sum[:, here] += jnp.dot(
            hidden[...], down_weight[:, here], preferred_element_type=jnp.float32
        )
        in_sum[here] += jnp.dot(
            gate_weight[here], grad_pre_t, preferred_element_type=jnp.float32
        ) + jnp.dot(up_weight[here], grad_lifted_t, preferred_element_type=jnp.float32)

    @pl.when(step == pl.num_programs(0) - 1)
    def _():
        kept[0] = out_sum[:part].astype(kept.dtype)
        sent[0] = out_sum[part:].astype(sent.dtype)
        summed = in_sum[...].T
        kept[1] = summed[:part].astype(kept.dtype)
        sent[1] = summed[part:].astype(sent.dtype)


def own_rows(replica, n_dp, pieces, gate_weight, up_weight, down_weight):
    depth, hidden_units = gate_weight.shape
    count = height(pieces)
    tall = pl.BlockSpec((depth, TILE), lambda i: (0, i))
    wide = pl.BlockSpec((TILE, depth), lambda i: (i, 0))
    slim = pl.BlockSpec((count, TILE), lambda i: (0, i))
    whole = pl.BlockSpec((2, count // 2, depth), lambda i: (0, 0, 0))
    kept = jax.ShapeDtypeStruct((2, count // 2, depth), jnp.bfloat16)
    columns = (2, count, depth // n_dp)
    unit = pltpu.VMEM((count, hidden_units), jnp.bfloat16)
    return pl.pallas_call(
        functools.partial(own_kernel, len(pieces)),
        grid=(hidden_units // TILE,),
        in_specs=[pl.BlockSpec(memory_space=pltpu.SMEM)]
        + [pl.BlockSpec(memory_space=pl.ANY)] * len(pieces)
        + [tall, tall, wide],
        out_specs=[slim, slim, slim, pl.BlockSpec(columns, lambda i: (0, 0, 0)), whole, whole],
        out_shape=[unit, unit, unit, pltpu.VMEM(columns, jnp.bfloat16), kept, kept],
        scratch_shapes=[
            pltpu.VMEM((2, count, depth), jnp.bfloat16),
            pltpu.VMEM((depth, count), jnp.bfloat16),
            pltpu.VMEM((count, depth), jnp.float32),
            pltpu.VMEM((depth, count), jnp.float32),
            pltpu.SemaphoreType.DMA((2, len(pieces))),
        ],
        compiler_params=pltpu.CompilerParams(vmem_limit_bytes=28 * 2**20),
        cost_estimate=pl.CostEstimate(
            flops=12 * count * depth * hidden_units,
            bytes_accessed=6 * depth * hidden_units,
            transcendentals=count * hidden_units,
        ),
        name="own_rows",
    )(replica, *in_vmem(*pieces), *in_hbm(gate_weight, up_weight, down_weight))


def all_kernel(n_pieces, *refs):
    replica, pieces, refs = refs[0], refs[1 : n_pieces + 1], refs[n_pieces + 1 :]
    own_hidden, own_grad_pre, own_grad_lifted, own_columns = refs[:4]
    gate_weight, up_weight, down_weight, grad_gate, grad_up, grad_down = refs[4:10]
    rows, normed_t, grad_out, grad_out_t, hidden, grad_pre, grad_lifted, arrived = refs[10:]
    step, last = pl.program_id(0), pl.num_programs(0) - 1
    ahead = own_columns.shape[1]
    width = normed_t.shape[0]

    def weight_gradients():
        grad_gate[...] = jnp.dot(
            normed_t[...], grad_pre[...], preferred_element_type=jnp.float32
        ).astype(grad_gate.dtype)
        grad_up[...] = jnp.dot(
            normed_t[...], grad_lifted[...], preferred_element_type=jnp.float32
        ).astype(grad_up.dtype)
        grad_down[...] = jnp.dot(
            hidden[...].T, grad_out[...], preferred_element_type=jnp.float32
        ).astype(grad_down.dtype)

    def fill(gate, lifted, grad_hidden):
        hidden[:ahead] = own_hidden[...]
        grad_pre[:ahead] = own_grad_pre[...]
        grad_lifted[:ahead] = own_grad_lifted[...]
        hidden[ahead:], grad_pre[ahead:], grad_lifted[ahead:] = activations(
            gate, lifted, grad_hidden
        )

    @pl.when(step == 0)
    def _():
        columns = pl.ds(pl.multiple_of(replica[0] * width, 128), width)
        normed_copies, grad_out_copies = pack(pieces, rows, arrived)
        normed_t[:, :ahead] = own_columns[0].T
        grad_out[:ahead] = own_columns[1]
        wait(normed_copies)
        gate = jnp.dot(rows[0], gate_weight[...], preferred_element_type=jnp.float32)
        lifted = jnp.dot(rows[0], up_weight[...], preferred_element_type=jnp.float32)
        normed_t[:, ahead:] = rows[0, :, columns].T
        wait(grad_out_copies)
        grad_out_t[...] = rows[1].T
        grad_out[ahead:] = rows[1, :, columns]
        fill(gate, lifted, project_back(grad_out_t[...], down_weight[...]))

    @pl.when((step > 0) & (step < last))
    def _():
        products = project(
            rows[0], grad_out_t[...], gate_weight[...], up_weight[...], down_weight[...]
        )
        weight_gradients()
        fill(*products)

    @pl.when(step == last)
    def _():
        weight_gradients()


def all_rows(replica, pieces, units, own_columns, gate_weight, up_weight, down_weight):
    depth, hidden_units = gate_weight.shape
    ahead, width = own_columns.shape[1:]
    behind = height(pieces)
    count = ahead + behind
    tiles = hidden_units // TILE
    tall = pl.BlockSpec((depth, TILE), lambda i: (0, jnp.minimum(i, tiles - 1)))
    wide = pl.BlockSpec((TILE, depth), lambda i: (jnp.minimum(i, tiles - 1), 0))
    slim = pl.BlockSpec((ahead, TILE), lambda i: (0, jnp.minimum(i, tiles - 1)))
    return pl.pallas_call(
        functools.partial(all_kernel, len(pieces)),
        grid=(tiles + 1,),
        in_specs=[pl.BlockSpec(memory_space=pltpu.SMEM)]
        + [pl.BlockSpec(memory_space=pl.ANY)] * len(pieces)
        + [slim, slim, slim, pl.BlockSpec(own_columns.shape, lambda i: (0, 0, 0))]
        + [tall, tall, wide],
        out_specs=[
            pl.BlockSpec((width, TILE), lambda i: (0, jnp.maximum(i - 1, 0))),
            pl.BlockSpec((width, TILE), lambda i: (0, jnp.maximum(i - 1, 0))),
            pl.BlockSpec((TILE, width), lambda i: (jnp.maximum(i - 1, 0), 0)),
        ],
        out_shape=[
            jax.ShapeDtypeStruct((width, hidden_units), jnp.bfloat16),
            jax.ShapeDtypeStruct((width, hidden_units), jnp.bfloat16),
            jax.ShapeDtypeStruct((hidden_units, width), jnp.bfloat16),
        ],
        scratch_shapes=[
            pltpu.VMEM((2, behind, depth), jnp.bfloat16),
            pltpu.VMEM((width, count), jnp.bfloat16),
            pltpu.VMEM((count, width), jnp.bfloat16),
            pltpu.VMEM((depth, behind), jnp.bfloat16),
            pltpu.VMEM((count, TILE), jnp.bfloat16),
            pltpu.VMEM((count, TILE), jnp.bfloat16),
            pltpu.VMEM((count, TILE), jnp.bfloat16),
            pltpu.SemaphoreType.DMA((2, len(pieces))),
        ],
        compiler_params=pltpu.CompilerParams(vmem_limit_bytes=32 * 2**20),
        cost_estimate=pl.CostEstimate(
            flops=6 * (behind * depth + count * width) * hidden_units,
            bytes_accessed=6 * (depth + width) * hidden_units,
            transcendentals=behind * hidden_units,
        ),
        name="all_rows",
    )(
        replica,
        *in_vmem(*pieces, *units, own_columns),
        *in_hbm(gate_weight, up_weight, down_weight),
    )


def gather_tokens(tokens, norm_scale_vector, gate_weight, up_weight, down_weight, cotangent):
    n_dp = lax.axis_size("dp")
    n_tp = lax.axis_size("tp")
    replica = lax.axis_index("dp").astype(jnp.int32).reshape(1)
    rows = tokens.shape[0]

    def swap(array, dp_bits, tp_bits):
        pairs = [
            (d * n_tp + t, (d ^ dp_bits) * n_tp + (t ^ tp_bits))
            for d in range(n_dp)
            for t in range(n_tp)
        ]
        return lax.ppermute(array, ("dp", "tp"), pairs)

    def far(pieces):
        return [swap(piece, 0, 1) for piece in pieces]

    expanded_hidden = tokens.astype(jnp.float32)
    reciprocal_root_mean = lax.rsqrt(
        jnp.mean(expanded_hidden * expanded_hidden, axis=-1, keepdims=True) + 1e-05
    )
    unit_input = expanded_hidden * reciprocal_root_mean
    unit0 = normalize(tokens, norm_scale_vector, cotangent)
    unit2, unit1 = swap(unit0, 0, 4), swap(unit0, 0, 2)
    across0 = [swap(unit0, b, 0) for b in range(1, n_dp)]
    unit2, unit1, across0, again0 = lax.optimization_barrier((unit2, unit1, across0, unit0))
    unit3 = swap(unit2, 0, 2)
    across1 = [swap(unit1, 1, 0), swap(unit1, 2, 0)]
    far_units, far_across0 = far([again0, unit1]), far(across0)
    unit3, across1, far_units, far_across0 = lax.optimization_barrier(
        (unit3, across1, far_units, far_across0)
    )
    last = jnp.concatenate([unit2, unit3], axis=1)
    late = jnp.concatenate([unit1, unit2, unit3], axis=1)
    own = [unit0, unit1, last] + far_units + [swap(last, 0, 1)]
    rest = [swap(last, 1, 0), swap(last, 2, 0), swap(late, 3, 0)]
    *units, own_columns, kept, sent = own_rows(
        replica, n_dp, own, gate_weight, up_weight, down_weight
    )
    kept, sent, rest = lax.optimization_barrier((kept, sent, rest))
    pair = (kept.astype(jnp.float32) + swap(sent, 0, 1).astype(jnp.float32)).astype(jnp.bfloat16)
    rest += across1 + far(across1 + rest) + across0 + far_across0
    parts = [swap(pair[:, k * rows : (k + 1) * rows], 0, 2 * k) for k in range(1, n_tp // 2)]
    weight_gradients = all_rows(
        replica, rest, units, own_columns, gate_weight, up_weight, down_weight
    )
    parts, weight_gradients = lax.optimization_barrier((parts, weight_gradients))
    total = pair[:, :rows].astype(jnp.float32) + sum(part.astype(jnp.float32) for part in parts)
    branch, grad_normed = total[0], total[1]
    mixed = (expanded_hidden + branch).astype(jnp.bfloat16)
    gain_applied = grad_normed * norm_scale_vector
    inner_product = jnp.mean(gain_applied * unit_input, axis=-1, keepdims=True)
    token_gradient = (
        cotangent.astype(jnp.float32)
        + reciprocal_root_mean * (gain_applied - unit_input * inner_product)
    ).astype(jnp.bfloat16)
    return mixed, token_gradient, *weight_gradients


def sum_weight_gradients(tokens, norm_scale_vector, gate_weight, up_weight, down_weight, cotangent):
    expanded_hidden = tokens.astype(jnp.float32)
    reciprocal_root_mean = lax.rsqrt(
        jnp.mean(expanded_hidden * expanded_hidden, axis=-1, keepdims=True) + 1e-05
    )
    unit_input = expanded_hidden * reciprocal_root_mean
    rescaled_input = (unit_input * norm_scale_vector).astype(jnp.bfloat16)
    normed_all = lax.all_gather(rescaled_input, "tp", axis=0, tiled=True)
    gate = jnp.dot(normed_all, gate_weight, preferred_element_type=jnp.float32)
    lifted = jnp.dot(normed_all, up_weight, preferred_element_type=jnp.float32)
    sigmoid_gate = jax.nn.sigmoid(gate)
    activated = gate * sigmoid_gate
    hidden = (activated * lifted).astype(jnp.bfloat16)
    branch = lax.psum_scatter(
        jnp.dot(hidden, down_weight, preferred_element_type=jnp.float32).astype(jnp.bfloat16),
        "tp",
        scatter_dimension=0,
        tiled=True,
    ).astype(jnp.float32)
    mixed = (expanded_hidden + branch).astype(jnp.bfloat16)
    grad_all = lax.all_gather(cotangent, "tp", axis=0, tiled=True)
    grad_hidden = contract_cols(grad_all, down_weight)
    grad_pre = (grad_hidden * lifted * sigmoid_gate * (1.0 + gate * (1.0 - sigmoid_gate))).astype(
        jnp.bfloat16
    )
    grad_lifted = (grad_hidden * activated).astype(jnp.bfloat16)
    grad_normed = lax.psum_scatter(
        (contract_cols(grad_pre, gate_weight) + contract_cols(grad_lifted, up_weight)).astype(
            jnp.bfloat16
        ),
        "tp",
        scatter_dimension=0,
        tiled=True,
    ).astype(jnp.float32)
    gain_applied = grad_normed * norm_scale_vector
    inner_product = jnp.mean(gain_applied * unit_input, axis=-1, keepdims=True)
    token_gradient = (
        cotangent.astype(jnp.float32)
        + reciprocal_root_mean * (gain_applied - unit_input * inner_product)
    ).astype(jnp.bfloat16)
    weight_gate = contract_rows(normed_all, grad_pre).astype(jnp.bfloat16)
    weight_up = contract_rows(normed_all, grad_lifted).astype(jnp.bfloat16)
    weight_down = contract_rows(hidden, grad_all).astype(jnp.bfloat16)
    sum_gate, sum_up, sum_down = (
        lax.psum_scatter(weight_gate, "dp", scatter_dimension=0, tiled=True).astype(jnp.float32),
        lax.psum_scatter(weight_up, "dp", scatter_dimension=0, tiled=True).astype(jnp.float32),
        lax.psum_scatter(weight_down, "dp", scatter_dimension=1, tiled=True).astype(jnp.float32),
    )
    return (
        mixed,
        token_gradient,
        sum_gate.astype(jnp.bfloat16),
        sum_up.astype(jnp.bfloat16),
        sum_down.astype(jnp.bfloat16),
    )


def solution(mesh):
    n_dp, n_tp = mesh.shape["dp"], mesh.shape["tp"]
    in_specs = (
        P(("dp", "tp"), None),
        P(),
        P(None, "tp"),
        P(None, "tp"),
        P("tp", None),
        P(("dp", "tp"), None),
    )
    out_specs = (
        P(("dp", "tp"), None),
        P(("dp", "tp"), None),
        P("dp", "tp"),
        P("dp", "tp"),
        P("tp", "dp"),
    )

    def run(tokens, norm_scale_vector, gate_weight, up_weight, down_weight, cotangent):
        gathered = tokens.size + cotangent.size
        weights = (gate_weight.size + up_weight.size + down_weight.size) // n_tp
        local = sum_weight_gradients
        if (n_dp, n_tp) == (4, 8) and gathered <= weights:
            local = gather_tokens
        return jax.shard_map(
            local, mesh=mesh, in_specs=in_specs, out_specs=out_specs, check_vma=False
        )(tokens, norm_scale_vector, gate_weight, up_weight, down_weight, cotangent)

    return run
```

```python
import functools

import jax
import jax.numpy as jnp
from jax import lax
from jax.experimental import pallas as pl
from jax.experimental.pallas import tpu as pltpu
from jax.sharding import PartitionSpec as P


def contract_rows(left, right):
    return lax.dot_general(
        left, right, (((0,), (0,)), ((), ())), preferred_element_type=jnp.float32
    )


def contract_cols(left, right):
    return lax.dot_general(
        left, right, (((1,), (1,)), ((), ())), preferred_element_type=jnp.float32
    )


TILE = 256
CHUNK = 1024


def project_back(grad_out_t, down_weight):
    return jnp.dot(down_weight, grad_out_t, preferred_element_type=jnp.float32).T


def project(normed, grad_out_t, gate_weight, up_weight, down_weight):
    gate = jnp.dot(normed, gate_weight, preferred_element_type=jnp.float32)
    lifted = jnp.dot(normed, up_weight, preferred_element_type=jnp.float32)
    return gate, lifted, project_back(grad_out_t, down_weight)


def activations(gate, lifted, grad_hidden):
    sigmoid_gate = jax.nn.sigmoid(gate)
    activated = gate * sigmoid_gate
    hidden = (activated * lifted).astype(jnp.bfloat16)
    grad_pre = (grad_hidden * lifted * sigmoid_gate * (1.0 + gate * (1.0 - sigmoid_gate))).astype(
        jnp.bfloat16
    )
    grad_lifted = (grad_hidden * activated).astype(jnp.bfloat16)
    return hidden, grad_pre, grad_lifted


def pack(pieces, rows):
    at = 0
    for piece in pieces:
        rows[:, at : at + piece.shape[1]] = piece[...]
        at += piece.shape[1]


def in_hbm(*arrays):
    return [pltpu.with_memory_space_constraint(array, pltpu.HBM) for array in arrays]


def in_vmem(*arrays):
    return [pltpu.with_memory_space_constraint(array, pltpu.VMEM) for array in arrays]


def height(pieces):
    return sum(piece.shape[1] for piece in pieces)


def norm_kernel(tokens, norm_scale_vector, cotangent, unit):
    expanded_hidden = tokens[...].astype(jnp.float32)
    reciprocal_root_mean = lax.rsqrt(
        jnp.mean(expanded_hidden * expanded_hidden, axis=-1, keepdims=True) + 1e-05
    )
    rescaled_input = expanded_hidden * reciprocal_root_mean * norm_scale_vector[...]
    unit[0] = rescaled_input.astype(unit.dtype)
    unit[1] = cotangent[...]


def normalize(tokens, norm_scale_vector, cotangent):
    return pl.pallas_call(
        norm_kernel,
        out_shape=pltpu.VMEM((2, *tokens.shape), jnp.bfloat16),
        name="normalize",
    )(*in_hbm(tokens, norm_scale_vector.reshape(1, -1), cotangent))


def own_kernel(n_pieces, *refs):
    replica, pieces, refs = refs[0], refs[1 : n_pieces + 1], refs[n_pieces + 1 :]
    weights, refs = refs[:3], refs[3:]
    columns, kept, sent, rows, grad_out_t, out_sum, in_sum = refs[3:]
    part = kept.shape[1]

    def first():
        pack(pieces, rows)
        width = columns.shape[2]
        columns[...] = rows[:, :, pl.ds(pl.multiple_of(replica[0] * width, 128), width)]
        grad_out_t[...] = rows[1].T
        out_sum[...] = jnp.zeros_like(out_sum)
        in_sum[...] = jnp.zeros_like(in_sum)

    def body(gate_weight, up_weight, down_weight):
        step = pl.program_id(0)
        pl.when(step == 0)(first)
        hidden, grad_pre, grad_lifted = activations(
            *project(rows[0], grad_out_t[...], gate_weight[...], up_weight[...], down_weight[...])
        )
        here = pl.ds(pl.multiple_of(step * TILE, TILE), TILE)
        for ref, unit in zip(refs, (hidden, grad_pre, grad_lifted)):
            ref[:, here] = unit
        grad_pre_t, grad_lifted_t = grad_pre.T, grad_lifted.T
        for at in range(0, out_sum.shape[1], CHUNK):
            here = slice(at, at + CHUNK)
            out_sum[:, here] += jnp.dot(
                hidden, down_weight[:, here], preferred_element_type=jnp.float32
            )
            in_sum[here] += jnp.dot(
                gate_weight[here], grad_pre_t, preferred_element_type=jnp.float32
            ) + jnp.dot(up_weight[here], grad_lifted_t, preferred_element_type=jnp.float32)

    depth, hidden_units = weights[0].shape
    tall = pl.BlockSpec((depth, TILE), lambda i: (0, i))
    wide = pl.BlockSpec((TILE, depth), lambda i: (i, 0))
    pltpu.emit_pipeline(body, grid=(hidden_units // TILE,), in_specs=[tall, tall, wide])(*weights)
    kept[0] = out_sum[:part].astype(kept.dtype)
    sent[0] = out_sum[part:].astype(sent.dtype)
    summed = in_sum[...].T
    kept[1] = summed[:part].astype(kept.dtype)
    sent[1] = summed[part:].astype(sent.dtype)


def own_rows(replica, n_dp, pieces, gate_weight, up_weight, down_weight):
    depth, hidden_units = gate_weight.shape
    count = height(pieces)
    half = pltpu.VMEM((2, count // 2, depth), jnp.bfloat16)
    columns = (2, count, depth // n_dp)
    unit = pltpu.VMEM((count, hidden_units), jnp.bfloat16)
    return pl.pallas_call(
        functools.partial(own_kernel, len(pieces)),
        in_specs=[pl.BlockSpec(memory_space=pltpu.SMEM)]
        + [pl.BlockSpec(memory_space=pltpu.VMEM)] * len(pieces)
        + [pl.BlockSpec(memory_space=pl.ANY)] * 3,
        out_shape=[unit, unit, unit, pltpu.VMEM(columns, jnp.bfloat16), half, half],
        scratch_shapes=[
            pltpu.VMEM((2, count, depth), jnp.bfloat16),
            pltpu.VMEM((depth, count), jnp.bfloat16),
            pltpu.VMEM((count, depth), jnp.float32),
            pltpu.VMEM((depth, count), jnp.float32),
        ],
        compiler_params=pltpu.CompilerParams(vmem_limit_bytes=28 * 2**20),
        cost_estimate=pl.CostEstimate(
            flops=12 * count * depth * hidden_units,
            bytes_accessed=6 * depth * hidden_units,
            transcendentals=count * hidden_units,
        ),
        name="own_rows",
    )(replica, *in_vmem(*pieces), *in_hbm(gate_weight, up_weight, down_weight))


def all_kernel(n_pieces, *refs):
    replica, pieces, refs = refs[0], refs[1 : n_pieces + 1], refs[n_pieces + 1 :]
    own_hidden, own_grad_pre, own_grad_lifted, own_columns = refs[:4]
    weights, gradients = refs[4:7], refs[7:10]
    rows, normed_t, grad_out, grad_out_t, hidden, grad_pre, grad_lifted = refs[10:]
    depth, hidden_units = weights[0].shape
    tiles = hidden_units // TILE
    ahead = own_columns.shape[1]
    width = normed_t.shape[0]

    def weight_gradients(grad_gate, grad_up, grad_down):
        grad_gate[...] = jnp.dot(
            normed_t[...], grad_pre[...], preferred_element_type=jnp.float32
        ).astype(grad_gate.dtype)
        grad_up[...] = jnp.dot(
            normed_t[...], grad_lifted[...], preferred_element_type=jnp.float32
        ).astype(grad_up.dtype)
        grad_down[...] = jnp.dot(
            hidden[...].T, grad_out[...], preferred_element_type=jnp.float32
        ).astype(grad_down.dtype)

    def fill(step, gate, lifted, grad_hidden):
        here = pl.ds(pl.multiple_of(step * TILE, TILE), TILE)
        hidden[:ahead] = own_hidden[:, here]
        grad_pre[:ahead] = own_grad_pre[:, here]
        grad_lifted[:ahead] = own_grad_lifted[:, here]
        hidden[ahead:], grad_pre[ahead:], grad_lifted[ahead:] = activations(
            gate, lifted, grad_hidden
        )

    def body(gate_weight, up_weight, down_weight, *outs):
        step = pl.program_id(0)

        @pl.when(step == 0)
        def _():
            columns = pl.ds(pl.multiple_of(replica[0] * width, 128), width)
            pack(pieces, rows)
            normed_t[:, :ahead] = own_columns[0].T
            normed_t[:, ahead:] = rows[0, :, columns].T
            grad_out[:ahead] = own_columns[1]
            grad_out[ahead:] = rows[1, :, columns]
            grad_out_t[...] = rows[1].T
            fill(
                0,
                *project(
                    rows[0], grad_out_t[...], gate_weight[...], up_weight[...], down_weight[...]
                ),
            )

        @pl.when((step > 0) & (step < tiles))
        def _():
            products = project(
                rows[0], grad_out_t[...], gate_weight[...], up_weight[...], down_weight[...]
            )
            weight_gradients(*outs)
            fill(step, *products)

        @pl.when(step == tiles)
        def _():
            weight_gradients(*outs)

    tall = pl.BlockSpec((depth, TILE), lambda i: (0, jnp.minimum(i, tiles - 1)))
    wide = pl.BlockSpec((TILE, depth), lambda i: (jnp.minimum(i, tiles - 1), 0))
    tall_out = pl.BlockSpec((width, TILE), lambda i: (0, jnp.maximum(i - 1, 0)))
    wide_out = pl.BlockSpec((TILE, width), lambda i: (jnp.maximum(i - 1, 0), 0))
    pltpu.emit_pipeline(
        body,
        grid=(tiles + 1,),
        in_specs=[tall, tall, wide],
        out_specs=[tall_out, tall_out, wide_out],
    )(*weights, *gradients)


def all_rows(replica, pieces, units, own_columns, gate_weight, up_weight, down_weight):
    depth, hidden_units = gate_weight.shape
    ahead, width = own_columns.shape[1:]
    behind = height(pieces)
    count = ahead + behind
    return pl.pallas_call(
        functools.partial(all_kernel, len(pieces)),
        in_specs=[pl.BlockSpec(memory_space=pltpu.SMEM)]
        + [pl.BlockSpec(memory_space=pltpu.VMEM)] * (len(pieces) + 4)
        + [pl.BlockSpec(memory_space=pl.ANY)] * 3,
        out_specs=[pl.BlockSpec(memory_space=pl.ANY)] * 3,
        out_shape=[
            jax.ShapeDtypeStruct((width, hidden_units), jnp.bfloat16),
            jax.ShapeDtypeStruct((width, hidden_units), jnp.bfloat16),
            jax.ShapeDtypeStruct((hidden_units, width), jnp.bfloat16),
        ],
        scratch_shapes=[
            pltpu.VMEM((2, behind, depth), jnp.bfloat16),
            pltpu.VMEM((width, count), jnp.bfloat16),
            pltpu.VMEM((count, width), jnp.bfloat16),
            pltpu.VMEM((depth, behind), jnp.bfloat16),
            pltpu.VMEM((count, TILE), jnp.bfloat16),
            pltpu.VMEM((count, TILE), jnp.bfloat16),
            pltpu.VMEM((count, TILE), jnp.bfloat16),
        ],
        compiler_params=pltpu.CompilerParams(vmem_limit_bytes=32 * 2**20),
        cost_estimate=pl.CostEstimate(
            flops=6 * (behind * depth + count * width) * hidden_units,
            bytes_accessed=6 * (depth + width) * hidden_units,
            transcendentals=behind * hidden_units,
        ),
        name="all_rows",
    )(
        replica,
        *in_vmem(*pieces, *units, own_columns),
        *in_hbm(gate_weight, up_weight, down_weight),
    )


def gather_tokens(tokens, norm_scale_vector, gate_weight, up_weight, down_weight, cotangent):
    n_dp = lax.axis_size("dp")
    n_tp = lax.axis_size("tp")
    replica = lax.axis_index("dp").astype(jnp.int32).reshape(1)
    rows = tokens.shape[0]

    def swap(array, dp_bits, tp_bits):
        pairs = [
            (d * n_tp + t, (d ^ dp_bits) * n_tp + (t ^ tp_bits))
            for d in range(n_dp)
            for t in range(n_tp)
        ]
        return lax.ppermute(array, ("dp", "tp"), pairs)

    def far(pieces):
        return [swap(piece, 0, 1) for piece in pieces]

    expanded_hidden = tokens.astype(jnp.float32)
    reciprocal_root_mean = lax.rsqrt(
        jnp.mean(expanded_hidden * expanded_hidden, axis=-1, keepdims=True) + 1e-05
    )
    unit_input = expanded_hidden * reciprocal_root_mean
    unit0 = normalize(tokens, norm_scale_vector, cotangent)
    unit2, unit1 = swap(unit0, 0, 4), swap(unit0, 0, 2)
    across0 = [swap(unit0, b, 0) for b in range(1, n_dp)]
    unit2, unit1, across0, again0 = lax.optimization_barrier((unit2, unit1, across0, unit0))
    unit3 = swap(unit2, 0, 2)
    across1 = [swap(unit1, 1, 0), swap(unit1, 2, 0)]
    far_units, far_across0 = far([again0, unit1]), far(across0)
    unit3, across1, far_units, far_across0 = lax.optimization_barrier(
        (unit3, across1, far_units, far_across0)
    )
    last = jnp.concatenate([unit2, unit3], axis=1)
    late = jnp.concatenate([unit1, unit2, unit3], axis=1)
    own = [unit0, unit1, last] + far_units + [swap(last, 0, 1)]
    rest = [swap(last, 1, 0), swap(last, 2, 0), swap(late, 3, 0)]
    *units, own_columns, kept, sent = own_rows(
        replica, n_dp, own, gate_weight, up_weight, down_weight
    )
    kept, sent, rest = lax.optimization_barrier((kept, sent, rest))
    pair = (kept.astype(jnp.float32) + swap(sent, 0, 1).astype(jnp.float32)).astype(jnp.bfloat16)
    rest += across1 + far(across1 + rest) + across0 + far_across0
    parts = [swap(pair[:, k * rows : (k + 1) * rows], 0, 2 * k) for k in range(1, n_tp // 2)]
    weight_gradients = all_rows(
        replica, rest, units, own_columns, gate_weight, up_weight, down_weight
    )
    parts, weight_gradients = lax.optimization_barrier((parts, weight_gradients))
    total = pair[:, :rows].astype(jnp.float32) + sum(part.astype(jnp.float32) for part in parts)
    branch, grad_normed = total[0], total[1]
    mixed = (expanded_hidden + branch).astype(jnp.bfloat16)
    gain_applied = grad_normed * norm_scale_vector
    inner_product = jnp.mean(gain_applied * unit_input, axis=-1, keepdims=True)
    token_gradient = (
        cotangent.astype(jnp.float32)
        + reciprocal_root_mean * (gain_applied - unit_input * inner_product)
    ).astype(jnp.bfloat16)
    return mixed, token_gradient, *weight_gradients


def sum_weight_gradients(tokens, norm_scale_vector, gate_weight, up_weight, down_weight, cotangent):
    expanded_hidden = tokens.astype(jnp.float32)
    reciprocal_root_mean = lax.rsqrt(
        jnp.mean(expanded_hidden * expanded_hidden, axis=-1, keepdims=True) + 1e-05
    )
    unit_input = expanded_hidden * reciprocal_root_mean
    rescaled_input = (unit_input * norm_scale_vector).astype(jnp.bfloat16)
    normed_all = lax.all_gather(rescaled_input, "tp", axis=0, tiled=True)
    gate = jnp.dot(normed_all, gate_weight, preferred_element_type=jnp.float32)
    lifted = jnp.dot(normed_all, up_weight, preferred_element_type=jnp.float32)
    sigmoid_gate = jax.nn.sigmoid(gate)
    activated = gate * sigmoid_gate
    hidden = (activated * lifted).astype(jnp.bfloat16)
    branch = lax.psum_scatter(
        jnp.dot(hidden, down_weight, preferred_element_type=jnp.float32).astype(jnp.bfloat16),
        "tp",
        scatter_dimension=0,
        tiled=True,
    ).astype(jnp.float32)
    mixed = (expanded_hidden + branch).astype(jnp.bfloat16)
    grad_all = lax.all_gather(cotangent, "tp", axis=0, tiled=True)
    grad_hidden = contract_cols(grad_all, down_weight)
    grad_pre = (grad_hidden * lifted * sigmoid_gate * (1.0 + gate * (1.0 - sigmoid_gate))).astype(
        jnp.bfloat16
    )
    grad_lifted = (grad_hidden * activated).astype(jnp.bfloat16)
    grad_normed = lax.psum_scatter(
        (contract_cols(grad_pre, gate_weight) + contract_cols(grad_lifted, up_weight)).astype(
            jnp.bfloat16
        ),
        "tp",
        scatter_dimension=0,
        tiled=True,
    ).astype(jnp.float32)
    gain_applied = grad_normed * norm_scale_vector
    inner_product = jnp.mean(gain_applied * unit_input, axis=-1, keepdims=True)
    token_gradient = (
        cotangent.astype(jnp.float32)
        + reciprocal_root_mean * (gain_applied - unit_input * inner_product)
    ).astype(jnp.bfloat16)
    weight_gate = contract_rows(normed_all, grad_pre).astype(jnp.bfloat16)
    weight_up = contract_rows(normed_all, grad_lifted).astype(jnp.bfloat16)
    weight_down = contract_rows(hidden, grad_all).astype(jnp.bfloat16)
    sum_gate, sum_up, sum_down = (
        lax.psum_scatter(weight_gate, "dp", scatter_dimension=0, tiled=True).astype(jnp.float32),
        lax.psum_scatter(weight_up, "dp", scatter_dimension=0, tiled=True).astype(jnp.float32),
        lax.psum_scatter(weight_down, "dp", scatter_dimension=1, tiled=True).astype(jnp.float32),
    )
    return (
        mixed,
        token_gradient,
        sum_gate.astype(jnp.bfloat16),
        sum_up.astype(jnp.bfloat16),
        sum_down.astype(jnp.bfloat16),
    )


def solution(mesh):
    n_dp, n_tp = mesh.shape["dp"], mesh.shape["tp"]
    in_specs = (
        P(("dp", "tp"), None),
        P(),
        P(None, "tp"),
        P(None, "tp"),
        P("tp", None),
        P(("dp", "tp"), None),
    )
    out_specs = (
        P(("dp", "tp"), None),
        P(("dp", "tp"), None),
        P("dp", "tp"),
        P("dp", "tp"),
        P("tp", "dp"),
    )

    def run(tokens, norm_scale_vector, gate_weight, up_weight, down_weight, cotangent):
        gathered = tokens.size + cotangent.size
        weights = (gate_weight.size + up_weight.size + down_weight.size) // n_tp
        local = sum_weight_gradients
        if (n_dp, n_tp) == (4, 8) and gathered <= weights:
            local = gather_tokens
        return jax.shard_map(
            local, mesh=mesh, in_specs=in_specs, out_specs=out_specs, check_vma=False
        )(tokens, norm_scale_vector, gate_weight, up_weight, down_weight, cotangent)

    return run
```

```python
import functools

import jax
import jax.numpy as jnp
from jax import lax
from jax.experimental import pallas as pl
from jax.experimental.pallas import tpu as pltpu
from jax.sharding import PartitionSpec as P


def contract_rows(left, right):
    return lax.dot_general(
        left, right, (((0,), (0,)), ((), ())), preferred_element_type=jnp.float32
    )


def contract_cols(left, right):
    return lax.dot_general(
        left, right, (((1,), (1,)), ((), ())), preferred_element_type=jnp.float32
    )


TILE = 256
CHUNK = 1024


def project_back(grad_out_t, down_weight):
    return jnp.dot(down_weight, grad_out_t, preferred_element_type=jnp.float32).T


def project(normed, grad_out_t, gate_weight, up_weight, down_weight):
    gate = jnp.dot(normed, gate_weight, preferred_element_type=jnp.float32)
    lifted = jnp.dot(normed, up_weight, preferred_element_type=jnp.float32)
    return gate, lifted, project_back(grad_out_t, down_weight)


def activations(gate, lifted, grad_hidden):
    sigmoid_gate = jax.nn.sigmoid(gate)
    activated = gate * sigmoid_gate
    hidden = (activated * lifted).astype(jnp.bfloat16)
    grad_pre = (grad_hidden * lifted * sigmoid_gate * (1.0 + gate * (1.0 - sigmoid_gate))).astype(
        jnp.bfloat16
    )
    grad_lifted = (grad_hidden * activated).astype(jnp.bfloat16)
    return hidden, grad_pre, grad_lifted


def pack(pieces, rows):
    at = 0
    for piece in pieces:
        rows[:, at : at + piece.shape[1]] = piece[...]
        at += piece.shape[1]


def in_hbm(*arrays):
    return [pltpu.with_memory_space_constraint(array, pltpu.HBM) for array in arrays]


def in_vmem(*arrays):
    return [pltpu.with_memory_space_constraint(array, pltpu.VMEM) for array in arrays]


def height(pieces):
    return sum(piece.shape[1] for piece in pieces)


def norm_kernel(tokens, norm_scale_vector, cotangent, unit):
    expanded_hidden = tokens[...].astype(jnp.float32)
    reciprocal_root_mean = lax.rsqrt(
        jnp.mean(expanded_hidden * expanded_hidden, axis=-1, keepdims=True) + 1e-05
    )
    rescaled_input = expanded_hidden * reciprocal_root_mean * norm_scale_vector[...]
    unit[0] = rescaled_input.astype(unit.dtype)
    unit[1] = cotangent[...]


def normalize(tokens, norm_scale_vector, cotangent):
    return pl.pallas_call(
        norm_kernel,
        out_shape=pltpu.VMEM((2, *tokens.shape), jnp.bfloat16),
        name="normalize",
    )(*in_hbm(tokens, norm_scale_vector.reshape(1, -1), cotangent))


def own_kernel(n_pieces, *refs):
    replica, pieces, refs = refs[0], refs[1 : n_pieces + 1], refs[n_pieces + 1 :]
    weights, refs = refs[:3], refs[3:]
    columns, kept, sent, rows, grad_out_t, out_sum, in_sum = refs[3:]
    part = kept.shape[1]

    def first():
        pack(pieces, rows)
        width = columns.shape[2]
        columns[...] = rows[:, :, pl.ds(pl.multiple_of(replica[0] * width, 128), width)]
        grad_out_t[...] = rows[1].T
        out_sum[...] = jnp.zeros_like(out_sum)
        in_sum[...] = jnp.zeros_like(in_sum)

    def body(gate_weight, up_weight, down_weight):
        step = pl.program_id(0)
        pl.when(step == 0)(first)
        hidden, grad_pre, grad_lifted = activations(
            *project(rows[0], grad_out_t[...], gate_weight[...], up_weight[...], down_weight[...])
        )
        here = pl.ds(pl.multiple_of(step * TILE, TILE), TILE)
        for ref, unit in zip(refs, (hidden, grad_pre, grad_lifted)):
            ref[:, here] = unit
        grad_pre_t, grad_lifted_t = grad_pre.T, grad_lifted.T
        for at in range(0, out_sum.shape[1], CHUNK):
            here = slice(at, at + CHUNK)
            out_sum[:, here] += jnp.dot(
                hidden, down_weight[:, here], preferred_element_type=jnp.float32
            )
            in_sum[here] += jnp.dot(
                gate_weight[here], grad_pre_t, preferred_element_type=jnp.float32
            ) + jnp.dot(up_weight[here], grad_lifted_t, preferred_element_type=jnp.float32)

    depth, hidden_units = weights[0].shape
    tall = pl.BlockSpec((depth, TILE), lambda i: (0, i))
    wide = pl.BlockSpec((TILE, depth), lambda i: (i, 0))
    pltpu.emit_pipeline(body, grid=(hidden_units // TILE,), in_specs=[tall, tall, wide])(*weights)
    kept[0] = out_sum[:part].astype(kept.dtype)
    sent[0] = out_sum[part:].astype(sent.dtype)
    summed = in_sum[...].T
    kept[1] = summed[:part].astype(kept.dtype)
    sent[1] = summed[part:].astype(sent.dtype)


def own_rows(replica, n_dp, pieces, gate_weight, up_weight, down_weight):
    depth, hidden_units = gate_weight.shape
    count = height(pieces)
    half = pltpu.VMEM((2, count // 2, depth), jnp.bfloat16)
    columns = (2, count, depth // n_dp)
    unit = pltpu.VMEM((count, hidden_units), jnp.bfloat16)
    return pl.pallas_call(
        functools.partial(own_kernel, len(pieces)),
        in_specs=[pl.BlockSpec(memory_space=pltpu.SMEM)]
        + [pl.BlockSpec(memory_space=pltpu.VMEM)] * len(pieces)
        + [pl.BlockSpec(memory_space=pl.ANY)] * 3,
        out_shape=[unit, unit, unit, pltpu.VMEM(columns, jnp.bfloat16), half, half],
        scratch_shapes=[
            pltpu.VMEM((2, count, depth), jnp.bfloat16),
            pltpu.VMEM((depth, count), jnp.bfloat16),
            pltpu.VMEM((count, depth), jnp.float32),
            pltpu.VMEM((depth, count), jnp.float32),
        ],
        compiler_params=pltpu.CompilerParams(vmem_limit_bytes=28 * 2**20),
        cost_estimate=pl.CostEstimate(
            flops=12 * count * depth * hidden_units,
            bytes_accessed=6 * depth * hidden_units,
            transcendentals=count * hidden_units,
        ),
        name="own_rows",
    )(replica, *in_vmem(*pieces), *in_hbm(gate_weight, up_weight, down_weight))


def all_kernel(n_pieces, *refs):
    replica, pieces, refs = refs[0], refs[1 : n_pieces + 1], refs[n_pieces + 1 :]
    own_hidden, own_grad_pre, own_grad_lifted, own_columns = refs[:4]
    weights, gradients = refs[4:7], refs[7:10]
    rows, normed_t, grad_out, grad_out_t, hidden, grad_pre, grad_lifted = refs[10:]
    depth, hidden_units = weights[0].shape
    tiles = hidden_units // TILE
    ahead = own_columns.shape[1]
    width = normed_t.shape[0]

    def weight_gradients(grad_gate, grad_up, grad_down):
        grad_gate[...] = jnp.dot(
            normed_t[...], grad_pre[...], preferred_element_type=jnp.float32
        ).astype(grad_gate.dtype)
        grad_up[...] = jnp.dot(
            normed_t[...], grad_lifted[...], preferred_element_type=jnp.float32
        ).astype(grad_up.dtype)
        grad_down[...] = jnp.dot(
            hidden[...].T, grad_out[...], preferred_element_type=jnp.float32
        ).astype(grad_down.dtype)

    def fill(step, gate, lifted, grad_hidden):
        here = pl.ds(pl.multiple_of(step * TILE, TILE), TILE)
        hidden[:ahead] = own_hidden[:, here]
        grad_pre[:ahead] = own_grad_pre[:, here]
        grad_lifted[:ahead] = own_grad_lifted[:, here]
        hidden[ahead:], grad_pre[ahead:], grad_lifted[ahead:] = activations(
            gate, lifted, grad_hidden
        )

    def body(gate_weight, up_weight, down_weight, *outs):
        step = pl.program_id(0)

        @pl.when(step == 0)
        def _():
            columns = pl.ds(pl.multiple_of(replica[0] * width, 128), width)
            pack(pieces, rows)
            normed_t[:, :ahead] = own_columns[0].T
            normed_t[:, ahead:] = rows[0, :, columns].T
            grad_out[:ahead] = own_columns[1]
            grad_out[ahead:] = rows[1, :, columns]
            grad_out_t[...] = rows[1].T
            fill(
                0,
                *project(
                    rows[0], grad_out_t[...], gate_weight[...], up_weight[...], down_weight[...]
                ),
            )

        @pl.when((step > 0) & (step < tiles))
        def _():
            products = project(
                rows[0], grad_out_t[...], gate_weight[...], up_weight[...], down_weight[...]
            )
            weight_gradients(*outs)
            fill(step, *products)

        @pl.when(step == tiles)
        def _():
            weight_gradients(*outs)

    tall = pl.BlockSpec((depth, TILE), lambda i: (0, jnp.minimum(i, tiles - 1)))
    wide = pl.BlockSpec((TILE, depth), lambda i: (jnp.minimum(i, tiles - 1), 0))
    tall_out = pl.BlockSpec((width, TILE), lambda i: (0, jnp.maximum(i - 1, 0)))
    wide_out = pl.BlockSpec((TILE, width), lambda i: (jnp.maximum(i - 1, 0), 0))
    pltpu.emit_pipeline(
        body,
        grid=(tiles + 1,),
        in_specs=[tall, tall, wide],
        out_specs=[tall_out, tall_out, wide_out],
    )(*weights, *gradients)


def all_rows(replica, pieces, units, own_columns, gate_weight, up_weight, down_weight):
    depth, hidden_units = gate_weight.shape
    ahead, width = own_columns.shape[1:]
    behind = height(pieces)
    count = ahead + behind
    return pl.pallas_call(
        functools.partial(all_kernel, len(pieces)),
        in_specs=[pl.BlockSpec(memory_space=pltpu.SMEM)]
        + [pl.BlockSpec(memory_space=pltpu.VMEM)] * (len(pieces) + 4)
        + [pl.BlockSpec(memory_space=pl.ANY)] * 3,
        out_specs=[pl.BlockSpec(memory_space=pl.ANY)] * 3,
        out_shape=[
            jax.ShapeDtypeStruct((width, hidden_units), jnp.bfloat16),
            jax.ShapeDtypeStruct((width, hidden_units), jnp.bfloat16),
            jax.ShapeDtypeStruct((hidden_units, width), jnp.bfloat16),
        ],
        scratch_shapes=[
            pltpu.VMEM((2, behind, depth), jnp.bfloat16),
            pltpu.VMEM((width, count), jnp.bfloat16),
            pltpu.VMEM((count, width), jnp.bfloat16),
            pltpu.VMEM((depth, behind), jnp.bfloat16),
            pltpu.VMEM((count, TILE), jnp.bfloat16),
            pltpu.VMEM((count, TILE), jnp.bfloat16),
            pltpu.VMEM((count, TILE), jnp.bfloat16),
        ],
        compiler_params=pltpu.CompilerParams(vmem_limit_bytes=32 * 2**20),
        cost_estimate=pl.CostEstimate(
            flops=6 * (behind * depth + count * width) * hidden_units,
            bytes_accessed=6 * (depth + width) * hidden_units,
            transcendentals=behind * hidden_units,
        ),
        name="all_rows",
    )(
        replica,
        *in_vmem(*pieces, *units, own_columns),
        *in_hbm(gate_weight, up_weight, down_weight),
    )


def gather_tokens(tokens, norm_scale_vector, gate_weight, up_weight, down_weight, cotangent):
    n_dp = lax.axis_size("dp")
    n_tp = lax.axis_size("tp")
    replica = lax.axis_index("dp").astype(jnp.int32).reshape(1)
    rows = tokens.shape[0]

    def swap(array, dp_bits, tp_bits):
        pairs = [
            (d * n_tp + t, (d ^ dp_bits) * n_tp + (t ^ tp_bits))
            for d in range(n_dp)
            for t in range(n_tp)
        ]
        return lax.ppermute(array, ("dp", "tp"), pairs)

    def far(pieces):
        return [swap(piece, 0, 1) for piece in pieces]

    expanded_hidden = tokens.astype(jnp.float32)
    reciprocal_root_mean = lax.rsqrt(
        jnp.mean(expanded_hidden * expanded_hidden, axis=-1, keepdims=True) + 1e-05
    )
    unit_input = expanded_hidden * reciprocal_root_mean
    unit0 = normalize(tokens, norm_scale_vector, cotangent)
    unit2, unit1 = swap(unit0, 0, 4), swap(unit0, 0, 2)
    across = [swap(unit0, 1, 0), swap(unit0, 2, 0)]
    early = jnp.concatenate([unit0, unit1], axis=1)
    unit2, unit1, across, early, again0 = lax.optimization_barrier(
        (unit2, unit1, across, early, unit0)
    )
    unit3 = swap(unit2, 0, 2)
    across1 = [swap(unit1, 1, 0), swap(unit1, 2, 0)]
    far_units = far([again0, unit1])
    last = jnp.concatenate([unit2, unit3], axis=1)
    across1, far_units, last = lax.optimization_barrier((across1, far_units, last))
    own = [unit0, unit1, last] + far_units + [swap(last, 0, 1)]
    rest = [swap(last, b, 0) for b in range(1, n_dp)] + [swap(early, 3, 0)]
    *units, own_columns, kept, sent = own_rows(
        replica, n_dp, own, gate_weight, up_weight, down_weight
    )
    kept, sent, rest = lax.optimization_barrier((kept, sent, rest))
    pair = (kept.astype(jnp.float32) + swap(sent, 0, 1).astype(jnp.float32)).astype(jnp.bfloat16)
    rest += across + across1
    rest += far(rest)
    parts = [swap(pair[:, k * rows : (k + 1) * rows], 0, 2 * k) for k in range(1, n_tp // 2)]
    weight_gradients = all_rows(
        replica, rest, units, own_columns, gate_weight, up_weight, down_weight
    )
    parts, weight_gradients = lax.optimization_barrier((parts, weight_gradients))
    total = pair[:, :rows].astype(jnp.float32) + sum(part.astype(jnp.float32) for part in parts)
    branch, grad_normed = total[0], total[1]
    mixed = (expanded_hidden + branch).astype(jnp.bfloat16)
    gain_applied = grad_normed * norm_scale_vector
    inner_product = jnp.mean(gain_applied * unit_input, axis=-1, keepdims=True)
    token_gradient = (
        cotangent.astype(jnp.float32)
        + reciprocal_root_mean * (gain_applied - unit_input * inner_product)
    ).astype(jnp.bfloat16)
    return mixed, token_gradient, *weight_gradients


def sum_weight_gradients(tokens, norm_scale_vector, gate_weight, up_weight, down_weight, cotangent):
    expanded_hidden = tokens.astype(jnp.float32)
    reciprocal_root_mean = lax.rsqrt(
        jnp.mean(expanded_hidden * expanded_hidden, axis=-1, keepdims=True) + 1e-05
    )
    unit_input = expanded_hidden * reciprocal_root_mean
    rescaled_input = (unit_input * norm_scale_vector).astype(jnp.bfloat16)
    normed_all = lax.all_gather(rescaled_input, "tp", axis=0, tiled=True)
    gate = jnp.dot(normed_all, gate_weight, preferred_element_type=jnp.float32)
    lifted = jnp.dot(normed_all, up_weight, preferred_element_type=jnp.float32)
    sigmoid_gate = jax.nn.sigmoid(gate)
    activated = gate * sigmoid_gate
    hidden = (activated * lifted).astype(jnp.bfloat16)
    branch = lax.psum_scatter(
        jnp.dot(hidden, down_weight, preferred_element_type=jnp.float32).astype(jnp.bfloat16),
        "tp",
        scatter_dimension=0,
        tiled=True,
    ).astype(jnp.float32)
    mixed = (expanded_hidden + branch).astype(jnp.bfloat16)
    grad_all = lax.all_gather(cotangent, "tp", axis=0, tiled=True)
    grad_hidden = contract_cols(grad_all, down_weight)
    grad_pre = (grad_hidden * lifted * sigmoid_gate * (1.0 + gate * (1.0 - sigmoid_gate))).astype(
        jnp.bfloat16
    )
    grad_lifted = (grad_hidden * activated).astype(jnp.bfloat16)
    grad_normed = lax.psum_scatter(
        (contract_cols(grad_pre, gate_weight) + contract_cols(grad_lifted, up_weight)).astype(
            jnp.bfloat16
        ),
        "tp",
        scatter_dimension=0,
        tiled=True,
    ).astype(jnp.float32)
    gain_applied = grad_normed * norm_scale_vector
    inner_product = jnp.mean(gain_applied * unit_input, axis=-1, keepdims=True)
    token_gradient = (
        cotangent.astype(jnp.float32)
        + reciprocal_root_mean * (gain_applied - unit_input * inner_product)
    ).astype(jnp.bfloat16)
    weight_gate = contract_rows(normed_all, grad_pre).astype(jnp.bfloat16)
    weight_up = contract_rows(normed_all, grad_lifted).astype(jnp.bfloat16)
    weight_down = contract_rows(hidden, grad_all).astype(jnp.bfloat16)
    sum_gate, sum_up, sum_down = (
        lax.psum_scatter(weight_gate, "dp", scatter_dimension=0, tiled=True).astype(jnp.float32),
        lax.psum_scatter(weight_up, "dp", scatter_dimension=0, tiled=True).astype(jnp.float32),
        lax.psum_scatter(weight_down, "dp", scatter_dimension=1, tiled=True).astype(jnp.float32),
    )
    return (
        mixed,
        token_gradient,
        sum_gate.astype(jnp.bfloat16),
        sum_up.astype(jnp.bfloat16),
        sum_down.astype(jnp.bfloat16),
    )


def solution(mesh):
    n_dp, n_tp = mesh.shape["dp"], mesh.shape["tp"]
    in_specs = (
        P(("dp", "tp"), None),
        P(),
        P(None, "tp"),
        P(None, "tp"),
        P("tp", None),
        P(("dp", "tp"), None),
    )
    out_specs = (
        P(("dp", "tp"), None),
        P(("dp", "tp"), None),
        P("dp", "tp"),
        P("dp", "tp"),
        P("tp", "dp"),
    )

    def run(tokens, norm_scale_vector, gate_weight, up_weight, down_weight, cotangent):
        gathered = tokens.size + cotangent.size
        weights = (gate_weight.size + up_weight.size + down_weight.size) // n_tp
        local = sum_weight_gradients
        if (n_dp, n_tp) == (4, 8) and gathered <= weights:
            local = gather_tokens
        return jax.shard_map(
            local, mesh=mesh, in_specs=in_specs, out_specs=out_specs, check_vma=False
        )(tokens, norm_scale_vector, gate_weight, up_weight, down_weight, cotangent)

    return run
```

```python
import functools

import jax
import jax.numpy as jnp
from jax import lax
from jax.experimental import pallas as pl
from jax.experimental.pallas import tpu as pltpu
from jax.sharding import PartitionSpec as P


def contract_rows(left, right):
    return lax.dot_general(
        left, right, (((0,), (0,)), ((), ())), preferred_element_type=jnp.float32
    )


def contract_cols(left, right):
    return lax.dot_general(
        left, right, (((1,), (1,)), ((), ())), preferred_element_type=jnp.float32
    )


TILE = 256
CHUNK = 1024


def project_back(grad_out_t, down_weight):
    return jnp.dot(down_weight, grad_out_t, preferred_element_type=jnp.float32).T


def project(normed, grad_out_t, gate_weight, up_weight, down_weight):
    gate = jnp.dot(normed, gate_weight, preferred_element_type=jnp.float32)
    lifted = jnp.dot(normed, up_weight, preferred_element_type=jnp.float32)
    return gate, lifted, project_back(grad_out_t, down_weight)


def activations(gate, lifted, grad_hidden):
    sigmoid_gate = jax.nn.sigmoid(gate)
    activated = gate * sigmoid_gate
    hidden = (activated * lifted).astype(jnp.bfloat16)
    grad_pre = (grad_hidden * lifted * sigmoid_gate * (1.0 + gate * (1.0 - sigmoid_gate))).astype(
        jnp.bfloat16
    )
    grad_lifted = (grad_hidden * activated).astype(jnp.bfloat16)
    return hidden, grad_pre, grad_lifted


def pack(pieces, rows):
    at = 0
    for piece in pieces:
        rows[:, at : at + piece.shape[1]] = piece[...]
        at += piece.shape[1]


def in_hbm(*arrays):
    return [pltpu.with_memory_space_constraint(array, pltpu.HBM) for array in arrays]


def in_vmem(*arrays):
    return [pltpu.with_memory_space_constraint(array, pltpu.VMEM) for array in arrays]


def height(pieces):
    return sum(piece.shape[1] for piece in pieces)


def norm_kernel(tokens, norm_scale_vector, cotangent, unit):
    expanded_hidden = tokens[...].astype(jnp.float32)
    reciprocal_root_mean = lax.rsqrt(
        jnp.mean(expanded_hidden * expanded_hidden, axis=-1, keepdims=True) + 1e-05
    )
    rescaled_input = expanded_hidden * reciprocal_root_mean * norm_scale_vector[...]
    unit[0] = rescaled_input.astype(unit.dtype)
    unit[1] = cotangent[...]


def normalize(tokens, norm_scale_vector, cotangent):
    return pl.pallas_call(
        norm_kernel,
        out_shape=pltpu.VMEM((2, *tokens.shape), jnp.bfloat16),
        name="normalize",
    )(*in_hbm(tokens, norm_scale_vector.reshape(1, -1), cotangent))


def first_kernel(n_pieces, *refs):
    replica, pieces, refs = refs[0], refs[1 : n_pieces + 1], refs[n_pieces + 1 :]
    weights, refs = refs[:3], refs[3:]
    columns, kept, sent, rows, grad_out_t, out_sum, in_sum = refs[3:]
    part, own = kept.shape[1], out_sum.shape[0]

    def first():
        pack(pieces, rows)
        width = columns.shape[2]
        columns[...] = rows[:, :, pl.ds(pl.multiple_of(replica[0] * width, 128), width)]
        grad_out_t[...] = rows[1].T
        out_sum[...] = jnp.zeros_like(out_sum)
        in_sum[...] = jnp.zeros_like(in_sum)

    def body(gate_weight, up_weight, down_weight):
        step = pl.program_id(0)
        pl.when(step == 0)(first)
        hidden, grad_pre, grad_lifted = activations(
            *project(rows[0], grad_out_t[...], gate_weight[...], up_weight[...], down_weight[...])
        )
        here = pl.ds(pl.multiple_of(step * TILE, TILE), TILE)
        for ref, unit in zip(refs, (hidden, grad_pre, grad_lifted)):
            ref[:, here] = unit
        grad_pre_t, grad_lifted_t = grad_pre[:own].T, grad_lifted[:own].T
        for at in range(0, out_sum.shape[1], CHUNK):
            here = slice(at, at + CHUNK)
            out_sum[:, here] += jnp.dot(
                hidden[:own], down_weight[:, here], preferred_element_type=jnp.float32
            )
            in_sum[here] += jnp.dot(
                gate_weight[here], grad_pre_t, preferred_element_type=jnp.float32
            ) + jnp.dot(up_weight[here], grad_lifted_t, preferred_element_type=jnp.float32)

    depth, hidden_units = weights[0].shape
    tall = pl.BlockSpec((depth, TILE), lambda i: (0, i))
    wide = pl.BlockSpec((TILE, depth), lambda i: (i, 0))
    pltpu.emit_pipeline(body, grid=(hidden_units // TILE,), in_specs=[tall, tall, wide])(*weights)
    kept[0] = out_sum[:part].astype(kept.dtype)
    sent[0] = out_sum[part:].astype(sent.dtype)
    summed = in_sum[...].T
    kept[1] = summed[:part].astype(kept.dtype)
    sent[1] = summed[part:].astype(sent.dtype)


def first_rows(replica, n_dp, own_pieces, more_pieces, gate_weight, up_weight, down_weight):
    depth, hidden_units = gate_weight.shape
    pieces = own_pieces + more_pieces
    own, count = height(own_pieces), height(pieces)
    half = pltpu.VMEM((2, own // 2, depth), jnp.bfloat16)
    columns = (2, count, depth // n_dp)
    unit = pltpu.VMEM((count, hidden_units), jnp.bfloat16)
    return pl.pallas_call(
        functools.partial(first_kernel, len(pieces)),
        in_specs=[pl.BlockSpec(memory_space=pltpu.SMEM)]
        + [pl.BlockSpec(memory_space=pltpu.VMEM)] * len(pieces)
        + [pl.BlockSpec(memory_space=pl.ANY)] * 3,
        out_shape=[unit, unit, unit, pltpu.VMEM(columns, jnp.bfloat16), half, half],
        scratch_shapes=[
            pltpu.VMEM((2, count, depth), jnp.bfloat16),
            pltpu.VMEM((depth, count), jnp.bfloat16),
            pltpu.VMEM((own, depth), jnp.float32),
            pltpu.VMEM((depth, own), jnp.float32),
        ],
        compiler_params=pltpu.CompilerParams(vmem_limit_bytes=32 * 2**20),
        cost_estimate=pl.CostEstimate(
            flops=6 * (count + own) * depth * hidden_units,
            bytes_accessed=6 * depth * hidden_units,
            transcendentals=count * hidden_units,
        ),
        name="first_rows",
    )(replica, *in_vmem(*pieces), *in_hbm(gate_weight, up_weight, down_weight))


def all_kernel(n_pieces, *refs):
    replica, pieces, refs = refs[0], refs[1 : n_pieces + 1], refs[n_pieces + 1 :]
    own_hidden, own_grad_pre, own_grad_lifted, own_columns = refs[:4]
    weights, gradients = refs[4:7], refs[7:10]
    rows, normed_t, grad_out, grad_out_t, hidden, grad_pre, grad_lifted = refs[10:]
    depth, hidden_units = weights[0].shape
    tiles = hidden_units // TILE
    ahead = own_columns.shape[1]
    width = normed_t.shape[0]

    def weight_gradients(grad_gate, grad_up, grad_down):
        grad_gate[...] = jnp.dot(
            normed_t[...], grad_pre[...], preferred_element_type=jnp.float32
        ).astype(grad_gate.dtype)
        grad_up[...] = jnp.dot(
            normed_t[...], grad_lifted[...], preferred_element_type=jnp.float32
        ).astype(grad_up.dtype)
        grad_down[...] = jnp.dot(
            hidden[...].T, grad_out[...], preferred_element_type=jnp.float32
        ).astype(grad_down.dtype)

    def fill(step, gate, lifted, grad_hidden):
        here = pl.ds(pl.multiple_of(step * TILE, TILE), TILE)
        hidden[:ahead] = own_hidden[:, here]
        grad_pre[:ahead] = own_grad_pre[:, here]
        grad_lifted[:ahead] = own_grad_lifted[:, here]
        hidden[ahead:], grad_pre[ahead:], grad_lifted[ahead:] = activations(
            gate, lifted, grad_hidden
        )

    def body(gate_weight, up_weight, down_weight, *outs):
        step = pl.program_id(0)

        @pl.when(step == 0)
        def _():
            columns = pl.ds(pl.multiple_of(replica[0] * width, 128), width)
            pack(pieces, rows)
            normed_t[:, :ahead] = own_columns[0].T
            normed_t[:, ahead:] = rows[0, :, columns].T
            grad_out[:ahead] = own_columns[1]
            grad_out[ahead:] = rows[1, :, columns]
            grad_out_t[...] = rows[1].T
            fill(
                0,
                *project(
                    rows[0], grad_out_t[...], gate_weight[...], up_weight[...], down_weight[...]
                ),
            )

        @pl.when((step > 0) & (step < tiles))
        def _():
            products = project(
                rows[0], grad_out_t[...], gate_weight[...], up_weight[...], down_weight[...]
            )
            weight_gradients(*outs)
            fill(step, *products)

        @pl.when(step == tiles)
        def _():
            weight_gradients(*outs)

    tall = pl.BlockSpec((depth, TILE), lambda i: (0, jnp.minimum(i, tiles - 1)))
    wide = pl.BlockSpec((TILE, depth), lambda i: (jnp.minimum(i, tiles - 1), 0))
    tall_out = pl.BlockSpec((width, TILE), lambda i: (0, jnp.maximum(i - 1, 0)))
    wide_out = pl.BlockSpec((TILE, width), lambda i: (jnp.maximum(i - 1, 0), 0))
    pltpu.emit_pipeline(
        body,
        grid=(tiles + 1,),
        in_specs=[tall, tall, wide],
        out_specs=[tall_out, tall_out, wide_out],
    )(*weights, *gradients)


def all_rows(replica, pieces, units, own_columns, gate_weight, up_weight, down_weight):
    depth, hidden_units = gate_weight.shape
    ahead, width = own_columns.shape[1:]
    behind = height(pieces)
    count = ahead + behind
    return pl.pallas_call(
        functools.partial(all_kernel, len(pieces)),
        in_specs=[pl.BlockSpec(memory_space=pltpu.SMEM)]
        + [pl.BlockSpec(memory_space=pltpu.VMEM)] * (len(pieces) + 4)
        + [pl.BlockSpec(memory_space=pl.ANY)] * 3,
        out_specs=[pl.BlockSpec(memory_space=pl.ANY)] * 3,
        out_shape=[
            jax.ShapeDtypeStruct((width, hidden_units), jnp.bfloat16),
            jax.ShapeDtypeStruct((width, hidden_units), jnp.bfloat16),
            jax.ShapeDtypeStruct((hidden_units, width), jnp.bfloat16),
        ],
        scratch_shapes=[
            pltpu.VMEM((2, behind, depth), jnp.bfloat16),
            pltpu.VMEM((width, count), jnp.bfloat16),
            pltpu.VMEM((count, width), jnp.bfloat16),
            pltpu.VMEM((depth, behind), jnp.bfloat16),
            pltpu.VMEM((count, TILE), jnp.bfloat16),
            pltpu.VMEM((count, TILE), jnp.bfloat16),
            pltpu.VMEM((count, TILE), jnp.bfloat16),
        ],
        compiler_params=pltpu.CompilerParams(vmem_limit_bytes=32 * 2**20),
        cost_estimate=pl.CostEstimate(
            flops=6 * (behind * depth + count * width) * hidden_units,
            bytes_accessed=6 * (depth + width) * hidden_units,
            transcendentals=behind * hidden_units,
        ),
        name="all_rows",
    )(
        replica,
        *in_vmem(*pieces, *units, own_columns),
        *in_hbm(gate_weight, up_weight, down_weight),
    )


def gather_tokens(tokens, norm_scale_vector, gate_weight, up_weight, down_weight, cotangent):
    n_dp = lax.axis_size("dp")
    n_tp = lax.axis_size("tp")
    replica = lax.axis_index("dp").astype(jnp.int32).reshape(1)
    rows = tokens.shape[0]

    def swap(array, dp_bits, tp_bits):
        pairs = [
            (d * n_tp + t, (d ^ dp_bits) * n_tp + (t ^ tp_bits))
            for d in range(n_dp)
            for t in range(n_tp)
        ]
        return lax.ppermute(array, ("dp", "tp"), pairs)

    def far(pieces):
        return [swap(piece, 0, 1) for piece in pieces]

    expanded_hidden = tokens.astype(jnp.float32)
    reciprocal_root_mean = lax.rsqrt(
        jnp.mean(expanded_hidden * expanded_hidden, axis=-1, keepdims=True) + 1e-05
    )
    unit_input = expanded_hidden * reciprocal_root_mean
    unit0 = normalize(tokens, norm_scale_vector, cotangent)
    unit2, unit1 = swap(unit0, 0, 4), swap(unit0, 0, 2)
    across = [swap(unit0, 1, 0), swap(unit0, 2, 0)]
    early = jnp.concatenate([unit0, unit1], axis=1)
    unit2, unit1, across, early, again0 = lax.optimization_barrier(
        (unit2, unit1, across, early, unit0)
    )
    unit3 = swap(unit2, 0, 2)
    across1 = [swap(unit1, 1, 0), swap(unit1, 2, 0)]
    far_units, far_across = far([again0, unit1]), far(across)
    last = jnp.concatenate([unit2, unit3], axis=1)
    across1, far_units, far_across, last = lax.optimization_barrier(
        (across1, far_units, far_across, last)
    )
    own = [unit0, unit1, last] + far_units + [swap(last, 0, 1)]
    more = across + across1 + far_across + far(across1)
    rest = [swap(last, b, 0) for b in range(1, n_dp)] + [swap(early, 3, 0)]
    *units, columns, kept, sent = first_rows(
        replica, n_dp, own, more, gate_weight, up_weight, down_weight
    )
    kept, sent, rest = lax.optimization_barrier((kept, sent, rest))
    pair = (kept.astype(jnp.float32) + swap(sent, 0, 1).astype(jnp.float32)).astype(jnp.bfloat16)
    rest += far(rest)
    parts = [swap(pair[:, k * rows : (k + 1) * rows], 0, 2 * k) for k in range(1, n_tp // 2)]
    weight_gradients = all_rows(
        replica, rest, units, columns, gate_weight, up_weight, down_weight
    )
    parts, weight_gradients = lax.optimization_barrier((parts, weight_gradients))
    total = pair[:, :rows].astype(jnp.float32) + sum(part.astype(jnp.float32) for part in parts)
    branch, grad_normed = total[0], total[1]
    mixed = (expanded_hidden + branch).astype(jnp.bfloat16)
    gain_applied = grad_normed * norm_scale_vector
    inner_product = jnp.mean(gain_applied * unit_input, axis=-1, keepdims=True)
    token_gradient = (
        cotangent.astype(jnp.float32)
        + reciprocal_root_mean * (gain_applied - unit_input * inner_product)
    ).astype(jnp.bfloat16)
    return mixed, token_gradient, *weight_gradients


def sum_weight_gradients(tokens, norm_scale_vector, gate_weight, up_weight, down_weight, cotangent):
    expanded_hidden = tokens.astype(jnp.float32)
    reciprocal_root_mean = lax.rsqrt(
        jnp.mean(expanded_hidden * expanded_hidden, axis=-1, keepdims=True) + 1e-05
    )
    unit_input = expanded_hidden * reciprocal_root_mean
    rescaled_input = (unit_input * norm_scale_vector).astype(jnp.bfloat16)
    normed_all = lax.all_gather(rescaled_input, "tp", axis=0, tiled=True)
    gate = jnp.dot(normed_all, gate_weight, preferred_element_type=jnp.float32)
    lifted = jnp.dot(normed_all, up_weight, preferred_element_type=jnp.float32)
    sigmoid_gate = jax.nn.sigmoid(gate)
    activated = gate * sigmoid_gate
    hidden = (activated * lifted).astype(jnp.bfloat16)
    branch = lax.psum_scatter(
        jnp.dot(hidden, down_weight, preferred_element_type=jnp.float32).astype(jnp.bfloat16),
        "tp",
        scatter_dimension=0,
        tiled=True,
    ).astype(jnp.float32)
    mixed = (expanded_hidden + branch).astype(jnp.bfloat16)
    grad_all = lax.all_gather(cotangent, "tp", axis=0, tiled=True)
    grad_hidden = contract_cols(grad_all, down_weight)
    grad_pre = (grad_hidden * lifted * sigmoid_gate * (1.0 + gate * (1.0 - sigmoid_gate))).astype(
        jnp.bfloat16
    )
    grad_lifted = (grad_hidden * activated).astype(jnp.bfloat16)
    grad_normed = lax.psum_scatter(
        (contract_cols(grad_pre, gate_weight) + contract_cols(grad_lifted, up_weight)).astype(
            jnp.bfloat16
        ),
        "tp",
        scatter_dimension=0,
        tiled=True,
    ).astype(jnp.float32)
    gain_applied = grad_normed * norm_scale_vector
    inner_product = jnp.mean(gain_applied * unit_input, axis=-1, keepdims=True)
    token_gradient = (
        cotangent.astype(jnp.float32)
        + reciprocal_root_mean * (gain_applied - unit_input * inner_product)
    ).astype(jnp.bfloat16)
    weight_gate = contract_rows(normed_all, grad_pre).astype(jnp.bfloat16)
    weight_up = contract_rows(normed_all, grad_lifted).astype(jnp.bfloat16)
    weight_down = contract_rows(hidden, grad_all).astype(jnp.bfloat16)
    sum_gate, sum_up, sum_down = (
        lax.psum_scatter(weight_gate, "dp", scatter_dimension=0, tiled=True).astype(jnp.float32),
        lax.psum_scatter(weight_up, "dp", scatter_dimension=0, tiled=True).astype(jnp.float32),
        lax.psum_scatter(weight_down, "dp", scatter_dimension=1, tiled=True).astype(jnp.float32),
    )
    return (
        mixed,
        token_gradient,
        sum_gate.astype(jnp.bfloat16),
        sum_up.astype(jnp.bfloat16),
        sum_down.astype(jnp.bfloat16),
    )


def solution(mesh):
    n_dp, n_tp = mesh.shape["dp"], mesh.shape["tp"]
    in_specs = (
        P(("dp", "tp"), None),
        P(),
        P(None, "tp"),
        P(None, "tp"),
        P("tp", None),
        P(("dp", "tp"), None),
    )
    out_specs = (
        P(("dp", "tp"), None),
        P(("dp", "tp"), None),
        P("dp", "tp"),
        P("dp", "tp"),
        P("tp", "dp"),
    )

    def run(tokens, norm_scale_vector, gate_weight, up_weight, down_weight, cotangent):
        gathered = tokens.size + cotangent.size
        weights = (gate_weight.size + up_weight.size + down_weight.size) // n_tp
        local = sum_weight_gradients
        if (n_dp, n_tp) == (4, 8) and gathered <= weights:
            local = gather_tokens
        return jax.shard_map(
            local, mesh=mesh, in_specs=in_specs, out_specs=out_specs, check_vma=False
        )(tokens, norm_scale_vector, gate_weight, up_weight, down_weight, cotangent)

    return run
```

```python
import functools

import jax
import jax.numpy as jnp
from jax import lax
from jax.experimental import pallas as pl
from jax.experimental.pallas import tpu as pltpu
from jax.sharding import PartitionSpec as P


def contract_rows(left, right):
    return lax.dot_general(
        left, right, (((0,), (0,)), ((), ())), preferred_element_type=jnp.float32
    )


def contract_cols(left, right):
    return lax.dot_general(
        left, right, (((1,), (1,)), ((), ())), preferred_element_type=jnp.float32
    )


TILE = 256
CHUNK = 1024


def project_back(grad_out_t, down_weight):
    return jnp.dot(down_weight, grad_out_t, preferred_element_type=jnp.float32).T


def project(normed, grad_out_t, gate_weight, up_weight, down_weight):
    gate = jnp.dot(normed, gate_weight, preferred_element_type=jnp.float32)
    lifted = jnp.dot(normed, up_weight, preferred_element_type=jnp.float32)
    return gate, lifted, project_back(grad_out_t, down_weight)


def activations(gate, lifted, grad_hidden):
    sigmoid_gate = jax.nn.sigmoid(gate)
    activated = gate * sigmoid_gate
    hidden = (activated * lifted).astype(jnp.bfloat16)
    grad_pre = (grad_hidden * lifted * sigmoid_gate * (1.0 + gate * (1.0 - sigmoid_gate))).astype(
        jnp.bfloat16
    )
    grad_lifted = (grad_hidden * activated).astype(jnp.bfloat16)
    return hidden, grad_pre, grad_lifted


def pack(pieces, rows):
    at = 0
    for piece in pieces:
        rows[:, at : at + piece.shape[1]] = piece[...]
        at += piece.shape[1]


def in_hbm(*arrays):
    return [pltpu.with_memory_space_constraint(array, pltpu.HBM) for array in arrays]


def in_vmem(*arrays):
    return [pltpu.with_memory_space_constraint(array, pltpu.VMEM) for array in arrays]


def height(pieces):
    return sum(piece.shape[1] for piece in pieces)


def norm_kernel(tokens, norm_scale_vector, cotangent, unit):
    expanded_hidden = tokens[...].astype(jnp.float32)
    reciprocal_root_mean = lax.rsqrt(
        jnp.mean(expanded_hidden * expanded_hidden, axis=-1, keepdims=True) + 1e-05
    )
    rescaled_input = expanded_hidden * reciprocal_root_mean * norm_scale_vector[...]
    unit[0] = rescaled_input.astype(unit.dtype)
    unit[1] = cotangent[...]


def normalize(tokens, norm_scale_vector, cotangent):
    return pl.pallas_call(
        norm_kernel,
        out_shape=pltpu.VMEM((2, *tokens.shape), jnp.bfloat16),
        name="normalize",
    )(*in_hbm(tokens, norm_scale_vector.reshape(1, -1), cotangent))


def own_kernel(n_pieces, n_more, *refs):
    replica, pieces, refs = refs[0], refs[1 : n_pieces + 1], refs[n_pieces + 1 :]
    more, refs = refs[:n_more], refs[n_more:]
    weights, refs = refs[:3], refs[3:]
    columns, kept, sent, packed, rows, grad_out_t, out_sum, in_sum = refs[3:]
    part = kept.shape[1]

    def first():
        pack(pieces, rows)
        pack(more, packed)
        width = columns.shape[2]
        columns[...] = rows[:, :, pl.ds(pl.multiple_of(replica[0] * width, 128), width)]
        grad_out_t[...] = rows[1].T
        out_sum[...] = jnp.zeros_like(out_sum)
        in_sum[...] = jnp.zeros_like(in_sum)

    def body(gate_weight, up_weight, down_weight):
        step = pl.program_id(0)
        pl.when(step == 0)(first)
        hidden, grad_pre, grad_lifted = activations(
            *project(rows[0], grad_out_t[...], gate_weight[...], up_weight[...], down_weight[...])
        )
        here = pl.ds(pl.multiple_of(step * TILE, TILE), TILE)
        for ref, unit in zip(refs, (hidden, grad_pre, grad_lifted)):
            ref[:, here] = unit
        grad_pre_t, grad_lifted_t = grad_pre.T, grad_lifted.T
        for at in range(0, out_sum.shape[1], CHUNK):
            here = slice(at, at + CHUNK)
            out_sum[:, here] += jnp.dot(
                hidden, down_weight[:, here], preferred_element_type=jnp.float32
            )
            in_sum[here] += jnp.dot(
                gate_weight[here], grad_pre_t, preferred_element_type=jnp.float32
            ) + jnp.dot(up_weight[here], grad_lifted_t, preferred_element_type=jnp.float32)

    depth, hidden_units = weights[0].shape
    tall = pl.BlockSpec((depth, TILE), lambda i: (0, i))
    wide = pl.BlockSpec((TILE, depth), lambda i: (i, 0))
    pltpu.emit_pipeline(body, grid=(hidden_units // TILE,), in_specs=[tall, tall, wide])(*weights)
    kept[0] = out_sum[:part].astype(kept.dtype)
    sent[0] = out_sum[part:].astype(sent.dtype)
    summed = in_sum[...].T
    kept[1] = summed[:part].astype(kept.dtype)
    sent[1] = summed[part:].astype(sent.dtype)


def own_rows(replica, n_dp, pieces, more, gate_weight, up_weight, down_weight):
    depth, hidden_units = gate_weight.shape
    count = height(pieces)
    half = pltpu.VMEM((2, count // 2, depth), jnp.bfloat16)
    columns = (2, count, depth // n_dp)
    unit = pltpu.VMEM((count, hidden_units), jnp.bfloat16)
    return pl.pallas_call(
        functools.partial(own_kernel, len(pieces), len(more)),
        in_specs=[pl.BlockSpec(memory_space=pltpu.SMEM)]
        + [pl.BlockSpec(memory_space=pltpu.VMEM)] * (len(pieces) + len(more))
        + [pl.BlockSpec(memory_space=pl.ANY)] * 3,
        out_shape=[
            unit,
            unit,
            unit,
            pltpu.VMEM(columns, jnp.bfloat16),
            half,
            half,
            pltpu.VMEM((2, height(more), depth), jnp.bfloat16),
        ],
        scratch_shapes=[
            pltpu.VMEM((2, count, depth), jnp.bfloat16),
            pltpu.VMEM((depth, count), jnp.bfloat16),
            pltpu.VMEM((count, depth), jnp.float32),
            pltpu.VMEM((depth, count), jnp.float32),
        ],
        compiler_params=pltpu.CompilerParams(vmem_limit_bytes=28 * 2**20),
        cost_estimate=pl.CostEstimate(
            flops=12 * count * depth * hidden_units,
            bytes_accessed=6 * depth * hidden_units,
            transcendentals=count * hidden_units,
        ),
        name="own_rows",
    )(replica, *in_vmem(*pieces, *more), *in_hbm(gate_weight, up_weight, down_weight))


def all_kernel(n_pieces, *refs):
    replica, pieces, refs = refs[0], refs[1 : n_pieces + 1], refs[n_pieces + 1 :]
    own_hidden, own_grad_pre, own_grad_lifted, own_columns = refs[:4]
    weights, gradients = refs[4:7], refs[7:10]
    rows, normed_t, grad_out, grad_out_t, hidden, grad_pre, grad_lifted = refs[10:]
    depth, hidden_units = weights[0].shape
    tiles = hidden_units // TILE
    ahead = own_columns.shape[1]
    width = normed_t.shape[0]

    def weight_gradients(grad_gate, grad_up, grad_down):
        grad_gate[...] = jnp.dot(
            normed_t[...], grad_pre[...], preferred_element_type=jnp.float32
        ).astype(grad_gate.dtype)
        grad_up[...] = jnp.dot(
            normed_t[...], grad_lifted[...], preferred_element_type=jnp.float32
        ).astype(grad_up.dtype)
        grad_down[...] = jnp.dot(
            hidden[...].T, grad_out[...], preferred_element_type=jnp.float32
        ).astype(grad_down.dtype)

    def fill(step, gate, lifted, grad_hidden):
        here = pl.ds(pl.multiple_of(step * TILE, TILE), TILE)
        hidden[:ahead] = own_hidden[:, here]
        grad_pre[:ahead] = own_grad_pre[:, here]
        grad_lifted[:ahead] = own_grad_lifted[:, here]
        hidden[ahead:], grad_pre[ahead:], grad_lifted[ahead:] = activations(
            gate, lifted, grad_hidden
        )

    def body(gate_weight, up_weight, down_weight, *outs):
        step = pl.program_id(0)

        @pl.when(step == 0)
        def _():
            columns = pl.ds(pl.multiple_of(replica[0] * width, 128), width)
            pack(pieces, rows)
            normed_t[:, :ahead] = own_columns[0].T
            normed_t[:, ahead:] = rows[0, :, columns].T
            grad_out[:ahead] = own_columns[1]
            grad_out[ahead:] = rows[1, :, columns]
            grad_out_t[...] = rows[1].T
            fill(
                0,
                *project(
                    rows[0], grad_out_t[...], gate_weight[...], up_weight[...], down_weight[...]
                ),
            )

        @pl.when((step > 0) & (step < tiles))
        def _():
            products = project(
                rows[0], grad_out_t[...], gate_weight[...], up_weight[...], down_weight[...]
            )
            weight_gradients(*outs)
            fill(step, *products)

        @pl.when(step == tiles)
        def _():
            weight_gradients(*outs)

    tall = pl.BlockSpec((depth, TILE), lambda i: (0, jnp.minimum(i, tiles - 1)))
    wide = pl.BlockSpec((TILE, depth), lambda i: (jnp.minimum(i, tiles - 1), 0))
    tall_out = pl.BlockSpec((width, TILE), lambda i: (0, jnp.maximum(i - 1, 0)))
    wide_out = pl.BlockSpec((TILE, width), lambda i: (jnp.maximum(i - 1, 0), 0))
    pltpu.emit_pipeline(
        body,
        grid=(tiles + 1,),
        in_specs=[tall, tall, wide],
        out_specs=[tall_out, tall_out, wide_out],
    )(*weights, *gradients)


def all_rows(replica, pieces, units, own_columns, gate_weight, up_weight, down_weight):
    depth, hidden_units = gate_weight.shape
    ahead, width = own_columns.shape[1:]
    behind = height(pieces)
    count = ahead + behind
    return pl.pallas_call(
        functools.partial(all_kernel, len(pieces)),
        in_specs=[pl.BlockSpec(memory_space=pltpu.SMEM)]
        + [pl.BlockSpec(memory_space=pltpu.VMEM)] * (len(pieces) + 4)
        + [pl.BlockSpec(memory_space=pl.ANY)] * 3,
        out_specs=[pl.BlockSpec(memory_space=pl.ANY)] * 3,
        out_shape=[
            jax.ShapeDtypeStruct((width, hidden_units), jnp.bfloat16),
            jax.ShapeDtypeStruct((width, hidden_units), jnp.bfloat16),
            jax.ShapeDtypeStruct((hidden_units, width), jnp.bfloat16),
        ],
        scratch_shapes=[
            pltpu.VMEM((2, behind, depth), jnp.bfloat16),
            pltpu.VMEM((width, count), jnp.bfloat16),
            pltpu.VMEM((count, width), jnp.bfloat16),
            pltpu.VMEM((depth, behind), jnp.bfloat16),
            pltpu.VMEM((count, TILE), jnp.bfloat16),
            pltpu.VMEM((count, TILE), jnp.bfloat16),
            pltpu.VMEM((count, TILE), jnp.bfloat16),
        ],
        compiler_params=pltpu.CompilerParams(vmem_limit_bytes=32 * 2**20),
        cost_estimate=pl.CostEstimate(
            flops=6 * (behind * depth + count * width) * hidden_units,
            bytes_accessed=6 * (depth + width) * hidden_units,
            transcendentals=behind * hidden_units,
        ),
        name="all_rows",
    )(
        replica,
        *in_vmem(*pieces, *units, own_columns),
        *in_hbm(gate_weight, up_weight, down_weight),
    )


def gather_tokens(tokens, norm_scale_vector, gate_weight, up_weight, down_weight, cotangent):
    n_dp = lax.axis_size("dp")
    n_tp = lax.axis_size("tp")
    replica = lax.axis_index("dp").astype(jnp.int32).reshape(1)
    rows = tokens.shape[0]

    def swap(array, dp_bits, tp_bits):
        pairs = [
            (d * n_tp + t, (d ^ dp_bits) * n_tp + (t ^ tp_bits))
            for d in range(n_dp)
            for t in range(n_tp)
        ]
        return lax.ppermute(array, ("dp", "tp"), pairs)

    def far(pieces):
        return [swap(piece, 0, 1) for piece in pieces]

    expanded_hidden = tokens.astype(jnp.float32)
    reciprocal_root_mean = lax.rsqrt(
        jnp.mean(expanded_hidden * expanded_hidden, axis=-1, keepdims=True) + 1e-05
    )
    unit_input = expanded_hidden * reciprocal_root_mean
    unit0 = normalize(tokens, norm_scale_vector, cotangent)
    unit2, unit1 = swap(unit0, 0, 4), swap(unit0, 0, 2)
    across = [swap(unit0, b, 0) for b in range(1, n_dp)]
    unit2, unit1, across, again0 = lax.optimization_barrier((unit2, unit1, across, unit0))
    unit3 = swap(unit2, 0, 2)
    across1 = [swap(unit1, 1, 0), swap(unit1, 2, 0)]
    far_units = far([again0, unit1])
    last = jnp.concatenate([unit2, unit3], axis=1)
    across1, far_units, last = lax.optimization_barrier((across1, far_units, last))
    own = [unit0, unit1, last] + far_units + [swap(last, 0, 1)]
    rest = [swap(last, b, 0) for b in range(1, n_dp)] + [swap(unit1, 3, 0)]
    *units, own_columns, kept, sent, packed = own_rows(
        replica, n_dp, own, across + across1, gate_weight, up_weight, down_weight
    )
    kept, sent, rest = lax.optimization_barrier((kept, sent, rest))
    pair = (kept.astype(jnp.float32) + swap(sent, 0, 1).astype(jnp.float32)).astype(jnp.bfloat16)
    rest += [packed]
    rest += far(rest)
    parts = [swap(pair[:, k * rows : (k + 1) * rows], 0, 2 * k) for k in range(1, n_tp // 2)]
    weight_gradients = all_rows(
        replica, rest, units, own_columns, gate_weight, up_weight, down_weight
    )
    parts, weight_gradients = lax.optimization_barrier((parts, weight_gradients))
    total = pair[:, :rows].astype(jnp.float32) + sum(part.astype(jnp.float32) for part in parts)
    branch, grad_normed = total[0], total[1]
    mixed = (expanded_hidden + branch).astype(jnp.bfloat16)
    gain_applied = grad_normed * norm_scale_vector
    inner_product = jnp.mean(gain_applied * unit_input, axis=-1, keepdims=True)
    token_gradient = (
        cotangent.astype(jnp.float32)
        + reciprocal_root_mean * (gain_applied - unit_input * inner_product)
    ).astype(jnp.bfloat16)
    return mixed, token_gradient, *weight_gradients


def sum_weight_gradients(tokens, norm_scale_vector, gate_weight, up_weight, down_weight, cotangent):
    expanded_hidden = tokens.astype(jnp.float32)
    reciprocal_root_mean = lax.rsqrt(
        jnp.mean(expanded_hidden * expanded_hidden, axis=-1, keepdims=True) + 1e-05
    )
    unit_input = expanded_hidden * reciprocal_root_mean
    rescaled_input = (unit_input * norm_scale_vector).astype(jnp.bfloat16)
    normed_all = lax.all_gather(rescaled_input, "tp", axis=0, tiled=True)
    gate = jnp.dot(normed_all, gate_weight, preferred_element_type=jnp.float32)
    lifted = jnp.dot(normed_all, up_weight, preferred_element_type=jnp.float32)
    sigmoid_gate = jax.nn.sigmoid(gate)
    activated = gate * sigmoid_gate
    hidden = (activated * lifted).astype(jnp.bfloat16)
    branch = lax.psum_scatter(
        jnp.dot(hidden, down_weight, preferred_element_type=jnp.float32).astype(jnp.bfloat16),
        "tp",
        scatter_dimension=0,
        tiled=True,
    ).astype(jnp.float32)
    mixed = (expanded_hidden + branch).astype(jnp.bfloat16)
    grad_all = lax.all_gather(cotangent, "tp", axis=0, tiled=True)
    grad_hidden = contract_cols(grad_all, down_weight)
    grad_pre = (grad_hidden * lifted * sigmoid_gate * (1.0 + gate * (1.0 - sigmoid_gate))).astype(
        jnp.bfloat16
    )
    grad_lifted = (grad_hidden * activated).astype(jnp.bfloat16)
    grad_normed = lax.psum_scatter(
        (contract_cols(grad_pre, gate_weight) + contract_cols(grad_lifted, up_weight)).astype(
            jnp.bfloat16
        ),
        "tp",
        scatter_dimension=0,
        tiled=True,
    ).astype(jnp.float32)
    gain_applied = grad_normed * norm_scale_vector
    inner_product = jnp.mean(gain_applied * unit_input, axis=-1, keepdims=True)
    token_gradient = (
        cotangent.astype(jnp.float32)
        + reciprocal_root_mean * (gain_applied - unit_input * inner_product)
    ).astype(jnp.bfloat16)
    weight_gate = contract_rows(normed_all, grad_pre).astype(jnp.bfloat16)
    weight_up = contract_rows(normed_all, grad_lifted).astype(jnp.bfloat16)
    weight_down = contract_rows(hidden, grad_all).astype(jnp.bfloat16)
    sum_gate, sum_up, sum_down = (
        lax.psum_scatter(weight_gate, "dp", scatter_dimension=0, tiled=True).astype(jnp.float32),
        lax.psum_scatter(weight_up, "dp", scatter_dimension=0, tiled=True).astype(jnp.float32),
        lax.psum_scatter(weight_down, "dp", scatter_dimension=1, tiled=True).astype(jnp.float32),
    )
    return (
        mixed,
        token_gradient,
        sum_gate.astype(jnp.bfloat16),
        sum_up.astype(jnp.bfloat16),
        sum_down.astype(jnp.bfloat16),
    )


def solution(mesh):
    n_dp, n_tp = mesh.shape["dp"], mesh.shape["tp"]
    in_specs = (
        P(("dp", "tp"), None),
        P(),
        P(None, "tp"),
        P(None, "tp"),
        P("tp", None),
        P(("dp", "tp"), None),
    )
    out_specs = (
        P(("dp", "tp"), None),
        P(("dp", "tp"), None),
        P("dp", "tp"),
        P("dp", "tp"),
        P("tp", "dp"),
    )

    def run(tokens, norm_scale_vector, gate_weight, up_weight, down_weight, cotangent):
        gathered = tokens.size + cotangent.size
        weights = (gate_weight.size + up_weight.size + down_weight.size) // n_tp
        local = sum_weight_gradients
        if (n_dp, n_tp) == (4, 8) and gathered <= weights:
            local = gather_tokens
        return jax.shard_map(
            local, mesh=mesh, in_specs=in_specs, out_specs=out_specs, check_vma=False
        )(tokens, norm_scale_vector, gate_weight, up_weight, down_weight, cotangent)

    return run
```

```python
import functools

import jax
import jax.numpy as jnp
from jax import lax
from jax.experimental import pallas as pl
from jax.experimental.pallas import tpu as pltpu
from jax.sharding import PartitionSpec as P


def contract_rows(left, right):
    return lax.dot_general(
        left, right, (((0,), (0,)), ((), ())), preferred_element_type=jnp.float32
    )


def contract_cols(left, right):
    return lax.dot_general(
        left, right, (((1,), (1,)), ((), ())), preferred_element_type=jnp.float32
    )


TILE = 256
CHUNK = 1024


def project_back(grad_out_t, down_weight):
    return jnp.dot(down_weight, grad_out_t, preferred_element_type=jnp.float32).T


def project(normed, grad_out_t, gate_weight, up_weight, down_weight):
    gate = jnp.dot(normed, gate_weight, preferred_element_type=jnp.float32)
    lifted = jnp.dot(normed, up_weight, preferred_element_type=jnp.float32)
    return gate, lifted, project_back(grad_out_t, down_weight)


def activations(gate, lifted, grad_hidden):
    sigmoid_gate = jax.nn.sigmoid(gate)
    activated = gate * sigmoid_gate
    hidden = (activated * lifted).astype(jnp.bfloat16)
    grad_pre = (grad_hidden * lifted * sigmoid_gate * (1.0 + gate * (1.0 - sigmoid_gate))).astype(
        jnp.bfloat16
    )
    grad_lifted = (grad_hidden * activated).astype(jnp.bfloat16)
    return hidden, grad_pre, grad_lifted


def pack(pieces, rows):
    at = 0
    for piece in pieces:
        rows[:, at : at + piece.shape[1]] = piece[...]
        at += piece.shape[1]


def in_hbm(*arrays):
    return [pltpu.with_memory_space_constraint(array, pltpu.HBM) for array in arrays]


def in_vmem(*arrays):
    return [pltpu.with_memory_space_constraint(array, pltpu.VMEM) for array in arrays]


def height(pieces):
    return sum(piece.shape[1] for piece in pieces)


def norm_kernel(tokens, norm_scale_vector, cotangent, unit):
    expanded_hidden = tokens[...].astype(jnp.float32)
    reciprocal_root_mean = lax.rsqrt(
        jnp.mean(expanded_hidden * expanded_hidden, axis=-1, keepdims=True) + 1e-05
    )
    rescaled_input = expanded_hidden * reciprocal_root_mean * norm_scale_vector[...]
    unit[0] = rescaled_input.astype(unit.dtype)
    unit[1] = cotangent[...]


def normalize(tokens, norm_scale_vector, cotangent):
    return pl.pallas_call(
        norm_kernel,
        out_shape=pltpu.VMEM((2, *tokens.shape), jnp.bfloat16),
        name="normalize",
    )(*in_hbm(tokens, norm_scale_vector.reshape(1, -1), cotangent))


def own_kernel(n_pieces, n_more, *refs):
    replica, pieces, refs = refs[0], refs[1 : n_pieces + 1], refs[n_pieces + 1 :]
    more, refs = refs[:n_more], refs[n_more:]
    weights, refs = refs[:3], refs[3:]
    columns, kept, sent, packed, rows, grad_out_t, out_sum, in_sum = refs[3:]
    part = kept.shape[1]

    def first():
        pack(pieces, rows)
        pack(more, packed)
        width = columns.shape[2]
        columns[...] = rows[:, :, pl.ds(pl.multiple_of(replica[0] * width, 128), width)]
        grad_out_t[...] = rows[1].T
        out_sum[...] = jnp.zeros_like(out_sum)
        in_sum[...] = jnp.zeros_like(in_sum)

    def body(gate_weight, up_weight, down_weight):
        step = pl.program_id(0)
        pl.when(step == 0)(first)
        hidden, grad_pre, grad_lifted = activations(
            *project(rows[0], grad_out_t[...], gate_weight[...], up_weight[...], down_weight[...])
        )
        here = pl.ds(pl.multiple_of(step * TILE, TILE), TILE)
        for ref, unit in zip(refs, (hidden, grad_pre, grad_lifted)):
            ref[:, here] = unit
        grad_pre_t, grad_lifted_t = grad_pre.T, grad_lifted.T
        for at in range(0, out_sum.shape[1], CHUNK):
            here = slice(at, at + CHUNK)
            out_sum[:, here] += jnp.dot(
                hidden, down_weight[:, here], preferred_element_type=jnp.float32
            )
            in_sum[here] += jnp.dot(
                gate_weight[here], grad_pre_t, preferred_element_type=jnp.float32
            ) + jnp.dot(up_weight[here], grad_lifted_t, preferred_element_type=jnp.float32)

    depth, hidden_units = weights[0].shape
    tall = pl.BlockSpec((depth, TILE), lambda i: (0, i))
    wide = pl.BlockSpec((TILE, depth), lambda i: (i, 0))
    pltpu.emit_pipeline(body, grid=(hidden_units // TILE,), in_specs=[tall, tall, wide])(*weights)
    kept[0] = out_sum[:part].astype(kept.dtype)
    sent[0] = out_sum[part:].astype(sent.dtype)
    summed = in_sum[...].T
    kept[1] = summed[:part].astype(kept.dtype)
    sent[1] = summed[part:].astype(sent.dtype)


def own_rows(replica, n_dp, pieces, more, gate_weight, up_weight, down_weight):
    depth, hidden_units = gate_weight.shape
    count = height(pieces)
    half = pltpu.VMEM((2, count // 2, depth), jnp.bfloat16)
    columns = (2, count, depth // n_dp)
    unit = pltpu.VMEM((count, hidden_units), jnp.bfloat16)
    return pl.pallas_call(
        functools.partial(own_kernel, len(pieces), len(more)),
        in_specs=[pl.BlockSpec(memory_space=pltpu.SMEM)]
        + [pl.BlockSpec(memory_space=pltpu.VMEM)] * (len(pieces) + len(more))
        + [pl.BlockSpec(memory_space=pl.ANY)] * 3,
        out_shape=[
            unit,
            unit,
            unit,
            pltpu.VMEM(columns, jnp.bfloat16),
            half,
            half,
            pltpu.VMEM((2, height(more), depth), jnp.bfloat16),
        ],
        scratch_shapes=[
            pltpu.VMEM((2, count, depth), jnp.bfloat16),
            pltpu.VMEM((depth, count), jnp.bfloat16),
            pltpu.VMEM((count, depth), jnp.float32),
            pltpu.VMEM((depth, count), jnp.float32),
        ],
        compiler_params=pltpu.CompilerParams(vmem_limit_bytes=28 * 2**20),
        cost_estimate=pl.CostEstimate(
            flops=12 * count * depth * hidden_units,
            bytes_accessed=6 * depth * hidden_units,
            transcendentals=count * hidden_units,
        ),
        name="own_rows",
    )(replica, *in_vmem(*pieces, *more), *in_hbm(gate_weight, up_weight, down_weight))


def all_kernel(n_pieces, *refs):
    replica, pieces, refs = refs[0], refs[1 : n_pieces + 1], refs[n_pieces + 1 :]
    own_hidden, own_grad_pre, own_grad_lifted, own_columns = refs[:4]
    weights, gradients = refs[4:7], refs[7:10]
    rows, normed_t, grad_out, grad_out_t, hidden, grad_pre, grad_lifted = refs[10:]
    depth, hidden_units = weights[0].shape
    tiles = hidden_units // TILE
    ahead = own_columns.shape[1]
    width = normed_t.shape[0]

    def weight_gradients(grad_gate, grad_up, grad_down):
        grad_gate[...] = jnp.dot(
            normed_t[...], grad_pre[...], preferred_element_type=jnp.float32
        ).astype(grad_gate.dtype)
        grad_up[...] = jnp.dot(
            normed_t[...], grad_lifted[...], preferred_element_type=jnp.float32
        ).astype(grad_up.dtype)
        grad_down[...] = jnp.dot(
            hidden[...].T, grad_out[...], preferred_element_type=jnp.float32
        ).astype(grad_down.dtype)

    def fill(step, gate, lifted, grad_hidden):
        here = pl.ds(pl.multiple_of(step * TILE, TILE), TILE)
        hidden[:ahead] = own_hidden[:, here]
        grad_pre[:ahead] = own_grad_pre[:, here]
        grad_lifted[:ahead] = own_grad_lifted[:, here]
        hidden[ahead:], grad_pre[ahead:], grad_lifted[ahead:] = activations(
            gate, lifted, grad_hidden
        )

    def body(gate_weight, up_weight, down_weight, *outs):
        step = pl.program_id(0)

        @pl.when(step == 0)
        def _():
            columns = pl.ds(pl.multiple_of(replica[0] * width, 128), width)
            pack(pieces, rows)
            normed_t[:, :ahead] = own_columns[0].T
            normed_t[:, ahead:] = rows[0, :, columns].T
            grad_out[:ahead] = own_columns[1]
            grad_out[ahead:] = rows[1, :, columns]
            grad_out_t[...] = rows[1].T
            fill(
                0,
                *project(
                    rows[0], grad_out_t[...], gate_weight[...], up_weight[...], down_weight[...]
                ),
            )

        @pl.when((step > 0) & (step < tiles))
        def _():
            products = project(
                rows[0], grad_out_t[...], gate_weight[...], up_weight[...], down_weight[...]
            )
            weight_gradients(*outs)
            fill(step, *products)

        @pl.when(step == tiles)
        def _():
            weight_gradients(*outs)

    tall = pl.BlockSpec((depth, TILE), lambda i: (0, jnp.minimum(i, tiles - 1)))
    wide = pl.BlockSpec((TILE, depth), lambda i: (jnp.minimum(i, tiles - 1), 0))
    tall_out = pl.BlockSpec((width, TILE), lambda i: (0, jnp.maximum(i - 1, 0)))
    wide_out = pl.BlockSpec((TILE, width), lambda i: (jnp.maximum(i - 1, 0), 0))
    pltpu.emit_pipeline(
        body,
        grid=(tiles + 1,),
        in_specs=[tall, tall, wide],
        out_specs=[tall_out, tall_out, wide_out],
    )(*weights, *gradients)


def all_rows(replica, pieces, units, own_columns, gate_weight, up_weight, down_weight):
    depth, hidden_units = gate_weight.shape
    ahead, width = own_columns.shape[1:]
    behind = height(pieces)
    count = ahead + behind
    return pl.pallas_call(
        functools.partial(all_kernel, len(pieces)),
        in_specs=[pl.BlockSpec(memory_space=pltpu.SMEM)]
        + [pl.BlockSpec(memory_space=pltpu.VMEM)] * (len(pieces) + 4)
        + [pl.BlockSpec(memory_space=pl.ANY)] * 3,
        out_specs=[pl.BlockSpec(memory_space=pl.ANY)] * 3,
        out_shape=[
            jax.ShapeDtypeStruct((width, hidden_units), jnp.bfloat16),
            jax.ShapeDtypeStruct((width, hidden_units), jnp.bfloat16),
            jax.ShapeDtypeStruct((hidden_units, width), jnp.bfloat16),
        ],
        scratch_shapes=[
            pltpu.VMEM((2, behind, depth), jnp.bfloat16),
            pltpu.VMEM((width, count), jnp.bfloat16),
            pltpu.VMEM((count, width), jnp.bfloat16),
            pltpu.VMEM((depth, behind), jnp.bfloat16),
            pltpu.VMEM((count, TILE), jnp.bfloat16),
            pltpu.VMEM((count, TILE), jnp.bfloat16),
            pltpu.VMEM((count, TILE), jnp.bfloat16),
        ],
        compiler_params=pltpu.CompilerParams(vmem_limit_bytes=32 * 2**20),
        cost_estimate=pl.CostEstimate(
            flops=6 * (behind * depth + count * width) * hidden_units,
            bytes_accessed=6 * (depth + width) * hidden_units,
            transcendentals=behind * hidden_units,
        ),
        name="all_rows",
    )(
        replica,
        *in_vmem(*pieces, *units, own_columns),
        *in_hbm(gate_weight, up_weight, down_weight),
    )


def gather_tokens(tokens, norm_scale_vector, gate_weight, up_weight, down_weight, cotangent):
    n_dp = lax.axis_size("dp")
    n_tp = lax.axis_size("tp")
    replica = lax.axis_index("dp").astype(jnp.int32).reshape(1)
    rows = tokens.shape[0]

    def swap(array, dp_bits, tp_bits):
        pairs = [
            (d * n_tp + t, (d ^ dp_bits) * n_tp + (t ^ tp_bits))
            for d in range(n_dp)
            for t in range(n_tp)
        ]
        return lax.ppermute(array, ("dp", "tp"), pairs)

    def far(pieces):
        return [swap(piece, 0, 1) for piece in pieces]

    expanded_hidden = tokens.astype(jnp.float32)
    reciprocal_root_mean = lax.rsqrt(
        jnp.mean(expanded_hidden * expanded_hidden, axis=-1, keepdims=True) + 1e-05
    )
    unit_input = expanded_hidden * reciprocal_root_mean
    unit0 = normalize(tokens, norm_scale_vector, cotangent)
    unit2, unit1 = swap(unit0, 0, 4), swap(unit0, 0, 2)
    across = [swap(unit0, b, 0) for b in range(1, n_dp)]
    unit2, unit1, across, again0 = lax.optimization_barrier((unit2, unit1, across, unit0))
    unit3 = swap(unit2, 0, 2)
    across1 = [swap(unit1, 1, 0), swap(unit1, 2, 0)]
    far_units, far_across = far([again0, unit1]), far(across)
    last = jnp.concatenate([unit2, unit3], axis=1)
    last, across1, far_units, far_across = lax.optimization_barrier(
        (last, across1, far_units, far_across)
    )
    more = across + far_across + across1 + far(across1)
    own = [unit0, unit1, last] + far_units + [swap(last, 0, 1)]
    rest = [swap(last, b, 0) for b in range(1, n_dp)] + [swap(unit1, 3, 0)]
    *units, own_columns, kept, sent, packed = own_rows(
        replica, n_dp, own, more, gate_weight, up_weight, down_weight
    )
    kept, sent, rest = lax.optimization_barrier((kept, sent, rest))
    pair = (kept.astype(jnp.float32) + swap(sent, 0, 1).astype(jnp.float32)).astype(jnp.bfloat16)
    rest += far(rest) + [packed]
    parts = [swap(pair[:, k * rows : (k + 1) * rows], 0, 2 * k) for k in range(1, n_tp // 2)]
    weight_gradients = all_rows(
        replica, rest, units, own_columns, gate_weight, up_weight, down_weight
    )
    parts, weight_gradients = lax.optimization_barrier((parts, weight_gradients))
    total = pair[:, :rows].astype(jnp.float32) + sum(part.astype(jnp.float32) for part in parts)
    branch, grad_normed = total[0], total[1]
    mixed = (expanded_hidden + branch).astype(jnp.bfloat16)
    gain_applied = grad_normed * norm_scale_vector
    inner_product = jnp.mean(gain_applied * unit_input, axis=-1, keepdims=True)
    token_gradient = (
        cotangent.astype(jnp.float32)
        + reciprocal_root_mean * (gain_applied - unit_input * inner_product)
    ).astype(jnp.bfloat16)
    return mixed, token_gradient, *weight_gradients


def sum_weight_gradients(tokens, norm_scale_vector, gate_weight, up_weight, down_weight, cotangent):
    expanded_hidden = tokens.astype(jnp.float32)
    reciprocal_root_mean = lax.rsqrt(
        jnp.mean(expanded_hidden * expanded_hidden, axis=-1, keepdims=True) + 1e-05
    )
    unit_input = expanded_hidden * reciprocal_root_mean
    rescaled_input = (unit_input * norm_scale_vector).astype(jnp.bfloat16)
    normed_all = lax.all_gather(rescaled_input, "tp", axis=0, tiled=True)
    gate = jnp.dot(normed_all, gate_weight, preferred_element_type=jnp.float32)
    lifted = jnp.dot(normed_all, up_weight, preferred_element_type=jnp.float32)
    sigmoid_gate = jax.nn.sigmoid(gate)
    activated = gate * sigmoid_gate
    hidden = (activated * lifted).astype(jnp.bfloat16)
    branch = lax.psum_scatter(
        jnp.dot(hidden, down_weight, preferred_element_type=jnp.float32).astype(jnp.bfloat16),
        "tp",
        scatter_dimension=0,
        tiled=True,
    ).astype(jnp.float32)
    mixed = (expanded_hidden + branch).astype(jnp.bfloat16)
    grad_all = lax.all_gather(cotangent, "tp", axis=0, tiled=True)
    grad_hidden = contract_cols(grad_all, down_weight)
    grad_pre = (grad_hidden * lifted * sigmoid_gate * (1.0 + gate * (1.0 - sigmoid_gate))).astype(
        jnp.bfloat16
    )
    grad_lifted = (grad_hidden * activated).astype(jnp.bfloat16)
    grad_normed = lax.psum_scatter(
        (contract_cols(grad_pre, gate_weight) + contract_cols(grad_lifted, up_weight)).astype(
            jnp.bfloat16
        ),
        "tp",
        scatter_dimension=0,
        tiled=True,
    ).astype(jnp.float32)
    gain_applied = grad_normed * norm_scale_vector
    inner_product = jnp.mean(gain_applied * unit_input, axis=-1, keepdims=True)
    token_gradient = (
        cotangent.astype(jnp.float32)
        + reciprocal_root_mean * (gain_applied - unit_input * inner_product)
    ).astype(jnp.bfloat16)
    weight_gate = contract_rows(normed_all, grad_pre).astype(jnp.bfloat16)
    weight_up = contract_rows(normed_all, grad_lifted).astype(jnp.bfloat16)
    weight_down = contract_rows(hidden, grad_all).astype(jnp.bfloat16)
    sum_gate, sum_up, sum_down = (
        lax.psum_scatter(weight_gate, "dp", scatter_dimension=0, tiled=True).astype(jnp.float32),
        lax.psum_scatter(weight_up, "dp", scatter_dimension=0, tiled=True).astype(jnp.float32),
        lax.psum_scatter(weight_down, "dp", scatter_dimension=1, tiled=True).astype(jnp.float32),
    )
    return (
        mixed,
        token_gradient,
        sum_gate.astype(jnp.bfloat16),
        sum_up.astype(jnp.bfloat16),
        sum_down.astype(jnp.bfloat16),
    )


def solution(mesh):
    n_dp, n_tp = mesh.shape["dp"], mesh.shape["tp"]
    in_specs = (
        P(("dp", "tp"), None),
        P(),
        P(None, "tp"),
        P(None, "tp"),
        P("tp", None),
        P(("dp", "tp"), None),
    )
    out_specs = (
        P(("dp", "tp"), None),
        P(("dp", "tp"), None),
        P("dp", "tp"),
        P("dp", "tp"),
        P("tp", "dp"),
    )

    def run(tokens, norm_scale_vector, gate_weight, up_weight, down_weight, cotangent):
        gathered = tokens.size + cotangent.size
        weights = (gate_weight.size + up_weight.size + down_weight.size) // n_tp
        local = sum_weight_gradients
        if (n_dp, n_tp) == (4, 8) and gathered <= weights:
            local = gather_tokens
        return jax.shard_map(
            local, mesh=mesh, in_specs=in_specs, out_specs=out_specs, check_vma=False
        )(tokens, norm_scale_vector, gate_weight, up_weight, down_weight, cotangent)

    return run
```

```python
import functools

import jax
import jax.numpy as jnp
from jax import lax
from jax.experimental import pallas as pl
from jax.experimental.pallas import tpu as pltpu
from jax.sharding import PartitionSpec as P


def contract_rows(left, right):
    return lax.dot_general(
        left, right, (((0,), (0,)), ((), ())), preferred_element_type=jnp.float32
    )


def contract_cols(left, right):
    return lax.dot_general(
        left, right, (((1,), (1,)), ((), ())), preferred_element_type=jnp.float32
    )


TILE = 256
CHUNK = 1024


def project_back(grad_out_t, down_weight):
    return jnp.dot(down_weight, grad_out_t, preferred_element_type=jnp.float32).T


def project(normed, grad_out_t, gate_weight, up_weight, down_weight):
    gate = jnp.dot(normed, gate_weight, preferred_element_type=jnp.float32)
    lifted = jnp.dot(normed, up_weight, preferred_element_type=jnp.float32)
    return gate, lifted, project_back(grad_out_t, down_weight)


def activations(gate, lifted, grad_hidden):
    sigmoid_gate = jax.nn.sigmoid(gate)
    activated = gate * sigmoid_gate
    hidden = (activated * lifted).astype(jnp.bfloat16)
    grad_pre = (grad_hidden * lifted * sigmoid_gate * (1.0 + gate * (1.0 - sigmoid_gate))).astype(
        jnp.bfloat16
    )
    grad_lifted = (grad_hidden * activated).astype(jnp.bfloat16)
    return hidden, grad_pre, grad_lifted


def pack(pieces, rows):
    at = 0
    for piece in pieces:
        rows[:, at : at + piece.shape[1]] = piece[...]
        at += piece.shape[1]


def in_hbm(*arrays):
    return [pltpu.with_memory_space_constraint(array, pltpu.HBM) for array in arrays]


def in_vmem(*arrays):
    return [pltpu.with_memory_space_constraint(array, pltpu.VMEM) for array in arrays]


def height(pieces):
    return sum(piece.shape[1] for piece in pieces)


def norm_kernel(tokens, norm_scale_vector, cotangent, unit):
    expanded_hidden = tokens[...].astype(jnp.float32)
    reciprocal_root_mean = lax.rsqrt(
        jnp.mean(expanded_hidden * expanded_hidden, axis=-1, keepdims=True) + 1e-05
    )
    rescaled_input = expanded_hidden * reciprocal_root_mean * norm_scale_vector[...]
    unit[0] = rescaled_input.astype(unit.dtype)
    unit[1] = cotangent[...]


def normalize(tokens, norm_scale_vector, cotangent):
    return pl.pallas_call(
        norm_kernel,
        out_shape=pltpu.VMEM((2, *tokens.shape), jnp.bfloat16),
        name="normalize",
    )(*in_hbm(tokens, norm_scale_vector.reshape(1, -1), cotangent))


def own_kernel(n_pieces, n_more, *refs):
    replica, pieces, refs = refs[0], refs[1 : n_pieces + 1], refs[n_pieces + 1 :]
    more, refs = refs[:n_more], refs[n_more:]
    weights, refs = refs[:3], refs[3:]
    columns, kept, sent, packed, rows, grad_out_t, out_sum, in_sum = refs[3:]
    part = kept.shape[1]

    def first():
        pack(pieces, rows)
        pack(more, packed)
        width = columns.shape[2]
        columns[...] = rows[:, :, pl.ds(pl.multiple_of(replica[0] * width, 128), width)]
        grad_out_t[...] = rows[1].T
        out_sum[...] = jnp.zeros_like(out_sum)
        in_sum[...] = jnp.zeros_like(in_sum)

    def body(gate_weight, up_weight, down_weight):
        step = pl.program_id(0)
        pl.when(step == 0)(first)
        hidden, grad_pre, grad_lifted = activations(
            *project(rows[0], grad_out_t[...], gate_weight[...], up_weight[...], down_weight[...])
        )
        here = pl.ds(pl.multiple_of(step * TILE, TILE), TILE)
        for ref, unit in zip(refs, (hidden, grad_pre, grad_lifted)):
            ref[:, here] = unit
        grad_pre_t, grad_lifted_t = grad_pre.T, grad_lifted.T
        for at in range(0, out_sum.shape[1], CHUNK):
            here = slice(at, at + CHUNK)
            out_sum[:, here] += jnp.dot(
                hidden, down_weight[:, here], preferred_element_type=jnp.float32
            )
            in_sum[here] += jnp.dot(
                gate_weight[here], grad_pre_t, preferred_element_type=jnp.float32
            ) + jnp.dot(up_weight[here], grad_lifted_t, preferred_element_type=jnp.float32)

    depth, hidden_units = weights[0].shape
    tall = pl.BlockSpec((depth, TILE), lambda i: (0, i))
    wide = pl.BlockSpec((TILE, depth), lambda i: (i, 0))
    pltpu.emit_pipeline(body, grid=(hidden_units // TILE,), in_specs=[tall, tall, wide])(*weights)
    kept[0] = out_sum[:part].astype(kept.dtype)
    sent[0] = out_sum[part:].astype(sent.dtype)
    summed = in_sum[...].T
    kept[1] = summed[:part].astype(kept.dtype)
    sent[1] = summed[part:].astype(sent.dtype)


def own_rows(replica, n_dp, pieces, more, gate_weight, up_weight, down_weight):
    depth, hidden_units = gate_weight.shape
    count = height(pieces)
    half = pltpu.VMEM((2, count // 2, depth), jnp.bfloat16)
    columns = (2, count, depth // n_dp)
    unit = pltpu.VMEM((count, hidden_units), jnp.bfloat16)
    return pl.pallas_call(
        functools.partial(own_kernel, len(pieces), len(more)),
        in_specs=[pl.BlockSpec(memory_space=pltpu.SMEM)]
        + [pl.BlockSpec(memory_space=pltpu.VMEM)] * (len(pieces) + len(more))
        + [pl.BlockSpec(memory_space=pl.ANY)] * 3,
        out_shape=[
            unit,
            unit,
            unit,
            pltpu.VMEM(columns, jnp.bfloat16),
            half,
            half,
            pltpu.VMEM((2, height(more), depth), jnp.bfloat16),
        ],
        scratch_shapes=[
            pltpu.VMEM((2, count, depth), jnp.bfloat16),
            pltpu.VMEM((depth, count), jnp.bfloat16),
            pltpu.VMEM((count, depth), jnp.float32),
            pltpu.VMEM((depth, count), jnp.float32),
        ],
        compiler_params=pltpu.CompilerParams(vmem_limit_bytes=28 * 2**20),
        cost_estimate=pl.CostEstimate(
            flops=12 * count * depth * hidden_units,
            bytes_accessed=6 * depth * hidden_units,
            transcendentals=count * hidden_units,
        ),
        name="own_rows",
    )(replica, *in_vmem(*pieces, *more), *in_hbm(gate_weight, up_weight, down_weight))


def all_kernel(n_pieces, *refs):
    replica, pieces, refs = refs[0], refs[1 : n_pieces + 1], refs[n_pieces + 1 :]
    own_hidden, own_grad_pre, own_grad_lifted, own_columns = refs[:4]
    weights, gradients = refs[4:7], refs[7:10]
    rows, normed_t, grad_out, grad_out_t, hidden, grad_pre, grad_lifted = refs[10:]
    depth, hidden_units = weights[0].shape
    tiles = hidden_units // TILE
    ahead = own_columns.shape[1]
    width = normed_t.shape[0]

    def weight_gradients(grad_gate, grad_up, grad_down):
        grad_gate[...] = jnp.dot(
            normed_t[...], grad_pre[...], preferred_element_type=jnp.float32
        ).astype(grad_gate.dtype)
        grad_up[...] = jnp.dot(
            normed_t[...], grad_lifted[...], preferred_element_type=jnp.float32
        ).astype(grad_up.dtype)
        grad_down[...] = jnp.dot(
            hidden[...].T, grad_out[...], preferred_element_type=jnp.float32
        ).astype(grad_down.dtype)

    def fill(step, gate, lifted, grad_hidden):
        here = pl.ds(pl.multiple_of(step * TILE, TILE), TILE)
        hidden[:ahead] = own_hidden[:, here]
        grad_pre[:ahead] = own_grad_pre[:, here]
        grad_lifted[:ahead] = own_grad_lifted[:, here]
        hidden[ahead:], grad_pre[ahead:], grad_lifted[ahead:] = activations(
            gate, lifted, grad_hidden
        )

    def body(gate_weight, up_weight, down_weight, *outs):
        step = pl.program_id(0)

        @pl.when(step == 0)
        def _():
            columns = pl.ds(pl.multiple_of(replica[0] * width, 128), width)
            pack(pieces, rows)
            normed_t[:, :ahead] = own_columns[0].T
            normed_t[:, ahead:] = rows[0, :, columns].T
            grad_out[:ahead] = own_columns[1]
            grad_out[ahead:] = rows[1, :, columns]
            grad_out_t[...] = rows[1].T
            fill(
                0,
                *project(
                    rows[0], grad_out_t[...], gate_weight[...], up_weight[...], down_weight[...]
                ),
            )

        @pl.when((step > 0) & (step < tiles))
        def _():
            products = project(
                rows[0], grad_out_t[...], gate_weight[...], up_weight[...], down_weight[...]
            )
            weight_gradients(*outs)
            fill(step, *products)

        @pl.when(step == tiles)
        def _():
            weight_gradients(*outs)

    tall = pl.BlockSpec((depth, TILE), lambda i: (0, jnp.minimum(i, tiles - 1)))
    wide = pl.BlockSpec((TILE, depth), lambda i: (jnp.minimum(i, tiles - 1), 0))
    tall_out = pl.BlockSpec((width, TILE), lambda i: (0, jnp.maximum(i - 1, 0)))
    wide_out = pl.BlockSpec((TILE, width), lambda i: (jnp.maximum(i - 1, 0), 0))
    pltpu.emit_pipeline(
        body,
        grid=(tiles + 1,),
        in_specs=[tall, tall, wide],
        out_specs=[tall_out, tall_out, wide_out],
    )(*weights, *gradients)


def all_rows(replica, pieces, units, own_columns, gate_weight, up_weight, down_weight):
    depth, hidden_units = gate_weight.shape
    ahead, width = own_columns.shape[1:]
    behind = height(pieces)
    count = ahead + behind
    return pl.pallas_call(
        functools.partial(all_kernel, len(pieces)),
        in_specs=[pl.BlockSpec(memory_space=pltpu.SMEM)]
        + [pl.BlockSpec(memory_space=pltpu.VMEM)] * (len(pieces) + 4)
        + [pl.BlockSpec(memory_space=pl.ANY)] * 3,
        out_specs=[pl.BlockSpec(memory_space=pl.ANY)] * 3,
        out_shape=[
            jax.ShapeDtypeStruct((width, hidden_units), jnp.bfloat16),
            jax.ShapeDtypeStruct((width, hidden_units), jnp.bfloat16),
            jax.ShapeDtypeStruct((hidden_units, width), jnp.bfloat16),
        ],
        scratch_shapes=[
            pltpu.VMEM((2, behind, depth), jnp.bfloat16),
            pltpu.VMEM((width, count), jnp.bfloat16),
            pltpu.VMEM((count, width), jnp.bfloat16),
            pltpu.VMEM((depth, behind), jnp.bfloat16),
            pltpu.VMEM((count, TILE), jnp.bfloat16),
            pltpu.VMEM((count, TILE), jnp.bfloat16),
            pltpu.VMEM((count, TILE), jnp.bfloat16),
        ],
        compiler_params=pltpu.CompilerParams(vmem_limit_bytes=32 * 2**20),
        cost_estimate=pl.CostEstimate(
            flops=6 * (behind * depth + count * width) * hidden_units,
            bytes_accessed=6 * (depth + width) * hidden_units,
            transcendentals=behind * hidden_units,
        ),
        name="all_rows",
    )(
        replica,
        *in_vmem(*pieces, *units, own_columns),
        *in_hbm(gate_weight, up_weight, down_weight),
    )


def gather_tokens(tokens, norm_scale_vector, gate_weight, up_weight, down_weight, cotangent):
    n_dp = lax.axis_size("dp")
    n_tp = lax.axis_size("tp")
    replica = lax.axis_index("dp").astype(jnp.int32).reshape(1)
    rows = tokens.shape[0]

    def swap(array, dp_bits, tp_bits):
        pairs = [
            (d * n_tp + t, (d ^ dp_bits) * n_tp + (t ^ tp_bits))
            for d in range(n_dp)
            for t in range(n_tp)
        ]
        return lax.ppermute(array, ("dp", "tp"), pairs)

    def far(pieces):
        return [swap(piece, 0, 1) for piece in pieces]

    expanded_hidden = tokens.astype(jnp.float32)
    reciprocal_root_mean = lax.rsqrt(
        jnp.mean(expanded_hidden * expanded_hidden, axis=-1, keepdims=True) + 1e-05
    )
    unit_input = expanded_hidden * reciprocal_root_mean
    unit0 = normalize(tokens, norm_scale_vector, cotangent)
    unit2, unit1 = swap(unit0, 0, 4), swap(unit0, 0, 2)
    across = [swap(unit0, b, 0) for b in range(1, n_dp)]
    unit2, unit1, across, again0 = lax.optimization_barrier((unit2, unit1, across, unit0))
    unit3 = swap(unit2, 0, 2)
    across1 = [swap(unit1, 1, 0), swap(unit1, 2, 0)]
    far_units = far([again0, unit1])
    last = jnp.concatenate([unit2, unit3], axis=1)
    across1, far_units, last = lax.optimization_barrier((across1, far_units, last))
    own = [unit0, unit1, last] + far_units + [swap(last, 0, 1)]
    rest = [swap(last, b, 0) for b in range(1, n_dp)] + [swap(unit1, 3, 0)]
    *units, own_columns, kept, sent, packed = own_rows(
        replica, n_dp, own, across + across1, gate_weight, up_weight, down_weight
    )
    kept, sent, rest = lax.optimization_barrier((kept, sent, rest))
    came, far_packed = far([sent, packed])
    pair = (kept.astype(jnp.float32) + came.astype(jnp.float32)).astype(jnp.bfloat16)
    pair, far_packed = lax.optimization_barrier((pair, far_packed))
    rest += far(rest) + [packed, far_packed]
    parts = [swap(pair[:, k * rows : (k + 1) * rows], 0, 2 * k) for k in range(1, n_tp // 2)]
    weight_gradients = all_rows(
        replica, rest, units, own_columns, gate_weight, up_weight, down_weight
    )
    parts, weight_gradients = lax.optimization_barrier((parts, weight_gradients))
    total = pair[:, :rows].astype(jnp.float32) + sum(part.astype(jnp.float32) for part in parts)
    branch, grad_normed = total[0], total[1]
    mixed = (expanded_hidden + branch).astype(jnp.bfloat16)
    gain_applied = grad_normed * norm_scale_vector
    inner_product = jnp.mean(gain_applied * unit_input, axis=-1, keepdims=True)
    token_gradient = (
        cotangent.astype(jnp.float32)
        + reciprocal_root_mean * (gain_applied - unit_input * inner_product)
    ).astype(jnp.bfloat16)
    return mixed, token_gradient, *weight_gradients


def sum_weight_gradients(tokens, norm_scale_vector, gate_weight, up_weight, down_weight, cotangent):
    expanded_hidden = tokens.astype(jnp.float32)
    reciprocal_root_mean = lax.rsqrt(
        jnp.mean(expanded_hidden * expanded_hidden, axis=-1, keepdims=True) + 1e-05
    )
    unit_input = expanded_hidden * reciprocal_root_mean
    rescaled_input = (unit_input * norm_scale_vector).astype(jnp.bfloat16)
    normed_all = lax.all_gather(rescaled_input, "tp", axis=0, tiled=True)
    gate = jnp.dot(normed_all, gate_weight, preferred_element_type=jnp.float32)
    lifted = jnp.dot(normed_all, up_weight, preferred_element_type=jnp.float32)
    sigmoid_gate = jax.nn.sigmoid(gate)
    activated = gate * sigmoid_gate
    hidden = (activated * lifted).astype(jnp.bfloat16)
    branch = lax.psum_scatter(
        jnp.dot(hidden, down_weight, preferred_element_type=jnp.float32).astype(jnp.bfloat16),
        "tp",
        scatter_dimension=0,
        tiled=True,
    ).astype(jnp.float32)
    mixed = (expanded_hidden + branch).astype(jnp.bfloat16)
    grad_all = lax.all_gather(cotangent, "tp", axis=0, tiled=True)
    grad_hidden = contract_cols(grad_all, down_weight)
    grad_pre = (grad_hidden * lifted * sigmoid_gate * (1.0 + gate * (1.0 - sigmoid_gate))).astype(
        jnp.bfloat16
    )
    grad_lifted = (grad_hidden * activated).astype(jnp.bfloat16)
    grad_normed = lax.psum_scatter(
        (contract_cols(grad_pre, gate_weight) + contract_cols(grad_lifted, up_weight)).astype(
            jnp.bfloat16
        ),
        "tp",
        scatter_dimension=0,
        tiled=True,
    ).astype(jnp.float32)
    gain_applied = grad_normed * norm_scale_vector
    inner_product = jnp.mean(gain_applied * unit_input, axis=-1, keepdims=True)
    token_gradient = (
        cotangent.astype(jnp.float32)
        + reciprocal_root_mean * (gain_applied - unit_input * inner_product)
    ).astype(jnp.bfloat16)
    weight_gate = contract_rows(normed_all, grad_pre).astype(jnp.bfloat16)
    weight_up = contract_rows(normed_all, grad_lifted).astype(jnp.bfloat16)
    weight_down = contract_rows(hidden, grad_all).astype(jnp.bfloat16)
    sum_gate, sum_up, sum_down = (
        lax.psum_scatter(weight_gate, "dp", scatter_dimension=0, tiled=True).astype(jnp.float32),
        lax.psum_scatter(weight_up, "dp", scatter_dimension=0, tiled=True).astype(jnp.float32),
        lax.psum_scatter(weight_down, "dp", scatter_dimension=1, tiled=True).astype(jnp.float32),
    )
    return (
        mixed,
        token_gradient,
        sum_gate.astype(jnp.bfloat16),
        sum_up.astype(jnp.bfloat16),
        sum_down.astype(jnp.bfloat16),
    )


def solution(mesh):
    n_dp, n_tp = mesh.shape["dp"], mesh.shape["tp"]
    in_specs = (
        P(("dp", "tp"), None),
        P(),
        P(None, "tp"),
        P(None, "tp"),
        P("tp", None),
        P(("dp", "tp"), None),
    )
    out_specs = (
        P(("dp", "tp"), None),
        P(("dp", "tp"), None),
        P("dp", "tp"),
        P("dp", "tp"),
        P("tp", "dp"),
    )

    def run(tokens, norm_scale_vector, gate_weight, up_weight, down_weight, cotangent):
        gathered = tokens.size + cotangent.size
        weights = (gate_weight.size + up_weight.size + down_weight.size) // n_tp
        local = sum_weight_gradients
        if (n_dp, n_tp) == (4, 8) and gathered <= weights:
            local = gather_tokens
        return jax.shard_map(
            local, mesh=mesh, in_specs=in_specs, out_specs=out_specs, check_vma=False
        )(tokens, norm_scale_vector, gate_weight, up_weight, down_weight, cotangent)

    return run
```
